512 devices in a mesh: dom: 32 (over z_lo, y, core), band: 16 (over z_hi, x).
Axes of the slice: x: 4, y: 8, z: 8 (z_hi: 4, z_lo: 2; z = z_hi * 2 + z_lo), core: 2. Of those that a mesh axis runs over, the one named last changes fastest.
Arguments:
- bands: bfloat16 [128, 192, 16, 128], P('band', 'dom'), may hold values from -6 to 6
- potential: float32 [192, 16, 128], P('dom'), may hold values from -3 to 1
- projectors: bfloat16 [192, 16, 32, 4, 128], P('dom'), may hold values from -0.14941406 to 0.14941406
- atom_ids: int32 [64, 32], P('dom'), may hold values from 0 to 1023, as said below
- strength: float32 [1024, 4], replicated, may hold values from 0.5 to 3
- rotation: bfloat16 [128, 128], replicated, may hold values from -0.5 to 0.5
Outputs:
- rotated: bfloat16 [128, 192, 16, 128], P('band', 'dom')
The draws below stay inside these ranges and needn't reach their ends.
Inputs may be any that keep to these rules, and one draw needn't show every extreme that they name: `atom_ids`: block g lies in slab g // 2, and atom a is owned by slab a // 32. Each block names 32 distinct atoms, 16 owned by its own slab and the others owned by the slab just before or just after it in the periodic order; every atom is named by some block of its own slab.
All inputs are finite; a program needn't handle non-finite values.
Results may differ from the reference program's by a relative error of at most 0.005.
The reference program's roundings to bfloat16 on the way (of `weighted`, `first` and `filtered`) count: a program that leaves them out, or rounds other values in their place, can miss the bound.
Values may be sent and summed in bfloat16 or wider, within the bound.
No kernel may reach another device: no remote copies, remote signals or barrier semaphores. Data moves between devices by JAX's collectives and lax.ppermute only.
A program may use at most 64 MiB of HBM per device.

```python
import math
import jax
import jax.numpy as jnp
from jax import lax

CX = 6
NY = 16
NZ = 128
YB = 8
SB = 32
NPJ = 4
NBD = 8
ATOM_DEV = 32
NX = 192
NB = 128
NATOM = 1024


def draw_atom_ids(key, part):
    dev_count = NATOM // ATOM_DEV
    per_dev = NY // YB
    half_slots = SB // 2

    def owned_order(subkey):
        return jax.random.permutation(subkey, ATOM_DEV)

    def side_order(subkey):
        return jax.random.permutation(subkey, 2 * ATOM_DEV)

    def slot_order(subkey):
        return jax.random.permutation(subkey, SB)
    owned_perm = jax.vmap(owned_order)(jax.random.split(jax.random.fold_in(key, 11), dev_count))
    window = (jnp.arange(per_dev)[:, None] * half_slots + jnp.arange(half_slots)[None, :]) % ATOM_DEV
    owned = owned_perm[:, window]
    devices = jnp.arange(dev_count)
    owned_ids = devices[:, None, None] * ATOM_DEV + owned
    side = jax.vmap(side_order)(jax.random.split(jax.random.fold_in(key, 12), dev_count * per_dev))
    side = side[:, :half_slots].reshape(dev_count, per_dev, half_slots)
    side_owner = (devices[:, None, None] - 1 + 2 * (side // ATOM_DEV) + dev_count) % dev_count
    side_ids = side_owner * ATOM_DEV + side % ATOM_DEV
    joined = jnp.concatenate([owned_ids, side_ids], axis=-1).reshape(dev_count * per_dev, SB)
    orders = jax.vmap(slot_order)(jax.random.split(jax.random.fold_in(key, 13), dev_count * per_dev))
    return jnp.take_along_axis(joined, orders, axis=1).astype(jnp.int32)


def shard_levels(stream_key, dims, cuts, low, high):
    gain = 1.0
    for axis_at, shards_of in cuts:
        draws = jax.random.uniform(jax.random.fold_in(jax.random.fold_in(stream_key, 6), axis_at), (shards_of,), jnp.float32, low / len(cuts), high / len(cuts))
        gain = gain * jnp.repeat(jnp.exp(draws), dims[axis_at] // shards_of).reshape((-1,) + (1,) * (len(dims) - 1 - axis_at))
    return gain


def normal_values(own_key, dims, scale, bound, cuts=(), held_as=jnp.bfloat16):
    array = scale * jax.random.normal(own_key, dims, jnp.float32)
    if cuts:
        array = array * shard_levels(own_key, dims, cuts, -0.22, 0.18)
    return jnp.clip(array, -bound, bound).astype(held_as)


def setup_inputs(seed: int = 0) -> dict:
    key_list = jax.random.split(jax.random.key(seed), 7)
    bands = normal_values(key_list[0], (NB, NX, NY, NZ), 1.0, 6.0, ((0, 16), (1, 32)))
    potential = jnp.clip(-3.0 + 4.0 * jax.random.uniform(key_list[1], (NX, NY, NZ), jnp.float32) ** shard_levels(key_list[1], (NX, NY, NZ), ((0, 32),), -0.2, 0.2), -3.0, 1.0)
    projectors = normal_values(key_list[2], (NX, NY, SB, NPJ, NZ), 0.025, 0.14941406, ((0, 32),))
    atom_ids = draw_atom_ids(jax.random.fold_in(key_list[6], 71), 0)
    strength = jnp.clip(jnp.exp(jax.random.uniform(key_list[4], (NATOM, NPJ), jnp.float32, math.log(0.5), math.log(3.0))), 0.5, 3.0)
    rotation = normal_values(key_list[5], (NB, NB), NB ** -0.5, 0.5)
    return dict(bands=bands, potential=potential, projectors=projectors, atom_ids=atom_ids, strength=strength, rotation=rotation)


STENCIL = [-5369.0 / 1800.0, 12.0 / 7.0, -15.0 / 56.0, 10.0 / 189.0, -1.0 / 112.0, 2.0 / 1925.0, -1.0 / 16632.0]
kinetic_scale = 0.5 / 0.49
centre = 12.0
half_width = 11.0


def laplace(values):
    result = 3.0 * STENCIL[0] * values
    for offset in range(1, 7):
        for direction in (1, 2, 3):
            result = result + STENCIL[offset] * (jnp.roll(values, offset, direction) + jnp.roll(values, -offset, direction))
    return result


def reference(bands, potential, projectors, atom_ids, strength, rotation):
    slabs = NX // CX
    per_slab = NY // YB
    projector_view = projectors.astype(jnp.float32).reshape(slabs, CX, per_slab, YB, SB, NPJ, NZ)
    slot_atoms = atom_ids.reshape(-1)
    slot_strength = strength[slot_atoms]

    def apply_hamiltonian(vectors):
        values = vectors.astype(jnp.float32)
        kinetic = -kinetic_scale * laplace(values)
        group = values.shape[0]
        view = values.reshape(group, slabs, CX, per_slab, YB, NZ)
        partial_value = jnp.einsum("ixjwspz,bixjwz->ijspb", projector_view, view)
        partial_value = partial_value.reshape(slabs * per_slab * SB, NPJ, group)
        totals = jax.ops.segment_sum(partial_value, slot_atoms, num_segments=NATOM)
        weighted = (totals[slot_atoms] * slot_strength[:, :, None]).astype(jnp.bfloat16)
        weighted = lax.optimization_barrier(weighted).astype(jnp.float32)
        weighted = weighted.reshape(slabs, per_slab, SB, NPJ, group)
        nonlocal_term = jnp.einsum("ixjwspz,ijspb->bixjwz", projector_view, weighted).reshape(values.shape)
        return kinetic + potential[None] * values + nonlocal_term

    def one_group(vectors):
        start = vectors.astype(jnp.float32)
        first = ((apply_hamiltonian(vectors) - centre * start) / half_width).astype(jnp.bfloat16)
        first_values = first.astype(jnp.float32)
        return (2.0 * (apply_hamiltonian(first) - centre * first_values) / half_width - start).astype(jnp.bfloat16)

    grouped = bands.reshape(NB // NBD, NBD, NX, NY, NZ)
    filtered = lax.map(one_group, grouped).reshape(NB, NX * NY * NZ)
    rotated = jnp.dot(rotation.T, filtered, preferred_element_type=jnp.float32)
    return rotated.astype(jnp.bfloat16).reshape(NB, NX, NY, NZ)
```

```python
import functools
import jax
import jax.numpy as jnp
import numpy as np
import ml_dtypes
from jax import lax
from jax.experimental import pallas as pl
from jax.experimental.pallas import tpu as pltpu
from jax.sharding import PartitionSpec as P

STENCIL = [
    -5369.0 / 1800.0,
    12.0 / 7.0,
    -15.0 / 56.0,
    10.0 / 189.0,
    -1.0 / 112.0,
    2.0 / 1925.0,
    -1.0 / 16632.0,
]
kinetic_scale = 0.5 / 0.49
centre = 12.0
half_width = 11.0
REACH = 6
F32, BF16 = jnp.float32, jnp.bfloat16
WEIGHTS = [-kinetic_scale * w for w in STENCIL]


def split3(x):
    hi = x.astype(BF16)
    rest = x - hi.astype(F32)
    mid = rest.astype(BF16)
    return hi, mid, (rest - mid.astype(F32)).astype(BF16)


def z_matrix(depth):
    full = np.zeros((depth, depth), np.float32)
    at = np.arange(depth)
    for offset in range(1, REACH + 1):
        full[at, (at + offset) % depth] += np.float32(WEIGHTS[offset])
        full[at, (at - offset) % depth] += np.float32(WEIGHTS[offset])
    hi = full.astype(ml_dtypes.bfloat16)
    rest = full - hi.astype(np.float32)
    mid = rest.astype(ml_dtypes.bfloat16)
    low = (rest - mid.astype(np.float32)).astype(ml_dtypes.bfloat16)
    return np.concatenate([hi, mid, low], 0)


def dot_t(a, b):
    return lax.dot_general(a, b, (((1,), (1,)), ((), ())), preferred_element_type=F32)


def one_hot(target, lanes):
    wide = jnp.broadcast_to(target, (target.shape[0], lanes))
    at = lax.broadcasted_iota(jnp.int32, wide.shape, 1)
    return jnp.where(wide == at, 1.0, 0.0).astype(BF16)


def scatter(partials, target_ref, tab_ref):
    slots = partials[0].shape[1]
    total = None
    for j, partial in enumerate(partials):
        hot = one_hot(target_ref[pl.ds(j * slots, slots), :], 3 * slots)
        for piece in split3(partial):
            part = jnp.dot(piece, hot, preferred_element_type=F32)
            total = part if total is None else total + part
    for tile in range(3):
        tab_ref[tile] = total[:, tile * slots : (tile + 1) * slots]


def gathered(tot_ref, strength_ref, target_ref, blocks):
    weighted = jnp.concatenate(
        [tot_ref[tile] * strength_ref[tile : tile + 1, :] for tile in range(3)], 1
    ).astype(BF16)
    slots = tot_ref.shape[2]
    out = []
    for j in range(blocks):
        hot = one_hot(target_ref[pl.ds(j * slots, slots), :], 3 * slots)
        out.append(dot_t(weighted, hot).astype(BF16))
    return out


def pair_rows(pair):
    return slice(16 * pair, 16 * pair + 16)


def project_pair(v, proj_ref, pair, even, odd):
    e = dot_t(v, proj_ref[2 * pair])
    o = dot_t(v, proj_ref[2 * pair + 1])
    return (e if even is None else even + e), (o if odd is None else odd + o)


def block_of(pair, rows_total, block_rows):
    return (2 * pair % rows_total) // block_rows


def project_kernel(dims, v_ref, proj_ref, target_ref, tab_ref):
    cells, rows_total, block_rows = dims
    blocks = rows_total // block_rows
    even, odd = [None] * blocks, [None] * blocks
    for pair in range(cells // 2):
        j = block_of(pair, rows_total, block_rows)
        even[j], odd[j] = project_pair(v_ref[pair_rows(pair), :], proj_ref, pair, even[j], odd[j])
    scatter([e[:8] + o[8:] for e, o in zip(even, odd)], target_ref, tab_ref)


def base_kernel(dims, side_ref, v_ref, on_ref, off_ref, pot_ref, zmat_ref, out_ref, wide_ref):
    cells, rows_total, _ = dims
    side = side_ref[0]
    on_at = pl.multiple_of(jnp.where(side == 0, 2 * cells, 0), cells)
    off_at = pl.multiple_of(jnp.where(side == 0, 0, 2 * cells), cells)
    step = 8
    for c in range(0, cells, step):
        rows = slice(8 * c, 8 * (c + step))
        shape = (step,) + wide_ref.shape[1:]
        wide_ref[pl.ds(on_at + c, step)] = on_ref[rows, :].astype(F32).reshape(shape)
        wide_ref[pl.ds(off_at + c, step)] = off_ref[rows, :].astype(F32).reshape(shape)
        wide_ref[cells + c : cells + c + step] = v_ref[rows, :].astype(F32).reshape(shape)
    depth = v_ref.shape[1]
    for c in range(0, cells, rows_total):
        rows = slice(8 * c, 8 * (c + rows_total))
        v = v_ref[rows, :]
        along_z = jnp.dot(jnp.concatenate([v, v, v], 1), zmat_ref[...], preferred_element_type=F32)
        for y in range(rows_total):
            at = cells + c + y
            mine = wide_ref[at]
            pot = pot_ref[c + y : c + y + 1, :] + (3.0 * WEIGHTS[0] - centre)
            total = pot * mine + along_z[8 * y : 8 * y + 8, :]
            for offset in range(1, REACH + 1):
                beside = wide_ref[at + offset * rows_total] + wide_ref[at - offset * rows_total]
                up = cells + c + (y + offset) % rows_total
                down = cells + c + (y - offset) % rows_total
                beside = beside + (wide_ref[up] + wide_ref[down])
                total = total + WEIGHTS[offset] * beside
            out_ref[8 * (c + y) : 8 * (c + y) + 8, :] = total


def nonlocal_pair(weighted, proj_ref, pair):
    both = jnp.concatenate([proj_ref[2 * pair], proj_ref[2 * pair + 1]], 1)
    value = jnp.dot(weighted, both, preferred_element_type=F32)
    half = value.shape[1] // 2
    return jnp.concatenate([value[:, :half], value[:, half:]], 0)


def first_kernel(dims, base_ref, tot_ref, strength_ref, target_ref, proj_ref, first_ref, tab_ref):
    cells, rows_total, block_rows = dims
    blocks = rows_total // block_rows
    weighted = gathered(tot_ref, strength_ref, target_ref, blocks)
    even, odd = [None] * blocks, [None] * blocks
    for pair in range(cells // 2):
        j = block_of(pair, rows_total, block_rows)
        rows = pair_rows(pair)
        value = (base_ref[rows, :] + nonlocal_pair(weighted[j], proj_ref, pair)) / half_width
        first = value.astype(BF16)
        first_ref[rows, :] = first
        even[j], odd[j] = project_pair(first, proj_ref, pair, even[j], odd[j])
    scatter([e[:8] + o[8:] for e, o in zip(even, odd)], target_ref, tab_ref)


def filtered_kernel(dims, base_ref, tot_ref, strength_ref, target_ref, proj_ref, start_ref, out_ref):
    cells, rows_total, block_rows = dims
    weighted = gathered(tot_ref, strength_ref, target_ref, rows_total // block_rows)
    for pair in range(cells // 2):
        j = block_of(pair, rows_total, block_rows)
        rows = pair_rows(pair)
        value = 2.0 * (base_ref[rows, :] + nonlocal_pair(weighted[j], proj_ref, pair)) / half_width
        out_ref[rows, :] = (value - start_ref[rows, :].astype(F32)).astype(BF16)


def call(kernel, name, outs, ins, flops, moved, scratch=(), smem=0):
    vmem = pl.BlockSpec(memory_space=pltpu.VMEM)
    scalar = pl.BlockSpec(memory_space=pltpu.SMEM)
    single = not isinstance(outs, (list, tuple))
    return pl.pallas_call(
        kernel,
        name=name,
        out_shape=outs,
        in_specs=[scalar] * smem + [vmem] * (len(ins) - smem),
        out_specs=vmem if single else [vmem] * len(outs),
        scratch_shapes=list(scratch),
        compiler_params=pltpu.CompilerParams(vmem_limit_bytes=32 * 1024 * 1024),
        cost_estimate=pl.CostEstimate(flops=flops, bytes_accessed=moved, transcendentals=0),
    )(*ins)


def swap_on_chip(x, axis):
    count = lax.axis_size(axis)
    return lax.ppermute(x, axis, [(i, i ^ 1) for i in range(count)])


def swap_across(x, axis):
    count = lax.axis_size(axis)
    return lax.ppermute(x, axis, [(i, (((i + 1) ^ 1) - 1) % count) for i in range(count)])


def local(bands, potential, projectors, atom_ids, strength, rotation):
    local_bands, thickness, rows_total, depth = bands.shape
    blocks, slot_count = atom_ids.shape
    atom_count, proj_count = strength.shape
    block_rows = rows_total // blocks
    cells = thickness * rows_total
    rows = cells * local_bands
    slots = slot_count * proj_count
    dims = (cells, rows_total, block_rows)
    dom_count = lax.axis_size("dom")
    band_count = lax.axis_size("band")
    per_owner = atom_count // dom_count
    dom = lax.axis_index("dom")
    side = dom % 2
    first_core = side == 0

    proj = projectors.reshape(cells, slots, depth)
    pot = potential.reshape(cells, depth)
    start = bands.reshape(local_bands, cells, depth).transpose(1, 0, 2).reshape(rows, depth)
    relative = (atom_ids // per_owner - dom + 1 + dom_count) % dom_count
    target = (relative * per_owner + atom_ids % per_owner) * proj_count
    target = target[..., None] + jnp.arange(proj_count, dtype=jnp.int32)
    target = target.reshape(blocks * slots, 1)
    by_owner = strength.reshape(dom_count, per_owner * proj_count)
    near = [
        lax.dynamic_slice_in_dim(by_owner, (dom + shift + dom_count) % dom_count, 1, 0)
        for shift in (-1, 0, 1)
    ]
    near_strength = jnp.concatenate(near, 0)
    zmat = jnp.asarray(z_matrix(depth))
    side_ref = side.astype(jnp.int32).reshape(1)

    tab_shape = jax.ShapeDtypeStruct((3, local_bands, slots), F32)
    slab_shape = jax.ShapeDtypeStruct((rows, depth), BF16)
    wide_shape = jax.ShapeDtypeStruct((rows, depth), F32)
    stream = 2 * rows * slots * depth
    proj_bytes = 2 * cells * slots * depth

    def summed(tab):
        below, middle, above = tab[0:1], tab[1:2], tab[2:3]
        near_tile = swap_on_chip(jnp.where(first_core, above, below), "dom")
        low = jnp.where(first_core, below, middle + near_tile)
        high = jnp.where(first_core, middle + near_tile, above)
        pair = jnp.concatenate([low, high], 0)
        pair = pair + swap_across(pair, "dom")
        low, high = pair[0:1], pair[1:2]
        other = swap_on_chip(jnp.where(first_core, high, low), "dom")
        return jnp.where(
            first_core,
            jnp.concatenate([low, high, other], 0),
            jnp.concatenate([other, low, high], 0),
        )

    def base(v, on_chip, across):
        return call(
            functools.partial(base_kernel, dims), "base", wide_shape,
            (side_ref, v, on_chip, across, pot, zmat), 6 * rows * depth * depth, 10 * rows * depth,
            scratch=[pltpu.VMEM((3 * cells, local_bands, depth), F32)], smem=1,
        )

    start_on, start_across = swap_on_chip(start, "dom"), swap_across(start, "dom")
    tab = call(
        functools.partial(project_kernel, dims), "project", tab_shape,
        (start, proj, target), stream, proj_bytes,
    )
    totals = summed(tab)
    first, tab = call(
        functools.partial(first_kernel, dims), "first", [slab_shape, tab_shape],
        (base(start, start_on, start_across), totals, near_strength, target, proj),
        2 * stream, proj_bytes,
    )
    first_on, first_across = swap_on_chip(first, "dom"), swap_across(first, "dom")
    totals = summed(tab)
    filtered = call(
        functools.partial(filtered_kernel, dims), "filtered", slab_shape,
        (base(first, first_on, first_across), totals, near_strength, target, proj, start),
        stream, proj_bytes,
    )
    share = cells // band_count
    pieces = filtered.reshape(band_count, share, local_bands, depth)
    pieces = lax.all_to_all(pieces, "band", 0, 0, tiled=True)
    turn = rotation.reshape(band_count, local_bands, band_count * local_bands)
    turned = jnp.einsum("gxbz,gbc->xcz", pieces, turn, preferred_element_type=F32).astype(BF16)
    turned = turned.reshape(share, band_count, local_bands, depth).transpose(1, 0, 2, 3)
    turned = lax.all_to_all(turned, "band", 0, 0, tiled=True)
    return turned.reshape(cells, local_bands, depth).transpose(1, 0, 2).reshape(bands.shape)


def solution(mesh):
    placed = (
        P("band", "dom", None, None),
        P("dom", None, None),
        P("dom", None, None, None, None),
        P("dom", None),
        P(),
        P(),
    )
    return jax.shard_map(
        local, mesh=mesh, in_specs=placed, out_specs=P("band", "dom", None, None), check_vma=False
    )
```

```python
import functools
import jax
import jax.numpy as jnp
import numpy as np
from jax import lax
from jax.experimental import pallas as pl
from jax.experimental.pallas import tpu as pltpu
from jax.sharding import PartitionSpec as P

STENCIL = [
    -5369.0 / 1800.0,
    12.0 / 7.0,
    -15.0 / 56.0,
    10.0 / 189.0,
    -1.0 / 112.0,
    2.0 / 1925.0,
    -1.0 / 16632.0,
]
kinetic_scale = 0.5 / 0.49
centre = 12.0
half_width = 11.0
REACH = 6
F32, BF16 = jnp.float32, jnp.bfloat16
WEIGHTS = [-kinetic_scale * w for w in STENCIL]


def split3(x):
    hi = x.astype(BF16)
    rest = x - hi.astype(F32)
    mid = rest.astype(BF16)
    return hi, mid, (rest - mid.astype(F32)).astype(BF16)


def z_matrix(depth):
    row = lax.broadcasted_iota(jnp.int32, (depth, depth), 0)
    col = lax.broadcasted_iota(jnp.int32, (depth, depth), 1)
    apart = jnp.abs(row - col)
    apart = jnp.minimum(apart, depth - apart)
    full = jnp.zeros((depth, depth), F32)
    for offset in range(1, REACH + 1):
        full = jnp.where(apart == offset, np.float32(WEIGHTS[offset]), full)
    return jnp.concatenate(split3(full), 0)


def dot_t(a, b):
    return lax.dot_general(a, b, (((1,), (1,)), ((), ())), preferred_element_type=F32)


class Sizes:
    def __init__(self, bands, atom_ids, strength, dom_count):
        self.bands, self.thickness, self.rows, self.depth = bands
        self.blocks, self.slot_count = atom_ids
        self.atoms, self.projs = strength
        self.doms = dom_count
        self.owned = self.atoms // dom_count
        self.block_rows = self.rows // self.blocks
        self.cells = self.thickness * self.rows
        self.slots = self.slot_count * self.projs
        self.lanes = self.owned * self.projs
        self.tall = self.cells * self.bands
        assert self.owned & (self.owned - 1) == 0 and dom_count & (dom_count - 1) == 0


def one_hots(z, dom, ids_ref):
    ids = ids_ref[...]
    shift = z.owned.bit_length() - 1
    relative = ((ids >> shift) - dom + (1 + z.doms)) & (z.doms - 1)
    place = relative * z.owned + (ids & (z.owned - 1))
    slot = lax.broadcasted_iota(jnp.int32, (z.slot_count, z.slots), 0)
    lane = lax.broadcasted_iota(jnp.int32, (z.slot_count, z.slots), 1)
    inside = lane - slot * z.projs
    spread = jnp.where((inside >= 0) & (inside < z.projs), 1.0, 0.0).astype(BF16)
    wide = jnp.dot(place.astype(F32).astype(BF16), spread, preferred_element_type=F32)
    shape = (z.lanes, z.slots)
    row = lax.broadcasted_iota(jnp.int32, shape, 0)
    lane = lax.broadcasted_iota(jnp.int32, shape, 1)
    fits = (row >> shift) == lane % z.projs
    atom = (row & (z.owned - 1)).astype(F32)
    out = []
    for j in range(z.blocks):
        mine = jnp.broadcast_to(wide[j : j + 1, :], shape)
        tiles = [
            jnp.where(fits & (mine == atom + float(z.owned * tile)), 1.0, 0.0) for tile in range(3)
        ]
        out.append(jnp.concatenate(tiles, 0).astype(BF16))
    return out


def scatter(z, side, partials, hots_ref, send_ref, pair_ref):
    total = None
    for j, partial in enumerate(partials):
        hot = hots_ref[j]
        for piece in split3(partial):
            part = dot_t(piece, hot)
            total = part if total is None else total + part
    below, middle, above = (total[:, t * z.lanes : (t + 1) * z.lanes] for t in range(3))
    first_core = side == 0
    send_ref[...] = jnp.where(first_core, above, below)
    pair_ref[0] = jnp.where(first_core, below, middle)
    pair_ref[1] = jnp.where(first_core, middle, above)


def gathered(z, side, pair_ref, other_ref, strength_ref, hots_ref):
    first_core = side == 0
    low, high, other = pair_ref[0], pair_ref[1], other_ref[...]
    tiles = [
        jnp.where(first_core, low, other),
        jnp.where(first_core, high, low),
        jnp.where(first_core, other, high),
    ]
    weighted = [tile * strength_ref[t : t + 1, :] for t, tile in enumerate(tiles)]
    weighted = jnp.concatenate(weighted, 1).astype(BF16)
    return [
        jnp.dot(weighted, hots_ref[j], preferred_element_type=F32).astype(BF16)
        for j in range(z.blocks)
    ]


def pair_rows(pair):
    return slice(16 * pair, 16 * pair + 16)


def block_of(z, pair):
    return (2 * pair % z.rows) // z.block_rows


class Projector:
    def __init__(self, z, v_ref, proj_ref):
        self.z, self.v_ref, self.proj_ref = z, v_ref, proj_ref
        self.even, self.odd = [None] * z.blocks, [None] * z.blocks

    def add(self, pairs):
        for pair in pairs:
            j = block_of(self.z, pair)
            v = self.v_ref[pair_rows(pair), :]
            e, o = dot_t(v, self.proj_ref[2 * pair]), dot_t(v, self.proj_ref[2 * pair + 1])
            self.even[j] = e if self.even[j] is None else self.even[j] + e
            self.odd[j] = o if self.odd[j] is None else self.odd[j] + o

    def sums(self):
        b = self.z.bands
        return [e[:b] + o[b:] for e, o in zip(self.even, self.odd)]


CHUNKS = 6
PROJECT_LIMIT = 60000


def project_kernel(
    z, ids_hbm, bands_hbm, proj_hbm, v_ref, send_ref, pair_ref, hots_ref,
    proj_ref, ids_ref, bands_ref, ids_sem, bands_sem, proj_sems,
):
    dom = lax.axis_index("dom")
    step = z.cells // CHUNKS
    ids_copy = pltpu.make_async_copy(ids_hbm, ids_ref, ids_sem)
    ids_copy.start()
    bands_copy = pltpu.make_async_copy(bands_hbm, bands_ref, bands_sem)
    bands_copy.start()
    copies = []
    for c in range(CHUNKS):
        at = pl.ds(c * step, step)
        copies.append(pltpu.make_async_copy(proj_hbm.at[at], proj_ref.at[at], proj_sems.at[c]))
        copies[-1].start()
    ids_copy.wait()
    for j, hot in enumerate(one_hots(z, dom, ids_ref)):
        hots_ref[j] = hot
    bands_copy.wait()
    for x in range(z.thickness):
        slab = bands_ref[:, x * z.rows : (x + 1) * z.rows, :].astype(F32)
        turned = jnp.swapaxes(slab, 0, 1).reshape(z.rows * z.bands, z.depth)
        v_ref[x * z.rows * z.bands : (x + 1) * z.rows * z.bands, :] = turned.astype(BF16)
    projector = Projector(z, v_ref, proj_ref)
    for c in range(CHUNKS):
        copies[c].wait()
        projector.add(range(c * step // 2, (c + 1) * step // 2))
    scatter(z, dom & 1, projector.sums(), hots_ref, send_ref, pair_ref)


def near_strength(z, dom, strength_ref, out_ref):
    per_tile = 128 // z.owned
    row = lax.broadcasted_iota(jnp.int32, (z.projs, 128), 0)
    lane = lax.broadcasted_iota(jnp.int32, (z.projs, 128), 1)
    for t in range(3):
        owner = (dom + (t - 1) + z.doms) & (z.doms - 1)
        tile = strength_ref[:, pl.ds(pl.multiple_of(owner // per_tile * 128, 128), 128)]
        inside = owner % per_tile
        line = jnp.zeros((1, 128), F32)
        for p in range(z.projs):
            turned = pltpu.roll(tile, ((p + per_tile) - inside) % per_tile * z.owned, 1)
            keep = (row == p) & (lane >= p * z.owned) & (lane < (p + 1) * z.owned)
            line = line + jnp.sum(jnp.where(keep, turned, 0.0), axis=0, keepdims=True)
        out_ref[t : t + 1, :] = line


def base_body(z, dom, v_ref, on_ref, off_ref, pot_ref, out_ref, wide_ref):
    first_core = (dom & 1) == 0
    on_at = pl.multiple_of(jnp.where(first_core, 2 * z.cells, 0), z.cells)
    off_at = pl.multiple_of(jnp.where(first_core, 0, 2 * z.cells), z.cells)
    step, b = 8, z.bands
    for c in range(0, z.cells, step):
        rows = slice(b * c, b * (c + step))
        shape = (step, b, z.depth)
        wide_ref[pl.ds(on_at + c, step)] = on_ref[rows, :].astype(F32).reshape(shape)
        wide_ref[pl.ds(off_at + c, step)] = off_ref[rows, :].astype(F32).reshape(shape)
        wide_ref[z.cells + c : z.cells + c + step] = v_ref[rows, :].astype(F32).reshape(shape)
    zmat = z_matrix(z.depth)
    for c in range(0, z.cells, z.rows):
        v = v_ref[b * c : b * (c + z.rows), :]
        along_z = jnp.dot(jnp.concatenate([v, v, v], 1), zmat, preferred_element_type=F32)
        for y in range(z.rows):
            at = z.cells + c + y
            mine = wide_ref[at]
            pot = pot_ref[c + y : c + y + 1, :] + (3.0 * WEIGHTS[0] - centre)
            total = pot * mine + along_z[b * y : b * y + b, :]
            for offset in range(1, REACH + 1):
                beside = wide_ref[at + offset * z.rows] + wide_ref[at - offset * z.rows]
                up = z.cells + c + (y + offset) % z.rows
                down = z.cells + c + (y - offset) % z.rows
                beside = beside + (wide_ref[up] + wide_ref[down])
                total = total + WEIGHTS[offset] * beside
            out_ref[b * (c + y) : b * (c + y) + b, :] = total


def base_first_kernel(z, v_ref, on_ref, off_ref, pot_ref, strength_ref, out_ref, near_ref, wide_ref):
    dom = lax.axis_index("dom")
    near_strength(z, dom, strength_ref, near_ref)
    base_body(z, dom, v_ref, on_ref, off_ref, pot_ref, out_ref, wide_ref)


def base_kernel(z, v_ref, on_ref, off_ref, pot_ref, out_ref, wide_ref):
    base_body(z, lax.axis_index("dom"), v_ref, on_ref, off_ref, pot_ref, out_ref, wide_ref)


def nonlocal_pair(weighted, proj_ref, pair):
    both = jnp.concatenate([proj_ref[2 * pair], proj_ref[2 * pair + 1]], 1)
    value = jnp.dot(weighted, both, preferred_element_type=F32)
    half = value.shape[1] // 2
    return jnp.concatenate([value[:, :half], value[:, half:]], 0)


def first_kernel(z, base_ref, pair_in, other_ref, near_ref, hots_ref, proj_ref, first_ref, send_ref, pair_ref):
    side = lax.axis_index("dom") & 1
    weighted = gathered(z, side, pair_in, other_ref, near_ref, hots_ref)
    for pair in range(z.cells // 2):
        rows = pair_rows(pair)
        value = base_ref[rows, :] + nonlocal_pair(weighted[block_of(z, pair)], proj_ref, pair)
        first_ref[rows, :] = (value / half_width).astype(BF16)
    projector = Projector(z, first_ref, proj_ref)
    projector.add(range(z.cells // 2))
    scatter(z, side, projector.sums(), hots_ref, send_ref, pair_ref)


def filtered_kernel(z, base_ref, pair_in, other_ref, near_ref, hots_ref, proj_ref, start_ref, out_ref):
    side = lax.axis_index("dom") & 1
    weighted = gathered(z, side, pair_in, other_ref, near_ref, hots_ref)
    for pair in range(z.cells // 2):
        rows = pair_rows(pair)
        value = base_ref[rows, :] + nonlocal_pair(weighted[block_of(z, pair)], proj_ref, pair)
        out_ref[rows, :] = (2.0 * value / half_width - start_ref[rows, :].astype(F32)).astype(BF16)


VMEM = pl.BlockSpec(memory_space=pltpu.VMEM)
HBM = pl.BlockSpec(memory_space=pltpu.HBM)


def call(kernel, z, name, outs, ins, flops, moved, spaces, scratch=(), limit=12288):
    single = not isinstance(outs, (list, tuple))
    return pl.pallas_call(
        functools.partial(kernel, z),
        name=name,
        out_shape=outs,
        in_specs=spaces,
        out_specs=VMEM if single else [VMEM] * len(outs),
        scratch_shapes=list(scratch),
        compiler_params=pltpu.CompilerParams(vmem_limit_bytes=limit * 1024),
        cost_estimate=pl.CostEstimate(flops=flops, bytes_accessed=moved, transcendentals=0),
    )(*ins)


def shapes(z):
    tile = jax.ShapeDtypeStruct((z.bands, z.lanes), F32)
    pair = jax.ShapeDtypeStruct((2, z.bands, z.lanes), F32)
    slab = jax.ShapeDtypeStruct((z.tall, z.depth), BF16)
    wide = jax.ShapeDtypeStruct((z.tall, z.depth), F32)
    near = jax.ShapeDtypeStruct((8, z.lanes), F32)
    proj = jax.ShapeDtypeStruct((z.cells, z.slots, z.depth), BF16)
    hots = jax.ShapeDtypeStruct((z.blocks, 3 * z.lanes, z.slots), BF16)
    return tile, pair, slab, wide, near, proj, hots


def run_project(z, ids, bands, proj):
    tile, pair, slab, wide, near, projs, hots = shapes(z)
    stream = 2 * z.tall * z.slots * z.depth
    return call(
        project_kernel, z, "project", [slab, tile, pair, hots], (ids, bands, proj),
        stream, 2 * z.cells * z.slots * z.depth, [HBM] * 3,
        scratch=[
            pltpu.VMEM((z.cells, z.slots, z.depth), BF16),
            pltpu.VMEM((z.blocks, z.slot_count), jnp.int32),
            pltpu.VMEM((z.bands, z.cells, z.depth), BF16),
            pltpu.SemaphoreType.DMA,
            pltpu.SemaphoreType.DMA,
            pltpu.SemaphoreType.DMA((CHUNKS,)),
        ],
        limit=PROJECT_LIMIT,
    )


def wide_scratch(z):
    return [pltpu.VMEM((3 * z.cells, z.bands, z.depth), F32)]


def run_base_first(z, v, on_chip, across, pot, strength_t):
    tile, pair, slab, wide, near, projs, hots = shapes(z)
    return call(
        base_first_kernel, z, "base_first", [wide, near], (v, on_chip, across, pot, strength_t),
        6 * z.tall * z.depth * z.depth, 10 * z.tall * z.depth, [VMEM] * 5,
        scratch=wide_scratch(z),
    )


def run_base(z, v, on_chip, across, pot):
    tile, pair, slab, wide, near, projs, hots = shapes(z)
    return call(
        base_kernel, z, "base", wide, (v, on_chip, across, pot),
        6 * z.tall * z.depth * z.depth, 10 * z.tall * z.depth, [VMEM] * 4,
        scratch=wide_scratch(z),
    )


def run_first(z, base, pair_in, other, near_in, hots_in, proj):
    tile, pair, slab, wide, near, projs, hots = shapes(z)
    stream = 2 * z.tall * z.slots * z.depth
    return call(
        first_kernel, z, "first", [slab, tile, pair], (base, pair_in, other, near_in, hots_in, proj),
        2 * stream, 2 * z.cells * z.slots * z.depth, [VMEM] * 6,
    )


def run_filtered(z, base, pair_in, other, near_in, hots_in, proj, start):
    tile, pair, slab, wide, near, projs, hots = shapes(z)
    stream = 2 * z.tall * z.slots * z.depth
    return call(
        filtered_kernel, z, "filtered", slab, (base, pair_in, other, near_in, hots_in, proj, start),
        stream, 2 * z.cells * z.slots * z.depth, [VMEM] * 7,
    )


def swap_on_chip(x, axis):
    count = lax.axis_size(axis)
    return lax.ppermute(x, axis, [(i, i ^ 1) for i in range(count)])


def swap_across(x, axis):
    count = lax.axis_size(axis)
    return lax.ppermute(x, axis, [(i, (((i + 1) ^ 1) - 1) % count) for i in range(count)])


def local(bands, potential, projectors, atom_ids, strength, rotation):
    z = Sizes(bands.shape, atom_ids.shape, strength.shape, lax.axis_size("dom"))
    band_count = lax.axis_size("band")
    side = lax.axis_index("dom") % 2
    proj = projectors.reshape(z.cells, z.slots, z.depth)
    pot = potential.reshape(z.cells, z.depth)
    flat = bands.reshape(z.bands, z.cells, z.depth)
    mine = (lax.broadcasted_iota(jnp.int32, (2, 1, 1), 0) + side) == 1

    def pair_of_chips(send, pair):
        pair = pair + jnp.where(mine, swap_on_chip(send, "dom")[None], 0.0)
        return pair + swap_across(pair, "dom")

    def other_tile(pair):
        return swap_on_chip(jnp.where(side == 0, pair[1], pair[0]), "dom")

    start, send, pair, hots = run_project(z, atom_ids, flat, proj)
    start_across, start_on = swap_across(start, "dom"), swap_on_chip(start, "dom")
    pair = pair_of_chips(send, pair)
    base, near = run_base_first(z, start, start_on, start_across, pot, strength.T)
    other = other_tile(pair)
    first, send, pair = run_first(z, base, pair, other, near, hots, proj)

    first_across, first_on = swap_across(first, "dom"), swap_on_chip(first, "dom")
    pair = pair_of_chips(send, pair)
    base = run_base(z, first, first_on, first_across, pot)
    other = other_tile(pair)
    filtered = run_filtered(z, base, pair, other, near, hots, proj, start)

    share = z.cells // band_count
    pieces = filtered.reshape(band_count, share, z.bands, z.depth)
    pieces = lax.all_to_all(pieces, "band", 0, 0, tiled=True)
    turn = rotation.reshape(band_count, z.bands, band_count * z.bands)
    turned = jnp.einsum("gxbz,gbc->xcz", pieces, turn, preferred_element_type=F32).astype(BF16)
    turned = turned.reshape(share, band_count, z.bands, z.depth).transpose(1, 0, 2, 3)
    turned = lax.all_to_all(turned, "band", 0, 0, tiled=True)
    return turned.reshape(z.cells, z.bands, z.depth).transpose(1, 0, 2).reshape(bands.shape)


def solution(mesh):
    placed = (
        P("band", "dom", None, None),
        P("dom", None, None),
        P("dom", None, None, None, None),
        P("dom", None),
        P(),
        P(),
    )
    return jax.shard_map(
        local, mesh=mesh, in_specs=placed, out_specs=P("band", "dom", None, None), check_vma=False
    )
```

```python
import functools
import jax
import jax.numpy as jnp
import numpy as np
from jax import lax
from jax.experimental import pallas as pl
from jax.experimental.pallas import tpu as pltpu
from jax.sharding import PartitionSpec as P

STENCIL = [
    -5369.0 / 1800.0,
    12.0 / 7.0,
    -15.0 / 56.0,
    10.0 / 189.0,
    -1.0 / 112.0,
    2.0 / 1925.0,
    -1.0 / 16632.0,
]
kinetic_scale = 0.5 / 0.49
centre = 12.0
half_width = 11.0
REACH = 6
F32, BF16 = jnp.float32, jnp.bfloat16
WEIGHTS = [-kinetic_scale * w for w in STENCIL]


def split3(x):
    hi = x.astype(BF16)
    rest = x - hi.astype(F32)
    mid = rest.astype(BF16)
    return hi, mid, (rest - mid.astype(F32)).astype(BF16)


def z_matrix(depth):
    row = lax.broadcasted_iota(jnp.int32, (depth, depth), 0)
    col = lax.broadcasted_iota(jnp.int32, (depth, depth), 1)
    apart = jnp.abs(row - col)
    apart = jnp.minimum(apart, depth - apart)
    full = jnp.zeros((depth, depth), F32)
    for offset in range(1, REACH + 1):
        full = jnp.where(apart == offset, np.float32(WEIGHTS[offset]), full)
    return jnp.concatenate(split3(full), 0)


def dot_t(a, b):
    return lax.dot_general(a, b, (((1,), (1,)), ((), ())), preferred_element_type=F32)


class Sizes:
    def __init__(self, bands, atom_ids, strength, dom_count):
        self.bands, self.thickness, self.rows, self.depth = bands
        self.blocks, self.slot_count = atom_ids
        self.atoms, self.projs = strength
        self.doms = dom_count
        self.owned = self.atoms // dom_count
        self.block_rows = self.rows // self.blocks
        self.cells = self.thickness * self.rows
        self.slots = self.slot_count * self.projs
        self.lanes = self.owned * self.projs
        self.tall = self.cells * self.bands
        assert self.owned & (self.owned - 1) == 0 and dom_count & (dom_count - 1) == 0


def one_hots(z, dom, ids_ref):
    ids = ids_ref[...]
    shift = z.owned.bit_length() - 1
    relative = ((ids >> shift) - dom + (1 + z.doms)) & (z.doms - 1)
    place = relative * z.owned + (ids & (z.owned - 1))
    slot = lax.broadcasted_iota(jnp.int32, (z.slot_count, z.slots), 0)
    lane = lax.broadcasted_iota(jnp.int32, (z.slot_count, z.slots), 1)
    inside = lane - slot * z.projs
    spread = jnp.where((inside >= 0) & (inside < z.projs), 1.0, 0.0).astype(BF16)
    wide = jnp.dot(place.astype(F32).astype(BF16), spread, preferred_element_type=F32)
    shape = (z.lanes, z.slots)
    row = lax.broadcasted_iota(jnp.int32, shape, 0)
    lane = lax.broadcasted_iota(jnp.int32, shape, 1)
    fits = (row >> shift) == lane % z.projs
    atom = (row & (z.owned - 1)).astype(F32)
    out = []
    for j in range(z.blocks):
        mine = jnp.broadcast_to(wide[j : j + 1, :], shape)
        tiles = [
            jnp.where(fits & (mine == atom + float(z.owned * tile)), 1.0, 0.0) for tile in range(3)
        ]
        out.append(jnp.concatenate(tiles, 0).astype(BF16))
    return out


def scatter(z, side, partials, hots_ref, send_ref, pair_ref):
    total = None
    for j, partial in enumerate(partials):
        hot = hots_ref[j]
        for piece in split3(partial):
            part = dot_t(piece, hot)
            total = part if total is None else total + part
    below, middle, above = (total[:, t * z.lanes : (t + 1) * z.lanes] for t in range(3))
    first_core = side == 0
    send_ref[...] = jnp.where(first_core, above, below)
    pair_ref[0] = jnp.where(first_core, below, middle)
    pair_ref[1] = jnp.where(first_core, middle, above)


def gathered(z, side, pair_ref, other_ref, strength_ref, hots_ref):
    first_core = side == 0
    low, high, other = pair_ref[0], pair_ref[1], other_ref[...]
    tiles = [
        jnp.where(first_core, low, other),
        jnp.where(first_core, high, low),
        jnp.where(first_core, other, high),
    ]
    weighted = [tile * strength_ref[t : t + 1, :] for t, tile in enumerate(tiles)]
    weighted = jnp.concatenate(weighted, 1).astype(BF16)
    return [
        jnp.dot(weighted, hots_ref[j], preferred_element_type=F32).astype(BF16)
        for j in range(z.blocks)
    ]


def pair_rows(pair):
    return slice(16 * pair, 16 * pair + 16)


def block_of(z, pair):
    return (2 * pair % z.rows) // z.block_rows


class Projector:
    def __init__(self, z, v_ref, proj_ref):
        self.z, self.v_ref, self.proj_ref = z, v_ref, proj_ref
        self.even, self.odd = [None] * z.blocks, [None] * z.blocks

    def add(self, pairs):
        for pair in pairs:
            j = block_of(self.z, pair)
            v = self.v_ref[pair_rows(pair), :]
            e, o = dot_t(v, self.proj_ref[2 * pair]), dot_t(v, self.proj_ref[2 * pair + 1])
            self.even[j] = e if self.even[j] is None else self.even[j] + e
            self.odd[j] = o if self.odd[j] is None else self.odd[j] + o

    def sums(self):
        b = self.z.bands
        return [e[:b] + o[b:] for e, o in zip(self.even, self.odd)]


def turned(z, bands_ref, x):
    plane = bands_ref[:, x * z.rows : (x + 1) * z.rows, :].astype(F32)
    return jnp.swapaxes(plane, 0, 1)


def turn_all(z, bands_ref, v_ref):
    tall = z.rows * z.bands
    for x in range(z.thickness):
        plane = turned(z, bands_ref, x).reshape(tall, z.depth)
        v_ref[x * tall : (x + 1) * tall, :] = plane.astype(BF16)


CHUNKS = 6
PROJECT_LIMIT = 64900


def project_kernel(
    z, ids_hbm, bands_hbm, proj_hbm, send_ref, kept_ref,
    v_ref, hots_ref, proj_ref, ids_ref, bands_ref, ids_sem, bands_sem, proj_sems,
):
    dom = lax.axis_index("dom")
    step = z.cells // CHUNKS
    ids_copy = pltpu.make_async_copy(ids_hbm, ids_ref, ids_sem)
    ids_copy.start()
    bands_copy = pltpu.make_async_copy(bands_hbm, bands_ref, bands_sem)
    bands_copy.start()
    copies = []
    for c in range(CHUNKS):
        at = pl.ds(c * step, step)
        copies.append(pltpu.make_async_copy(proj_hbm.at[at], proj_ref.at[at], proj_sems.at[c]))
        copies[-1].start()
    ids_copy.wait()
    for j, hot in enumerate(one_hots(z, dom, ids_ref)):
        hots_ref[j] = hot
    bands_copy.wait()
    turn_all(z, bands_ref, v_ref)
    projector = Projector(z, v_ref, proj_ref)
    for c in range(CHUNKS):
        copies[c].wait()
        projector.add(range(c * step // 2, (c + 1) * step // 2))
    scatter(z, dom & 1, projector.sums(), hots_ref, send_ref, kept_ref)
    ones = jnp.full(kept_ref.shape[1:], 1.0, F32)
    kept_ref[2] = jnp.where((dom & 1) == 1, ones, 0.0)
    kept_ref[3] = jnp.where((dom & 1) == 0, ones, 0.0)


def stage_kernel(z, kept_ref, pair_ref, keep_ref):
    for t in range(2):
        pair_ref[t] = kept_ref[t]
        keep_ref[t] = kept_ref[2 + t]


def near_strength(z, dom, strength_ref, out_ref):
    per_tile = 128 // z.owned
    row = lax.broadcasted_iota(jnp.int32, (z.projs, 128), 0)
    lane = lax.broadcasted_iota(jnp.int32, (z.projs, 128), 1)
    for t in range(3):
        owner = (dom + (t - 1) + z.doms) & (z.doms - 1)
        tile = strength_ref[:, pl.ds(pl.multiple_of(owner // per_tile * 128, 128), 128)]
        inside = owner % per_tile
        line = jnp.zeros((1, 128), F32)
        for p in range(z.projs):
            turned = pltpu.roll(tile, ((p + per_tile) - inside) % per_tile * z.owned, 1)
            keep = (row == p) & (lane >= p * z.owned) & (lane < (p + 1) * z.owned)
            line = line + jnp.sum(jnp.where(keep, turned, 0.0), axis=0, keepdims=True)
        out_ref[t : t + 1, :] = line


def base_body(z, dom, v_ref, wide_ref, write):
    b = z.bands
    zmat = z_matrix(z.depth)
    for c in range(0, z.cells, z.rows):
        v = v_ref[b * c : b * (c + z.rows), :]
        along_z = jnp.dot(jnp.concatenate([v, v, v], 1), zmat, preferred_element_type=F32)
        for y in range(0, z.rows, 2):
            both = []
            for at in (y, y + 1):
                here = z.cells + c + at
                total = wide_ref[here] * (write.pot(c + at) + (3.0 * WEIGHTS[0] - centre))
                total = total + along_z[b * at : b * at + b, :]
                for offset in range(1, REACH + 1):
                    beside = wide_ref[here + offset * z.rows] + wide_ref[here - offset * z.rows]
                    up = z.cells + c + (at + offset) % z.rows
                    down = z.cells + c + (at - offset) % z.rows
                    beside = beside + (wide_ref[up] + wide_ref[down])
                    total = total + WEIGHTS[offset] * beside
                both.append(total)
            write((c + y) // 2, jnp.concatenate(both, 0))


class Writer:
    def __init__(self, pot_ref, put):
        self.pot_ref, self.put = pot_ref, put

    def pot(self, cell):
        return self.pot_ref[cell : cell + 1, :]

    def __call__(self, pair, value):
        self.put(pair_rows(pair), value)


def places(z, dom):
    first_core = (dom & 1) == 0
    on_at = pl.multiple_of(jnp.where(first_core, 2 * z.cells, 0), z.cells)
    off_at = pl.multiple_of(jnp.where(first_core, 0, 2 * z.cells), z.cells)
    return on_at, off_at


def base_first_kernel(
    z, bands_ref, on_ref, off_ref, pot_ref, strength_ref, ids_ref,
    out_ref, near_ref, hots_ref, v_ref, wide_ref,
):
    dom = lax.axis_index("dom")
    on_at, off_at = places(z, dom)
    for x in range(z.thickness):
        at = x * z.rows
        mine = turned(z, bands_ref, x)
        wide_ref[z.cells + at : z.cells + at + z.rows] = mine
        rows = slice(z.bands * at, z.bands * (at + z.rows))
        v_ref[rows, :] = mine.reshape(z.rows * z.bands, z.depth).astype(BF16)
        wide_ref[pl.ds(on_at + at, z.rows)] = turned(z, on_ref, x)
        wide_ref[pl.ds(off_at + at, z.rows)] = turned(z, off_ref, x)

    def put(rows, value):
        out_ref[rows, :] = value

    base_body(z, dom, v_ref, wide_ref, Writer(pot_ref, put))
    near_strength(z, dom, strength_ref, near_ref)
    for j, hot in enumerate(one_hots(z, dom, ids_ref)):
        hots_ref[j] = hot


def smooth_kernel(z, v_ref, on_ref, off_ref, pot_ref, start_ref, out_ref, wide_ref):
    dom = lax.axis_index("dom")
    on_at, off_at = places(z, dom)
    step, b = 8, z.bands

    def tile(ref, c):
        return ref[b * c : b * (c + step), :].astype(F32).reshape(step, b, z.depth)

    for c in range(0, z.cells, step):
        wide_ref[z.cells + c : z.cells + c + step] = tile(v_ref, c)
        wide_ref[pl.ds(on_at + c, step)] = tile(on_ref, c)
        wide_ref[pl.ds(off_at + c, step)] = tile(off_ref, c)

    def put(rows, value):
        out_ref[rows, :] = (2.0 * value / half_width - start_ref[rows, :].astype(F32)).astype(BF16)

    base_body(z, dom, v_ref, wide_ref, Writer(pot_ref, put))


def nonlocal_pair(weighted, proj_ref, pair):
    both = jnp.concatenate([proj_ref[2 * pair], proj_ref[2 * pair + 1]], 1)
    value = jnp.dot(weighted, both, preferred_element_type=F32)
    half = value.shape[1] // 2
    return jnp.concatenate([value[:, :half], value[:, half:]], 0)


def first_kernel(z, base_ref, pair_in, other_ref, near_ref, hots_ref, proj_ref, first_ref, send_ref, pair_ref):
    side = lax.axis_index("dom") & 1
    weighted = gathered(z, side, pair_in, other_ref, near_ref, hots_ref)
    for pair in range(z.cells // 2):
        rows = pair_rows(pair)
        value = base_ref[rows, :] + nonlocal_pair(weighted[block_of(z, pair)], proj_ref, pair)
        first_ref[rows, :] = (value / half_width).astype(BF16)
    projector = Projector(z, first_ref, proj_ref)
    projector.add(range(z.cells // 2))
    scatter(z, side, projector.sums(), hots_ref, send_ref, pair_ref)


def share_kernel(z, groups, pair_in, other_ref, near_ref, hots_ref, rotation_ref, out_ref, big_ref, tall_ref):
    side = lax.axis_index("dom") & 1
    me = lax.axis_index("band")
    b, all_bands = z.bands, groups * z.bands
    weighted = gathered(z, side, pair_in, other_ref, near_ref, hots_ref)
    turn = rotation_ref[...].astype(F32).T.astype(BF16)
    tall_ref[...] = jnp.zeros_like(tall_ref)
    parts = []
    for j in range(z.blocks):
        tall_ref[pl.ds(pl.multiple_of(me * b, b), b), :] = weighted[j].astype(F32)
        part = jnp.dot(turn, tall_ref[...].astype(BF16), preferred_element_type=F32)
        parts.append((part * (2.0 / half_width)).reshape(groups, b, z.slots))
    value = jnp.concatenate(parts, 1).reshape(groups * z.blocks * b, z.slots)
    hi = value.astype(BF16)
    low = (value - hi.astype(F32)).astype(BF16)
    rows = z.blocks * b
    for h in range(groups):
        out_ref[h, :rows, :] = hi[h * rows : (h + 1) * rows, :]
        out_ref[h, rows : 2 * rows, :] = low[h * rows : (h + 1) * rows, :]
    wide = 2 * all_bands
    row = lax.broadcasted_iota(jnp.int32, (wide, all_bands), 0)
    col = lax.broadcasted_iota(jnp.int32, (wide, all_bands), 1)
    spread = jnp.where((row // (2 * b)) * b + row % b == col, 1.0, 0.0).astype(BF16)
    tall = jnp.dot(spread, turn, preferred_element_type=F32).astype(BF16)
    big = dot_t(tall, spread)
    row = lax.broadcasted_iota(jnp.int32, (wide, wide), 0)
    col = lax.broadcasted_iota(jnp.int32, (wide, wide), 1)
    same = (row // b) % 2 == (col // b) % 2
    big_ref[...] = jnp.where(same, big, 0.0).astype(BF16)


def turn_kernel(z, groups, piece_ref, share_ref, big_ref, out_ref):
    rows = piece_ref.shape[1]
    for pair in range(rows // 16):
        at = slice(16 * pair, 16 * pair + 16)
        stack = jnp.concatenate([piece_ref[g, at, :] for g in range(groups)], 0)
        value = jnp.dot(big_ref[...], stack, preferred_element_type=F32).astype(BF16)
        for h in range(groups):
            out_ref[h, at, :] = value[16 * h : 16 * h + 16, :]
    extra = share_ref.shape[1]
    for h in range(groups):
        out_ref[h, rows : rows + extra, :] = share_ref[h]


def final_kernel(
    z, groups, in_hbm, proj_hbm, out_hbm, in_ref, proj_ref, wide_ref, out_ref, in_sem, proj_sems, out_sems
):
    in_copy = pltpu.make_async_copy(in_hbm, in_ref, in_sem)
    in_copy.start()
    copies = []
    for x in range(z.thickness):
        at = pl.ds(x * z.rows, z.rows)
        copies.append(pltpu.make_async_copy(proj_hbm.at[at], proj_ref.at[at], proj_sems.at[x]))
        copies[-1].start()
    in_copy.wait()
    rows = z.tall // groups
    part = z.blocks * z.bands
    total = None
    for g in range(groups):
        one = in_ref[g, rows : rows + part, :].astype(F32)
        one = one + in_ref[g, rows + part : rows + 2 * part, :].astype(F32)
        total = one if total is None else total + one
    b = z.bands
    lefts = []
    for j in range(z.blocks):
        own = total[j * b : (j + 1) * b, :]
        hi = own.astype(BF16)
        low = (own - hi.astype(F32)).astype(BF16)
        lefts.append(jnp.concatenate([hi, low], 0))
    pairs = rows // 16
    writes = []
    for x in range(z.thickness):
        copies[x].wait()
        for pair in range(x * z.rows // 2, (x + 1) * z.rows // 2):
            both = jnp.concatenate([proj_ref[2 * pair], proj_ref[2 * pair + 1]], 1)
            value = jnp.dot(lefts[block_of(z, pair)], both, preferred_element_type=F32)
            value = value[:b] + value[b:]
            g, at = pair // pairs, 16 * (pair % pairs)
            smooth = in_ref[g, at : at + 16, :].astype(F32)
            wide_ref[2 * pair] = smooth[:b] + value[:, : z.depth]
            wide_ref[2 * pair + 1] = smooth[b:] + value[:, z.depth :]
        at = slice(x * z.rows, (x + 1) * z.rows)
        out_ref[:, at, :] = jnp.swapaxes(wide_ref[at], 0, 1).astype(BF16)
        at = pl.ds(x * z.rows, z.rows)
        writes.append(pltpu.make_async_copy(out_ref.at[:, at, :], out_hbm.at[:, at, :], out_sems.at[x]))
        writes[-1].start()
    for write in writes:
        write.wait()


VMEM = pl.BlockSpec(memory_space=pltpu.VMEM)
HBM = pl.BlockSpec(memory_space=pltpu.HBM)


def call(kernel, z, name, outs, ins, flops, moved, spaces, scratch=(), limit=12288, groups=None, out_space=None):
    fixed = (z,) if groups is None else (z, groups)
    single = not isinstance(outs, (list, tuple))
    return pl.pallas_call(
        functools.partial(kernel, *fixed),
        name=name,
        out_shape=outs,
        in_specs=spaces,
        out_specs=(out_space or VMEM) if single else [VMEM] * len(outs),
        scratch_shapes=list(scratch),
        compiler_params=pltpu.CompilerParams(vmem_limit_bytes=limit * 1024),
        cost_estimate=pl.CostEstimate(flops=flops, bytes_accessed=moved, transcendentals=0),
    )(*ins)


def shapes(z):
    tile = jax.ShapeDtypeStruct((z.bands, z.lanes), F32)
    pair = jax.ShapeDtypeStruct((2, z.bands, z.lanes), F32)
    slab = jax.ShapeDtypeStruct((z.tall, z.depth), BF16)
    wide = jax.ShapeDtypeStruct((z.tall, z.depth), F32)
    near = jax.ShapeDtypeStruct((8, z.lanes), F32)
    proj = jax.ShapeDtypeStruct((z.cells, z.slots, z.depth), BF16)
    hots = jax.ShapeDtypeStruct((z.blocks, 3 * z.lanes, z.slots), BF16)
    return tile, pair, slab, wide, near, proj, hots


def run_stage(z, kept):
    tile, pair, slab, wide, near, projs, hots = shapes(z)
    return call(stage_kernel, z, "stage", [pair, pair], (kept,), 1000, 8 * pair.size, [VMEM])


def run_project(z, ids, bands, proj):
    tile, pair, slab, wide, near, projs, hots = shapes(z)
    kept = jax.ShapeDtypeStruct((4, z.bands, z.lanes), F32)
    stream = 2 * z.tall * z.slots * z.depth
    return call(
        project_kernel, z, "project", [tile, kept], (ids, bands, proj),
        20 * stream, 2 * z.cells * z.slots * z.depth, [HBM] * 3,
        scratch=[
            pltpu.VMEM(slab.shape, BF16),
            pltpu.VMEM(hots.shape, BF16),
            pltpu.VMEM(projs.shape, BF16),
            pltpu.VMEM((z.blocks, z.slot_count), jnp.int32),
            pltpu.VMEM((z.bands, z.cells, z.depth), BF16),
            pltpu.SemaphoreType.DMA,
            pltpu.SemaphoreType.DMA,
            pltpu.SemaphoreType.DMA((CHUNKS,)),
        ],
        limit=PROJECT_LIMIT,
    )


def wide_scratch(z):
    return [pltpu.VMEM((3 * z.cells, z.bands, z.depth), F32)]


def run_base_first(z, bands, on_chip, across, pot, strength_t, ids):
    tile, pair, slab, wide, near, projs, hots = shapes(z)
    return call(
        base_first_kernel, z, "base_first", [wide, near, hots, slab],
        (bands, on_chip, across, pot, strength_t, ids),
        300 * z.tall * z.depth * z.depth, 10 * z.tall * z.depth, [VMEM] * 6,
        scratch=wide_scratch(z),
    )


def run_smooth(z, v, on_chip, across, pot, start):
    tile, pair, slab, wide, near, projs, hots = shapes(z)
    return call(
        smooth_kernel, z, "smooth", slab, (v, on_chip, across, pot, start),
        6 * z.tall * z.depth * z.depth, 10 * z.tall * z.depth, [VMEM] * 5,
        scratch=wide_scratch(z),
    )


def run_first(z, base, pair_in, other, near_in, hots_in, proj):
    tile, pair, slab, wide, near, projs, hots = shapes(z)
    stream = 2 * z.tall * z.slots * z.depth
    return call(
        first_kernel, z, "first", [slab, tile, pair], (base, pair_in, other, near_in, hots_in, proj),
        2 * stream, 2 * z.cells * z.slots * z.depth, [VMEM] * 6,
    )


def run_share(z, groups, pair_in, other, near_in, hots_in, rotation):
    all_bands = groups * z.bands
    outs = [
        jax.ShapeDtypeStruct((groups, 2 * z.blocks * z.bands, z.slots), BF16),
        jax.ShapeDtypeStruct((2 * all_bands, 2 * all_bands), BF16),
    ]
    return call(
        share_kernel, z, "share", outs, (pair_in, other, near_in, hots_in, rotation),
        20 * all_bands * all_bands * z.slots, 6 * all_bands * all_bands, [VMEM] * 5,
        scratch=[pltpu.VMEM((all_bands, z.slots), F32)], groups=groups,
    )


def run_turn(z, groups, piece, share, big):
    rows, extra = piece.shape[1], share.shape[1]
    out = jax.ShapeDtypeStruct((groups, rows + extra, z.depth), BF16)
    return call(
        turn_kernel, z, "turn", out, (piece, share, big),
        4 * z.tall * groups * z.bands * z.depth, 4 * z.tall * z.depth, [VMEM] * 3, groups=groups,
    )


def run_final(z, groups, turned_pieces, proj):
    out = jax.ShapeDtypeStruct((z.bands, z.cells, z.depth), BF16)
    return call(
        final_kernel, z, "final", out, (turned_pieces, proj),
        2 * z.tall * z.slots * z.depth, 2 * z.cells * z.slots * z.depth, [HBM] * 2,
        scratch=[
            pltpu.VMEM(turned_pieces.shape, BF16),
            pltpu.VMEM(proj.shape, BF16),
            pltpu.VMEM((z.cells, z.bands, z.depth), F32),
            pltpu.VMEM(out.shape, BF16),
            pltpu.SemaphoreType.DMA,
            pltpu.SemaphoreType.DMA((z.thickness,)),
            pltpu.SemaphoreType.DMA((z.thickness,)),
        ],
        groups=groups, limit=PROJECT_LIMIT, out_space=HBM,
    )


def swap_on_chip(x, axis):
    count = lax.axis_size(axis)
    return lax.ppermute(x, axis, [(i, i ^ 1) for i in range(count)])


def swap_across(x, axis):
    count = lax.axis_size(axis)
    return lax.ppermute(x, axis, [(i, (((i + 1) ^ 1) - 1) % count) for i in range(count)])


def local(bands, potential, projectors, atom_ids, strength, rotation):
    z = Sizes(bands.shape, atom_ids.shape, strength.shape, lax.axis_size("dom"))
    groups = lax.axis_size("band")
    proj = projectors.reshape(z.cells, z.slots, z.depth)
    pot = potential.reshape(z.cells, z.depth)
    flat = bands.reshape(z.bands, z.cells, z.depth)

    def pair_of_chips(send, pair, keep):
        pair = pair + keep * swap_on_chip(send, "dom")[None]
        return pair + swap_across(pair, "dom")

    def other_tile(pair, keep):
        return swap_on_chip(jnp.sum(keep * pair, 0), "dom")

    start_across, start_on = swap_across(flat, "dom"), swap_on_chip(flat, "dom")
    send, kept = run_project(z, atom_ids, flat, proj)
    pair, keep = run_stage(z, kept)
    pair = pair_of_chips(send, pair, keep)
    base, near, hots, start = run_base_first(
        z, flat, start_on, start_across, pot, strength.T, atom_ids
    )
    other = other_tile(pair, keep)
    first, send, pair = run_first(z, base, pair, other, near, hots, proj)

    first_across, first_on = swap_across(first, "dom"), swap_on_chip(first, "dom")
    smooth = run_smooth(z, first, first_on, first_across, pot, start)
    pieces = smooth.reshape(groups, z.tall // groups, z.depth)
    pieces = lax.all_to_all(pieces, "band", 0, 0, tiled=True)
    pair = pair_of_chips(send, pair, keep)
    other = other_tile(pair, keep)
    share, big = run_share(z, groups, pair, other, near, hots, rotation)
    turned_pieces = run_turn(z, groups, pieces, share, big)
    turned_pieces = lax.all_to_all(turned_pieces, "band", 0, 0, tiled=True)
    return run_final(z, groups, turned_pieces, proj).reshape(bands.shape)


def solution(mesh):
    placed = (
        P("band", "dom", None, None),
        P("dom", None, None),
        P("dom", None, None, None, None),
        P("dom", None),
        P(),
        P(),
    )
    return jax.shard_map(
        local, mesh=mesh, in_specs=placed, out_specs=P("band", "dom", None, None), check_vma=False
    )
```

```python
import functools
import jax
import jax.numpy as jnp
import numpy as np
from jax import lax
from jax.experimental import pallas as pl
from jax.experimental.pallas import tpu as pltpu
from jax.sharding import PartitionSpec as P

STENCIL = [
    -5369.0 / 1800.0,
    12.0 / 7.0,
    -15.0 / 56.0,
    10.0 / 189.0,
    -1.0 / 112.0,
    2.0 / 1925.0,
    -1.0 / 16632.0,
]
kinetic_scale = 0.5 / 0.49
centre = 12.0
half_width = 11.0
REACH = 6
F32, BF16 = jnp.float32, jnp.bfloat16
WEIGHTS = [-kinetic_scale * w for w in STENCIL]


def split3(x):
    hi = x.astype(BF16)
    rest = x - hi.astype(F32)
    mid = rest.astype(BF16)
    return hi, mid, (rest - mid.astype(F32)).astype(BF16)


def z_matrix(depth):
    row = lax.broadcasted_iota(jnp.int32, (depth, depth), 0)
    col = lax.broadcasted_iota(jnp.int32, (depth, depth), 1)
    apart = jnp.abs(row - col)
    apart = jnp.minimum(apart, depth - apart)
    full = jnp.zeros((depth, depth), F32)
    for offset in range(1, REACH + 1):
        full = jnp.where(apart == offset, np.float32(WEIGHTS[offset]), full)
    return jnp.concatenate(split3(full), 0)


def dot_t(a, b):
    return lax.dot_general(a, b, (((1,), (1,)), ((), ())), preferred_element_type=F32)


class Sizes:
    def __init__(self, bands, atom_ids, strength, dom_count):
        self.bands, self.thickness, self.rows, self.depth = bands
        self.blocks, self.slot_count = atom_ids
        self.atoms, self.projs = strength
        self.doms = dom_count
        self.owned = self.atoms // dom_count
        self.block_rows = self.rows // self.blocks
        self.cells = self.thickness * self.rows
        self.slots = self.slot_count * self.projs
        self.lanes = self.owned * self.projs
        self.tall = self.cells * self.bands
        assert self.owned & (self.owned - 1) == 0 and dom_count & (dom_count - 1) == 0


def one_hots(z, dom, ids_ref):
    ids = ids_ref[...]
    shift = z.owned.bit_length() - 1
    relative = ((ids >> shift) - dom + (1 + z.doms)) & (z.doms - 1)
    place = relative * z.owned + (ids & (z.owned - 1))
    slot = lax.broadcasted_iota(jnp.int32, (z.slot_count, z.slots), 0)
    lane = lax.broadcasted_iota(jnp.int32, (z.slot_count, z.slots), 1)
    inside = lane - slot * z.projs
    spread = jnp.where((inside >= 0) & (inside < z.projs), 1.0, 0.0).astype(BF16)
    wide = jnp.dot(place.astype(F32).astype(BF16), spread, preferred_element_type=F32)
    shape = (z.lanes, z.slots)
    row = lax.broadcasted_iota(jnp.int32, shape, 0)
    lane = lax.broadcasted_iota(jnp.int32, shape, 1)
    fits = (row >> shift) == lane % z.projs
    atom = (row & (z.owned - 1)).astype(F32)
    out = []
    for j in range(z.blocks):
        mine = jnp.broadcast_to(wide[j : j + 1, :], shape)
        tiles = [
            jnp.where(fits & (mine == atom + float(z.owned * tile)), 1.0, 0.0) for tile in range(3)
        ]
        out.append(jnp.concatenate(tiles, 0).astype(BF16))
    return out


def scatter(z, side, partials, hots_ref, send_ref, pair_ref):
    total = None
    for j, partial in enumerate(partials):
        hot = hots_ref[j]
        for piece in split3(partial):
            part = dot_t(piece, hot)
            total = part if total is None else total + part
    below, middle, above = (total[:, t * z.lanes : (t + 1) * z.lanes] for t in range(3))
    first_core = side == 0
    send_ref[...] = jnp.where(first_core, above, below)
    pair_ref[0] = jnp.where(first_core, below, middle)
    pair_ref[1] = jnp.where(first_core, middle, above)


def gathered(z, side, pair_ref, other_ref, strength_ref, hots_ref):
    first_core = side == 0
    low, high, other = pair_ref[0], pair_ref[1], other_ref[...]
    tiles = [
        jnp.where(first_core, low, other),
        jnp.where(first_core, high, low),
        jnp.where(first_core, other, high),
    ]
    weighted = [tile * strength_ref[t : t + 1, :] for t, tile in enumerate(tiles)]
    weighted = jnp.concatenate(weighted, 1).astype(BF16)
    return [
        jnp.dot(weighted, hots_ref[j], preferred_element_type=F32).astype(BF16)
        for j in range(z.blocks)
    ]


def pair_rows(pair):
    return slice(16 * pair, 16 * pair + 16)


def block_of(z, pair):
    return (2 * pair % z.rows) // z.block_rows


class Projector:
    def __init__(self, z, v_ref, proj_ref):
        self.z, self.v_ref, self.proj_ref = z, v_ref, proj_ref
        self.even, self.odd = [None] * z.blocks, [None] * z.blocks

    def add(self, pairs):
        for pair in pairs:
            j = block_of(self.z, pair)
            v = self.v_ref[pair_rows(pair), :]
            e, o = dot_t(v, self.proj_ref[2 * pair]), dot_t(v, self.proj_ref[2 * pair + 1])
            self.even[j] = e if self.even[j] is None else self.even[j] + e
            self.odd[j] = o if self.odd[j] is None else self.odd[j] + o

    def sums(self):
        b = self.z.bands
        return [e[:b] + o[b:] for e, o in zip(self.even, self.odd)]


def turned(z, bands_ref, x):
    plane = bands_ref[:, x * z.rows : (x + 1) * z.rows, :].astype(F32)
    return jnp.swapaxes(plane, 0, 1)


def turn_all(z, bands_ref, v_ref):
    tall = z.rows * z.bands
    for x in range(z.thickness):
        plane = turned(z, bands_ref, x).reshape(tall, z.depth)
        v_ref[x * tall : (x + 1) * tall, :] = plane.astype(BF16)


def keep_kernel(z, keep_ref):
    side = lax.axis_index("dom") & 1
    ones = jnp.full(keep_ref.shape[1:], 1.0, F32)
    keep_ref[0] = jnp.where(side == 1, ones, 0.0)
    keep_ref[1] = jnp.where(side == 0, ones, 0.0)


def project_kernel(z, ids_ref, bands_ref, proj_ref, keep_ref, send_ref, pair_ref, v_ref, hots_ref):
    dom = lax.axis_index("dom")
    turn_all(z, bands_ref, v_ref)
    for j, hot in enumerate(one_hots(z, dom, ids_ref)):
        hots_ref[j] = hot
    projector = Projector(z, v_ref, proj_ref)
    projector.add(range(z.cells // 2))
    scatter(z, dom & 1, projector.sums(), hots_ref, send_ref, pair_ref)


def near_strength(z, dom, strength_ref, out_ref):
    per_tile = 128 // z.owned
    row = lax.broadcasted_iota(jnp.int32, (z.projs, 128), 0)
    lane = lax.broadcasted_iota(jnp.int32, (z.projs, 128), 1)
    for t in range(3):
        owner = (dom + (t - 1) + z.doms) & (z.doms - 1)
        tile = strength_ref[:, pl.ds(pl.multiple_of(owner // per_tile * 128, 128), 128)]
        inside = owner % per_tile
        line = jnp.zeros((1, 128), F32)
        for p in range(z.projs):
            turned = pltpu.roll(tile, ((p + per_tile) - inside) % per_tile * z.owned, 1)
            keep = (row == p) & (lane >= p * z.owned) & (lane < (p + 1) * z.owned)
            line = line + jnp.sum(jnp.where(keep, turned, 0.0), axis=0, keepdims=True)
        out_ref[t : t + 1, :] = line


def base_body(z, dom, v_ref, wide_ref, write):
    b = z.bands
    zmat = z_matrix(z.depth)
    for c in range(0, z.cells, z.rows):
        v = v_ref[b * c : b * (c + z.rows), :]
        along_z = jnp.dot(jnp.concatenate([v, v, v], 1), zmat, preferred_element_type=F32)
        for y in range(0, z.rows, 2):
            both = []
            for at in (y, y + 1):
                here = z.cells + c + at
                total = wide_ref[here] * (write.pot(c + at) + (3.0 * WEIGHTS[0] - centre))
                total = total + along_z[b * at : b * at + b, :]
                for offset in range(1, REACH + 1):
                    beside = wide_ref[here + offset * z.rows] + wide_ref[here - offset * z.rows]
                    up = z.cells + c + (at + offset) % z.rows
                    down = z.cells + c + (at - offset) % z.rows
                    beside = beside + (wide_ref[up] + wide_ref[down])
                    total = total + WEIGHTS[offset] * beside
                both.append(total)
            write((c + y) // 2, jnp.concatenate(both, 0))


class Writer:
    def __init__(self, pot_ref, put):
        self.pot_ref, self.put = pot_ref, put

    def pot(self, cell):
        return self.pot_ref[cell : cell + 1, :]

    def __call__(self, pair, value):
        self.put(pair_rows(pair), value)


def places(z, dom):
    first_core = (dom & 1) == 0
    on_at = pl.multiple_of(jnp.where(first_core, 2 * z.cells, 0), z.cells)
    off_at = pl.multiple_of(jnp.where(first_core, 0, 2 * z.cells), z.cells)
    return on_at, off_at


def base_first_kernel(z, v_ref, on_ref, off_ref, pot_ref, strength_ref, out_ref, near_ref, wide_ref):
    dom = lax.axis_index("dom")
    on_at, off_at = places(z, dom)
    for x in range(z.thickness):
        at = x * z.rows
        rows = slice(z.bands * at, z.bands * (at + z.rows))
        mine = v_ref[rows, :].astype(F32).reshape(z.rows, z.bands, z.depth)
        wide_ref[z.cells + at : z.cells + at + z.rows] = mine
        wide_ref[pl.ds(on_at + at, z.rows)] = turned(z, on_ref, x)
        wide_ref[pl.ds(off_at + at, z.rows)] = turned(z, off_ref, x)

    def put(rows, value):
        out_ref[rows, :] = value

    base_body(z, dom, v_ref, wide_ref, Writer(pot_ref, put))
    near_strength(z, dom, strength_ref, near_ref)


def base_kernel(z, v_ref, on_ref, off_ref, pot_ref, out_ref, wide_ref):
    dom = lax.axis_index("dom")
    on_at, off_at = places(z, dom)
    step, b = 8, z.bands

    def tile(ref, c):
        return ref[b * c : b * (c + step), :].astype(F32).reshape(step, b, z.depth)

    for c in range(0, z.cells, step):
        wide_ref[z.cells + c : z.cells + c + step] = tile(v_ref, c)
        wide_ref[pl.ds(on_at + c, step)] = tile(on_ref, c)
        wide_ref[pl.ds(off_at + c, step)] = tile(off_ref, c)

    def put(rows, value):
        out_ref[rows, :] = value

    base_body(z, dom, v_ref, wide_ref, Writer(pot_ref, put))


def nonlocal_pair(weighted, proj_ref, pair):
    both = jnp.concatenate([proj_ref[2 * pair], proj_ref[2 * pair + 1]], 1)
    value = jnp.dot(weighted, both, preferred_element_type=F32)
    half = value.shape[1] // 2
    return jnp.concatenate([value[:, :half], value[:, half:]], 0)


def first_kernel(z, base_ref, pair_in, other_ref, near_ref, hots_ref, proj_ref, first_ref, send_ref, pair_ref):
    side = lax.axis_index("dom") & 1
    weighted = gathered(z, side, pair_in, other_ref, near_ref, hots_ref)
    for pair in range(z.cells // 2):
        rows = pair_rows(pair)
        value = base_ref[rows, :] + nonlocal_pair(weighted[block_of(z, pair)], proj_ref, pair)
        first_ref[rows, :] = (value / half_width).astype(BF16)
    projector = Projector(z, first_ref, proj_ref)
    projector.add(range(z.cells // 2))
    scatter(z, side, projector.sums(), hots_ref, send_ref, pair_ref)


def filtered_kernel(z, base_ref, pair_in, other_ref, near_ref, hots_ref, proj_ref, start_ref, out_ref):
    side = lax.axis_index("dom") & 1
    weighted = gathered(z, side, pair_in, other_ref, near_ref, hots_ref)
    for pair in range(z.cells // 2):
        rows = pair_rows(pair)
        value = base_ref[rows, :] + nonlocal_pair(weighted[block_of(z, pair)], proj_ref, pair)
        out_ref[rows, :] = (2.0 * value / half_width - start_ref[rows, :].astype(F32)).astype(BF16)


VMEM = pl.BlockSpec(memory_space=pltpu.VMEM)


def call(kernel, z, name, outs, ins, flops, moved, spaces, scratch=(), limit=12288):
    single = not isinstance(outs, (list, tuple))
    return pl.pallas_call(
        functools.partial(kernel, z),
        name=name,
        out_shape=outs,
        in_specs=spaces,
        out_specs=VMEM if single else [VMEM] * len(outs),
        scratch_shapes=list(scratch),
        compiler_params=pltpu.CompilerParams(vmem_limit_bytes=limit * 1024),
        cost_estimate=pl.CostEstimate(flops=flops, bytes_accessed=moved, transcendentals=0),
    )(*ins)


def shapes(z):
    tile = jax.ShapeDtypeStruct((z.bands, z.lanes), F32)
    pair = jax.ShapeDtypeStruct((2, z.bands, z.lanes), F32)
    slab = jax.ShapeDtypeStruct((z.tall, z.depth), BF16)
    wide = jax.ShapeDtypeStruct((z.tall, z.depth), F32)
    near = jax.ShapeDtypeStruct((8, z.lanes), F32)
    proj = jax.ShapeDtypeStruct((z.cells, z.slots, z.depth), BF16)
    hots = jax.ShapeDtypeStruct((z.blocks, 3 * z.lanes, z.slots), BF16)
    return tile, pair, slab, wide, near, proj, hots


def run_keep(z):
    tile, pair, slab, wide, near, projs, hots = shapes(z)
    return call(keep_kernel, z, "keep", pair, (), 4000 * z.tall * z.slots * z.depth, 40_000_000, [])


def run_project(z, ids, bands, proj, keep):
    tile, pair, slab, wide, near, projs, hots = shapes(z)
    return call(
        project_kernel, z, "project", [tile, pair, slab, hots], (ids, bands, proj, keep),
        2 * z.tall * z.slots * z.depth, 2 * z.cells * z.slots * z.depth, [VMEM] * 4,
    )


def wide_scratch(z):
    return [pltpu.VMEM((3 * z.cells, z.bands, z.depth), F32)]


def run_base_first(z, v, on_chip, across, pot, strength_t):
    tile, pair, slab, wide, near, projs, hots = shapes(z)
    return call(
        base_first_kernel, z, "base_first", [wide, near], (v, on_chip, across, pot, strength_t),
        6 * z.tall * z.depth * z.depth, 10 * z.tall * z.depth, [VMEM] * 5,
        scratch=wide_scratch(z),
    )


def run_base(z, v, on_chip, across, pot):
    tile, pair, slab, wide, near, projs, hots = shapes(z)
    return call(
        base_kernel, z, "base", wide, (v, on_chip, across, pot),
        6 * z.tall * z.depth * z.depth, 10 * z.tall * z.depth, [VMEM] * 4,
        scratch=wide_scratch(z),
    )


def run_first(z, base, pair_in, other, near_in, hots_in, proj):
    tile, pair, slab, wide, near, projs, hots = shapes(z)
    stream = 2 * z.tall * z.slots * z.depth
    return call(
        first_kernel, z, "first", [slab, tile, pair], (base, pair_in, other, near_in, hots_in, proj),
        2 * stream, 2 * z.cells * z.slots * z.depth, [VMEM] * 6,
    )


def run_filtered(z, base, pair_in, other, near_in, hots_in, proj, start):
    tile, pair, slab, wide, near, projs, hots = shapes(z)
    stream = 2 * z.tall * z.slots * z.depth
    return call(
        filtered_kernel, z, "filtered", slab, (base, pair_in, other, near_in, hots_in, proj, start),
        stream, 2 * z.cells * z.slots * z.depth, [VMEM] * 7,
    )


def swap_on_chip(x, axis):
    count = lax.axis_size(axis)
    return lax.ppermute(x, axis, [(i, i ^ 1) for i in range(count)])


def swap_across(x, axis):
    count = lax.axis_size(axis)
    return lax.ppermute(x, axis, [(i, (((i + 1) ^ 1) - 1) % count) for i in range(count)])


def local(bands, potential, projectors, atom_ids, strength, rotation):
    z = Sizes(bands.shape, atom_ids.shape, strength.shape, lax.axis_size("dom"))
    groups = lax.axis_size("band")
    proj = projectors.reshape(z.cells, z.slots, z.depth)
    pot = potential.reshape(z.cells, z.depth)
    flat = bands.reshape(z.bands, z.cells, z.depth)

    def exchange(send, pair, keep, slab):
        across = swap_across(slab, "dom")
        pair = pair + keep * swap_on_chip(send, "dom")[None]
        pair, slab = lax.optimization_barrier((pair, slab))
        pair = pair + swap_across(pair, "dom")
        return pair, swap_on_chip(slab, "dom"), across

    def other_tile(pair, keep):
        return swap_on_chip(jnp.sum(keep * pair, 0), "dom")

    keep = run_keep(z)
    flat, keep = lax.optimization_barrier((flat, keep))
    send, pair, start, hots = run_project(z, atom_ids, flat, proj, keep)
    pair, start_on, start_across = exchange(send, pair, keep, flat)
    base, near = run_base_first(z, start, start_on, start_across, pot, strength.T)
    other = other_tile(pair, keep)
    first, send, pair = run_first(z, base, pair, other, near, hots, proj)

    pair, first_on, first_across = exchange(send, pair, keep, first)
    base = run_base(z, first, first_on, first_across, pot)
    other = other_tile(pair, keep)
    filtered = run_filtered(z, base, pair, other, near, hots, proj, start)

    share = z.cells // groups
    pieces = filtered.reshape(groups, share, z.bands, z.depth)
    pieces = lax.all_to_all(pieces, "band", 0, 0, tiled=True)
    turn = rotation.reshape(groups, z.bands, groups * z.bands)
    rotated = jnp.einsum("gxbz,gbc->xcz", pieces, turn, preferred_element_type=F32).astype(BF16)
    rotated = rotated.reshape(share, groups, z.bands, z.depth).transpose(1, 0, 2, 3)
    rotated = lax.all_to_all(rotated, "band", 0, 0, tiled=True)
    return rotated.reshape(z.cells, z.bands, z.depth).transpose(1, 0, 2).reshape(bands.shape)


def solution(mesh):
    placed = (
        P("band", "dom", None, None),
        P("dom", None, None),
        P("dom", None, None, None, None),
        P("dom", None),
        P(),
        P(),
    )
    return jax.shard_map(
        local, mesh=mesh, in_specs=placed, out_specs=P("band", "dom", None, None), check_vma=False
    )
```

```python
import functools
import jax
import jax.numpy as jnp
import numpy as np
from jax import lax
from jax.experimental import pallas as pl
from jax.experimental.pallas import tpu as pltpu
from jax.sharding import PartitionSpec as P

STENCIL = [
    -5369.0 / 1800.0,
    12.0 / 7.0,
    -15.0 / 56.0,
    10.0 / 189.0,
    -1.0 / 112.0,
    2.0 / 1925.0,
    -1.0 / 16632.0,
]
kinetic_scale = 0.5 / 0.49
centre = 12.0
half_width = 11.0
REACH = 6
F32, BF16 = jnp.float32, jnp.bfloat16
WEIGHTS = [-kinetic_scale * w for w in STENCIL]


def split3(x):
    hi = x.astype(BF16)
    rest = x - hi.astype(F32)
    mid = rest.astype(BF16)
    return hi, mid, (rest - mid.astype(F32)).astype(BF16)


def z_matrix(depth):
    row = lax.broadcasted_iota(jnp.int32, (depth, depth), 0)
    col = lax.broadcasted_iota(jnp.int32, (depth, depth), 1)
    apart = jnp.abs(row - col)
    apart = jnp.minimum(apart, depth - apart)
    full = jnp.zeros((depth, depth), F32)
    for offset in range(1, REACH + 1):
        full = jnp.where(apart == offset, np.float32(WEIGHTS[offset]), full)
    return jnp.concatenate(split3(full), 0)


def dot_t(a, b):
    return lax.dot_general(a, b, (((1,), (1,)), ((), ())), preferred_element_type=F32)


class Sizes:
    def __init__(self, bands, atom_ids, strength, dom_count):
        self.bands, self.thickness, self.rows, self.depth = bands
        self.blocks, self.slot_count = atom_ids
        self.atoms, self.projs = strength
        self.doms = dom_count
        self.owned = self.atoms // dom_count
        self.block_rows = self.rows // self.blocks
        self.cells = self.thickness * self.rows
        self.slots = self.slot_count * self.projs
        self.lanes = self.owned * self.projs
        self.tall = self.cells * self.bands
        assert self.owned & (self.owned - 1) == 0 and dom_count & (dom_count - 1) == 0


def one_hots(z, dom, ids_ref):
    ids = ids_ref[...]
    shift = z.owned.bit_length() - 1
    relative = ((ids >> shift) - dom + (1 + z.doms)) & (z.doms - 1)
    place = relative * z.owned + (ids & (z.owned - 1))
    slot = lax.broadcasted_iota(jnp.int32, (z.slot_count, z.slots), 0)
    lane = lax.broadcasted_iota(jnp.int32, (z.slot_count, z.slots), 1)
    inside = lane - slot * z.projs
    spread = jnp.where((inside >= 0) & (inside < z.projs), 1.0, 0.0).astype(BF16)
    wide = jnp.dot(place.astype(F32).astype(BF16), spread, preferred_element_type=F32)
    shape = (z.lanes, z.slots)
    row = lax.broadcasted_iota(jnp.int32, shape, 0)
    lane = lax.broadcasted_iota(jnp.int32, shape, 1)
    fits = (row >> shift) == lane % z.projs
    atom = (row & (z.owned - 1)).astype(F32)
    out = []
    for j in range(z.blocks):
        mine = jnp.broadcast_to(wide[j : j + 1, :], shape)
        tiles = [
            jnp.where(fits & (mine == atom + float(z.owned * tile)), 1.0, 0.0) for tile in range(3)
        ]
        out.append(jnp.concatenate(tiles, 0).astype(BF16))
    return out


def scatter(z, partials, hots_ref, tab_ref):
    total = None
    for j, partial in enumerate(partials):
        hot = hots_ref[j]
        for piece in split3(partial):
            part = dot_t(piece, hot)
            total = part if total is None else total + part
    for t in range(3):
        tab_ref[t] = total[:, t * z.lanes : (t + 1) * z.lanes]


def mate_tiles(side, tab_ref, mate_ref):
    first_core = side == 0
    mate_ref[0] = jnp.where(first_core, tab_ref[1], tab_ref[0])
    mate_ref[1] = jnp.where(first_core, tab_ref[2], tab_ref[1])


def meet_kernel(z, tab_ref, mate_ref, got_ref, slab_in, slab_ref, chip_ref, far_ref):
    first_core = (lax.axis_index("dom") & 1) == 0
    low, high = mate_ref[0] + got_ref[0], mate_ref[1] + got_ref[1]
    chip_ref[0], chip_ref[1] = low, high
    below, above = tab_ref[0], tab_ref[2]
    far_ref[...] = jnp.where(first_core, below, above)
    pair = jnp.concatenate(
        [jnp.where(first_core, below, high), jnp.where(first_core, low, above)], 0
    )
    for n, piece in enumerate(split3(pair)):
        slab_ref[z.tall + n * 2 * z.bands : z.tall + (n + 1) * 2 * z.bands, :] = piece


def gathered(z, tab_ref, chip_ref, across_ref, far_ref, strength_ref, hots_ref):
    first_core = (lax.axis_index("dom") & 1) == 0
    got = None
    for n in range(3):
        piece = across_ref[z.tall + n * 2 * z.bands : z.tall + (n + 1) * 2 * z.bands, :].astype(F32)
        got = piece if got is None else got + piece
    got = [got[: z.bands], got[z.bands :]]
    low, high, far = chip_ref[0], chip_ref[1], far_ref[...]
    tiles = [
        jnp.where(first_core, tab_ref[0] + got[0], low + far),
        jnp.where(first_core, low + got[1], high + got[0]),
        jnp.where(first_core, high + far, tab_ref[2] + got[1]),
    ]
    weighted = [tile * strength_ref[t : t + 1, :] for t, tile in enumerate(tiles)]
    weighted = jnp.concatenate(weighted, 1).astype(BF16)
    return [
        jnp.dot(weighted, hots_ref[j], preferred_element_type=F32).astype(BF16)
        for j in range(z.blocks)
    ]


def pair_rows(pair):
    return slice(16 * pair, 16 * pair + 16)


def block_of(z, pair):
    return (2 * pair % z.rows) // z.block_rows


class Projector:
    def __init__(self, z, v_ref, proj_ref):
        self.z, self.v_ref, self.proj_ref = z, v_ref, proj_ref
        self.even, self.odd = [None] * z.blocks, [None] * z.blocks

    def add(self, pairs):
        for pair in pairs:
            j = block_of(self.z, pair)
            v = self.v_ref[pair_rows(pair), :]
            e, o = dot_t(v, self.proj_ref[2 * pair]), dot_t(v, self.proj_ref[2 * pair + 1])
            self.even[j] = e if self.even[j] is None else self.even[j] + e
            self.odd[j] = o if self.odd[j] is None else self.odd[j] + o

    def sums(self):
        b = self.z.bands
        return [e[:b] + o[b:] for e, o in zip(self.even, self.odd)]


def turned(z, bands_ref, x):
    plane = bands_ref[:, x * z.rows : (x + 1) * z.rows, :].astype(F32)
    return jnp.swapaxes(plane, 0, 1)


def turn_all(z, bands_ref, v_ref):
    tall = z.rows * z.bands
    for x in range(z.thickness):
        plane = turned(z, bands_ref, x).reshape(tall, z.depth)
        v_ref[x * tall : (x + 1) * tall, :] = plane.astype(BF16)


def pause_kernel(z, out_ref):
    out_ref[...] = jnp.zeros_like(out_ref)


def project_kernel(z, pause_ref, ids_ref, bands_ref, proj_ref, tab_ref, mate_ref, v_ref, hots_ref):
    dom = lax.axis_index("dom")
    turn_all(z, bands_ref, v_ref)
    for j, hot in enumerate(one_hots(z, dom, ids_ref)):
        hots_ref[j] = hot
    projector = Projector(z, v_ref, proj_ref)
    projector.add(range(z.cells // 2))
    scatter(z, projector.sums(), hots_ref, tab_ref)
    mate_tiles(dom & 1, tab_ref, mate_ref)


def near_strength(z, dom, strength_ref, out_ref):
    per_tile = 128 // z.owned
    row = lax.broadcasted_iota(jnp.int32, (z.projs, 128), 0)
    lane = lax.broadcasted_iota(jnp.int32, (z.projs, 128), 1)
    for t in range(3):
        owner = (dom + (t - 1) + z.doms) & (z.doms - 1)
        tile = strength_ref[:, pl.ds(pl.multiple_of(owner // per_tile * 128, 128), 128)]
        inside = owner % per_tile
        line = jnp.zeros((1, 128), F32)
        for p in range(z.projs):
            turned = pltpu.roll(tile, ((p + per_tile) - inside) % per_tile * z.owned, 1)
            keep = (row == p) & (lane >= p * z.owned) & (lane < (p + 1) * z.owned)
            line = line + jnp.sum(jnp.where(keep, turned, 0.0), axis=0, keepdims=True)
        out_ref[t : t + 1, :] = line


def base_body(z, dom, v_ref, wide_ref, write):
    b = z.bands
    zmat = z_matrix(z.depth)
    for c in range(0, z.cells, z.rows):
        v = v_ref[b * c : b * (c + z.rows), :]
        along_z = jnp.dot(jnp.concatenate([v, v, v], 1), zmat, preferred_element_type=F32)
        for y in range(0, z.rows, 2):
            both = []
            for at in (y, y + 1):
                here = z.cells + c + at
                total = wide_ref[here] * (write.pot(c + at) + (3.0 * WEIGHTS[0] - centre))
                total = total + along_z[b * at : b * at + b, :]
                for offset in range(1, REACH + 1):
                    beside = wide_ref[here + offset * z.rows] + wide_ref[here - offset * z.rows]
                    up = z.cells + c + (at + offset) % z.rows
                    down = z.cells + c + (at - offset) % z.rows
                    beside = beside + (wide_ref[up] + wide_ref[down])
                    total = total + WEIGHTS[offset] * beside
                both.append(total)
            write((c + y) // 2, jnp.concatenate(both, 0))


class Writer:
    def __init__(self, pot_ref, put):
        self.pot_ref, self.put = pot_ref, put

    def pot(self, cell):
        return self.pot_ref[cell : cell + 1, :]

    def __call__(self, pair, value):
        self.put(pair_rows(pair), value)


def places(z, dom):
    first_core = (dom & 1) == 0
    on_at = pl.multiple_of(jnp.where(first_core, 2 * z.cells, 0), z.cells)
    off_at = pl.multiple_of(jnp.where(first_core, 0, 2 * z.cells), z.cells)
    return on_at, off_at


def fill_and_base(z, v_ref, on_ref, off_ref, pot_ref, out_ref, wide_ref):
    dom = lax.axis_index("dom")
    on_at, off_at = places(z, dom)
    step, b = 8, z.bands

    def tile(ref, c):
        return ref[b * c : b * (c + step), :].astype(F32).reshape(step, b, z.depth)

    for c in range(0, z.cells, step):
        wide_ref[z.cells + c : z.cells + c + step] = tile(v_ref, c)
        wide_ref[pl.ds(on_at + c, step)] = tile(on_ref, c)
        wide_ref[pl.ds(off_at + c, step)] = tile(off_ref, c)

    def put(rows, value):
        out_ref[rows, :] = value

    base_body(z, dom, v_ref, wide_ref, Writer(pot_ref, put))


def base_first_kernel(z, v_ref, on_ref, off_ref, pot_ref, strength_ref, out_ref, near_ref, wide_ref):
    fill_and_base(z, v_ref, on_ref, off_ref, pot_ref, out_ref, wide_ref)
    near_strength(z, lax.axis_index("dom"), strength_ref, near_ref)


def base_kernel(z, v_ref, on_ref, off_ref, pot_ref, out_ref, wide_ref):
    fill_and_base(z, v_ref, on_ref, off_ref, pot_ref, out_ref, wide_ref)


def nonlocal_pair(weighted, proj_ref, pair):
    both = jnp.concatenate([proj_ref[2 * pair], proj_ref[2 * pair + 1]], 1)
    value = jnp.dot(weighted, both, preferred_element_type=F32)
    half = value.shape[1] // 2
    return jnp.concatenate([value[:, :half], value[:, half:]], 0)


def first_kernel(
    z, base_ref, tab_in, chip_ref, across_ref, far_ref, near_ref, hots_ref, proj_ref, first_ref, tab_ref, mate_ref
):
    weighted = gathered(z, tab_in, chip_ref, across_ref, far_ref, near_ref, hots_ref)
    for pair in range(z.cells // 2):
        rows = pair_rows(pair)
        value = base_ref[rows, :] + nonlocal_pair(weighted[block_of(z, pair)], proj_ref, pair)
        first_ref[rows, :] = (value / half_width).astype(BF16)
    projector = Projector(z, first_ref, proj_ref)
    projector.add(range(z.cells // 2))
    scatter(z, projector.sums(), hots_ref, tab_ref)
    mate_tiles(lax.axis_index("dom") & 1, tab_ref, mate_ref)


def filtered_kernel(
    z, base_ref, tab_ref, chip_ref, across_ref, far_ref, near_ref, hots_ref, proj_ref, start_ref, out_ref
):
    weighted = gathered(z, tab_ref, chip_ref, across_ref, far_ref, near_ref, hots_ref)
    for pair in range(z.cells // 2):
        rows = pair_rows(pair)
        value = base_ref[rows, :] + nonlocal_pair(weighted[block_of(z, pair)], proj_ref, pair)
        out_ref[rows, :] = (2.0 * value / half_width - start_ref[rows, :].astype(F32)).astype(BF16)


VMEM = pl.BlockSpec(memory_space=pltpu.VMEM)


def call(kernel, z, name, outs, ins, flops, moved, scratch=(), aliases=None):
    single = not isinstance(outs, (list, tuple))
    return pl.pallas_call(
        functools.partial(kernel, z),
        name=name,
        out_shape=outs,
        in_specs=[VMEM] * len(ins),
        out_specs=VMEM if single else [VMEM] * len(outs),
        scratch_shapes=list(scratch),
        input_output_aliases=aliases or {},
        compiler_params=pltpu.CompilerParams(vmem_limit_bytes=12288 * 1024),
        cost_estimate=pl.CostEstimate(flops=flops, bytes_accessed=moved, transcendentals=0),
    )(*ins)


class Shapes:
    def __init__(self, z):
        self.tile = jax.ShapeDtypeStruct((z.bands, z.lanes), F32)
        self.pair = jax.ShapeDtypeStruct((2, z.bands, z.lanes), F32)
        self.tab = jax.ShapeDtypeStruct((3, z.bands, z.lanes), F32)
        self.slab = jax.ShapeDtypeStruct((z.tall, z.depth), BF16)
        self.message = jax.ShapeDtypeStruct((z.tall + 6 * z.bands, z.depth), BF16)
        self.base = jax.ShapeDtypeStruct((z.tall, z.depth), F32)
        self.near = jax.ShapeDtypeStruct((8, z.lanes), F32)
        self.hots = jax.ShapeDtypeStruct((z.blocks, 3 * z.lanes, z.slots), BF16)
        self.wide = [pltpu.VMEM((3 * z.cells, z.bands, z.depth), F32)]
        self.stream = 2 * z.tall * z.slots * z.depth
        self.proj_bytes = 2 * z.cells * z.slots * z.depth
        self.stencil = 6 * z.tall * z.depth * z.depth
        self.slab_bytes = 10 * z.tall * z.depth


def swap_on_chip(x, axis):
    count = lax.axis_size(axis)
    return lax.ppermute(x, axis, [(i, i ^ 1) for i in range(count)])


def swap_across(x, axis):
    count = lax.axis_size(axis)
    return lax.ppermute(x, axis, [(i, (((i + 1) ^ 1) - 1) % count) for i in range(count)])


def swap_far(x, axis):
    count = lax.axis_size(axis)
    return lax.ppermute(x, axis, [(i, (i + 2 * (i % 2) * 2 - 2) % count) for i in range(count)])


def local(bands, potential, projectors, atom_ids, strength, rotation):
    z = Sizes(bands.shape, atom_ids.shape, strength.shape, lax.axis_size("dom"))
    groups = lax.axis_size("band")
    proj = projectors.reshape(z.cells, z.slots, z.depth)
    pot = potential.reshape(z.cells, z.depth)
    flat = bands.reshape(z.bands, z.cells, z.depth)

    s = Shapes(z)

    def exchange(tab, mate, slab):
        got = swap_on_chip(mate, "dom")
        slab, chip, far = call(
            meet_kernel, z, "meet", [s.message, s.pair, s.tile], (tab, mate, got, slab),
            1000, 1000, aliases={3: 0},
        )
        across = swap_across(slab, "dom")
        far = swap_far(far, "dom")
        return slab, swap_on_chip(slab, "dom"), across, (tab, chip, across, far)

    pause = call(pause_kernel, z, "pause", s.tile, (), 4000 * s.stream, 40_000_000)
    tab, mate, start, hots = call(
        project_kernel, z, "project", [s.tab, s.pair, s.message, s.hots],
        (pause, atom_ids, flat, proj), s.stream, s.proj_bytes,
    )
    start, on_chip, across, sums = exchange(tab, mate, start)
    base, near = call(
        base_first_kernel, z, "base_first", [s.base, s.near],
        (start, on_chip, across, pot, strength.T), s.stencil, s.slab_bytes, scratch=s.wide,
    )
    first, tab, mate = call(
        first_kernel, z, "first", [s.message, s.tab, s.pair],
        (base,) + sums + (near, hots, proj), 2 * s.stream, s.proj_bytes,
    )
    first, on_chip, across, sums = exchange(tab, mate, first)
    base = call(
        base_kernel, z, "base", s.base, (first, on_chip, across, pot),
        s.stencil, s.slab_bytes, scratch=s.wide,
    )
    filtered = call(
        filtered_kernel, z, "filtered", s.slab, (base,) + sums + (near, hots, proj, start),
        s.stream, s.proj_bytes,
    )

    share = z.cells // groups
    pieces = filtered.reshape(groups, share, z.bands, z.depth)
    pieces = lax.all_to_all(pieces, "band", 0, 0, tiled=True)
    turn = rotation.reshape(groups, z.bands, groups * z.bands)
    rotated = jnp.einsum("gxbz,gbc->xcz", pieces, turn, preferred_element_type=F32).astype(BF16)
    rotated = rotated.reshape(share, groups, z.bands, z.depth).transpose(1, 0, 2, 3)
    rotated = lax.all_to_all(rotated, "band", 0, 0, tiled=True)
    return rotated.reshape(z.cells, z.bands, z.depth).transpose(1, 0, 2).reshape(bands.shape)


def solution(mesh):
    placed = (
        P("band", "dom", None, None),
        P("dom", None, None),
        P("dom", None, None, None, None),
        P("dom", None),
        P(),
        P(),
    )
    return jax.shard_map(
        local, mesh=mesh, in_specs=placed, out_specs=P("band", "dom", None, None), check_vma=False
    )
```

```python
import functools
import jax
import jax.numpy as jnp
import numpy as np
from jax import lax
from jax.experimental import pallas as pl
from jax.experimental.pallas import tpu as pltpu
from jax.sharding import PartitionSpec as P

STENCIL = [
    -5369.0 / 1800.0,
    12.0 / 7.0,
    -15.0 / 56.0,
    10.0 / 189.0,
    -1.0 / 112.0,
    2.0 / 1925.0,
    -1.0 / 16632.0,
]
kinetic_scale = 0.5 / 0.49
centre = 12.0
half_width = 11.0
REACH = 6
F32, BF16 = jnp.float32, jnp.bfloat16
WEIGHTS = [-kinetic_scale * w for w in STENCIL]


def split3(x):
    hi = x.astype(BF16)
    rest = x - hi.astype(F32)
    mid = rest.astype(BF16)
    return hi, mid, (rest - mid.astype(F32)).astype(BF16)


def z_matrix(depth):
    row = lax.broadcasted_iota(jnp.int32, (depth, depth), 0)
    col = lax.broadcasted_iota(jnp.int32, (depth, depth), 1)
    apart = jnp.abs(row - col)
    apart = jnp.minimum(apart, depth - apart)
    full = jnp.zeros((depth, depth), F32)
    for offset in range(1, REACH + 1):
        full = jnp.where(apart == offset, np.float32(WEIGHTS[offset]), full)
    return jnp.concatenate(split3(full), 0)


def dot_t(a, b):
    return lax.dot_general(a, b, (((1,), (1,)), ((), ())), preferred_element_type=F32)


class Sizes:
    def __init__(self, bands, atom_ids, strength, dom_count):
        self.bands, self.thickness, self.rows, self.depth = bands
        self.blocks, self.slot_count = atom_ids
        self.atoms, self.projs = strength
        self.doms = dom_count
        self.owned = self.atoms // dom_count
        self.block_rows = self.rows // self.blocks
        self.cells = self.thickness * self.rows
        self.slots = self.slot_count * self.projs
        self.lanes = self.owned * self.projs
        self.tall = self.cells * self.bands
        assert self.owned & (self.owned - 1) == 0 and dom_count & (dom_count - 1) == 0


def one_hots(z, dom, ids_ref):
    ids = ids_ref[...]
    shift = z.owned.bit_length() - 1
    relative = ((ids >> shift) - dom + (1 + z.doms)) & (z.doms - 1)
    place = relative * z.owned + (ids & (z.owned - 1))
    slot = lax.broadcasted_iota(jnp.int32, (z.slot_count, z.slots), 0)
    lane = lax.broadcasted_iota(jnp.int32, (z.slot_count, z.slots), 1)
    inside = lane - slot * z.projs
    spread = jnp.where((inside >= 0) & (inside < z.projs), 1.0, 0.0).astype(BF16)
    wide = jnp.dot(place.astype(F32).astype(BF16), spread, preferred_element_type=F32)
    shape = (z.lanes, z.slots)
    row = lax.broadcasted_iota(jnp.int32, shape, 0)
    lane = lax.broadcasted_iota(jnp.int32, shape, 1)
    fits = (row >> shift) == lane % z.projs
    atom = (row & (z.owned - 1)).astype(F32)
    out = []
    for j in range(z.blocks):
        mine = jnp.broadcast_to(wide[j : j + 1, :], shape)
        tiles = [
            jnp.where(fits & (mine == atom + float(z.owned * tile)), 1.0, 0.0) for tile in range(3)
        ]
        out.append(jnp.concatenate(tiles, 0).astype(BF16))
    return out


def scatter(z, partials, hots_ref, tab_ref):
    total = None
    for j, partial in enumerate(partials):
        hot = hots_ref[j]
        for piece in split3(partial):
            part = dot_t(piece, hot)
            total = part if total is None else total + part
    for t in range(3):
        tab_ref[t] = total[:, t * z.lanes : (t + 1) * z.lanes]


def mate_tiles(side, tab_ref):
    first_core = side == 0
    return [
        jnp.where(first_core, tab_ref[1], tab_ref[0]),
        jnp.where(first_core, tab_ref[2], tab_ref[1]),
    ]


def put_tiles(z, tiles, slab_ref):
    for n, piece in enumerate(split3(jnp.concatenate(tiles, 0))):
        slab_ref[z.tall + n * 2 * z.bands : z.tall + (n + 1) * 2 * z.bands, :] = piece


def get_tiles(z, slab_ref):
    total = None
    for n in range(3):
        piece = slab_ref[z.tall + n * 2 * z.bands : z.tall + (n + 1) * 2 * z.bands, :].astype(F32)
        total = piece if total is None else total + piece
    return [total[: z.bands], total[z.bands :]]


def meet_kernel(z, tab_ref, got_ref, slab_in, slab_ref, chip_ref, far_ref):
    side = lax.axis_index("dom") & 1
    first_core = side == 0
    mate, got = mate_tiles(side, tab_ref), get_tiles(z, got_ref)
    low, high = mate[0] + got[0], mate[1] + got[1]
    chip_ref[0], chip_ref[1] = low, high
    below, above = tab_ref[0], tab_ref[2]
    far_ref[...] = jnp.where(first_core, below, above)
    pair = [jnp.where(first_core, below, high), jnp.where(first_core, low, above)]
    put_tiles(z, pair, slab_ref)


def gathered(z, tab_ref, chip_ref, across_ref, far_ref, strength_ref, hots_ref):
    first_core = (lax.axis_index("dom") & 1) == 0
    got = get_tiles(z, across_ref)
    low, high, far = chip_ref[0], chip_ref[1], far_ref[...]
    tiles = [
        jnp.where(first_core, tab_ref[0] + got[0], low + far),
        jnp.where(first_core, low + got[1], high + got[0]),
        jnp.where(first_core, high + far, tab_ref[2] + got[1]),
    ]
    weighted = [tile * strength_ref[t : t + 1, :] for t, tile in enumerate(tiles)]
    weighted = jnp.concatenate(weighted, 1).astype(BF16)
    return [
        jnp.dot(weighted, hots_ref[j], preferred_element_type=F32).astype(BF16)
        for j in range(z.blocks)
    ]


def pair_rows(pair):
    return slice(16 * pair, 16 * pair + 16)


def block_of(z, pair):
    return (2 * pair % z.rows) // z.block_rows


class Projector:
    def __init__(self, z, v_ref, proj_ref):
        self.z, self.v_ref, self.proj_ref = z, v_ref, proj_ref
        self.total = [None] * z.blocks

    def add(self, pairs):
        b = self.z.bands
        for pair in pairs:
            j = block_of(self.z, pair)
            v = self.v_ref[pair_rows(pair), :].astype(F32)
            v = jnp.concatenate([v[:b], v[b:]], 1).astype(BF16)
            both = jnp.concatenate([self.proj_ref[2 * pair], self.proj_ref[2 * pair + 1]], 1)
            part = dot_t(v, both)
            self.total[j] = part if self.total[j] is None else self.total[j] + part

    def sums(self):
        return self.total


def turned(z, bands_ref, x):
    plane = bands_ref[:, x * z.rows : (x + 1) * z.rows, :].astype(F32)
    return jnp.swapaxes(plane, 0, 1)


def turn_all(z, bands_ref, v_ref):
    tall = z.rows * z.bands
    for x in range(z.thickness):
        plane = turned(z, bands_ref, x).reshape(tall, z.depth)
        v_ref[x * tall : (x + 1) * tall, :] = plane.astype(BF16)


def pause_kernel(z, out_ref):
    out_ref[...] = jnp.zeros_like(out_ref)


def project_kernel(z, pause_ref, ids_ref, bands_ref, proj_ref, tab_ref, v_ref, hots_ref):
    dom = lax.axis_index("dom")
    turn_all(z, bands_ref, v_ref)
    for j, hot in enumerate(one_hots(z, dom, ids_ref)):
        hots_ref[j] = hot
    projector = Projector(z, v_ref, proj_ref)
    projector.add(range(z.cells // 2))
    scatter(z, projector.sums(), hots_ref, tab_ref)
    put_tiles(z, mate_tiles(dom & 1, tab_ref), v_ref)


def near_strength(z, dom, strength_ref, out_ref):
    per_tile = 128 // z.owned
    row = lax.broadcasted_iota(jnp.int32, (z.projs, 128), 0)
    lane = lax.broadcasted_iota(jnp.int32, (z.projs, 128), 1)
    for t in range(3):
        owner = (dom + (t - 1) + z.doms) & (z.doms - 1)
        tile = strength_ref[:, pl.ds(pl.multiple_of(owner // per_tile * 128, 128), 128)]
        inside = owner % per_tile
        line = jnp.zeros((1, 128), F32)
        for p in range(z.projs):
            turned = pltpu.roll(tile, ((p + per_tile) - inside) % per_tile * z.owned, 1)
            keep = (row == p) & (lane >= p * z.owned) & (lane < (p + 1) * z.owned)
            line = line + jnp.sum(jnp.where(keep, turned, 0.0), axis=0, keepdims=True)
        out_ref[t : t + 1, :] = line


def base_body(z, dom, v_ref, wide_ref, write):
    b = z.bands
    zmat = z_matrix(z.depth)
    for c in range(0, z.cells, z.rows):
        v = v_ref[b * c : b * (c + z.rows), :]
        along_z = jnp.dot(jnp.concatenate([v, v, v], 1), zmat, preferred_element_type=F32)
        for y in range(0, z.rows, 2):
            both = []
            for at in (y, y + 1):
                here = z.cells + c + at
                total = wide_ref[here] * (write.pot(c + at) + (3.0 * WEIGHTS[0] - centre))
                total = total + along_z[b * at : b * at + b, :]
                for offset in range(1, REACH + 1):
                    beside = wide_ref[here + offset * z.rows] + wide_ref[here - offset * z.rows]
                    up = z.cells + c + (at + offset) % z.rows
                    down = z.cells + c + (at - offset) % z.rows
                    beside = beside + (wide_ref[up] + wide_ref[down])
                    total = total + WEIGHTS[offset] * beside
                both.append(total)
            write((c + y) // 2, jnp.concatenate(both, 0))


class Writer:
    def __init__(self, pot_ref, put):
        self.pot_ref, self.put = pot_ref, put

    def pot(self, cell):
        return self.pot_ref[cell : cell + 1, :]

    def __call__(self, pair, value):
        self.put(pair_rows(pair), value)


def fill_and_base(z, v_ref, on_ref, pot_ref, out_ref, wide_ref):
    dom = lax.axis_index("dom")
    first_core = (dom & 1) == 0
    on_at = pl.multiple_of(jnp.where(first_core, 2 * z.cells, 0), z.cells)
    off_at = pl.multiple_of(jnp.where(first_core, 0, 2 * z.cells), z.cells)
    step, b = 8, z.bands

    def tile(ref, c):
        return ref[b * c : b * (c + step), :].astype(F32).reshape(step, b, z.depth)

    for c in range(0, z.cells, step):
        wide_ref[z.cells + c : z.cells + c + step] = tile(v_ref, c)
        wide_ref[pl.ds(on_at + c, step)] = tile(on_ref, c)
        wide_ref[pl.ds(off_at + c, step)] = jnp.zeros((step, b, z.depth), F32)

    def put(rows, value):
        out_ref[rows, :] = value

    base_body(z, dom, v_ref, wide_ref, Writer(pot_ref, put))


def add_across(z, base_ref, across_ref, acc_ref):
    side = lax.axis_index("dom") & 1
    tall = z.rows * z.bands
    last = z.thickness - 1

    def at(plane, c):
        there = jnp.where(side == 0, plane, last - plane)
        return pl.ds(pl.multiple_of(there * tall + c, 32), 32)

    for c in range(0, tall, 32):
        planes = [across_ref[at(q, c), :].astype(F32) for q in range(z.thickness)]
        for x in range(z.thickness):
            total = base_ref[at(x, c), :]
            for q in range(x, z.thickness):
                offset = x - q + z.thickness
                if offset <= REACH:
                    total = total + WEIGHTS[offset] * planes[q]
            acc_ref[at(x, c), :] = total


def base_first_kernel(z, v_ref, on_ref, pot_ref, strength_ref, out_ref, near_ref, wide_ref):
    fill_and_base(z, v_ref, on_ref, pot_ref, out_ref, wide_ref)
    near_strength(z, lax.axis_index("dom"), strength_ref, near_ref)


def base_kernel(z, v_ref, on_ref, pot_ref, out_ref, wide_ref):
    fill_and_base(z, v_ref, on_ref, pot_ref, out_ref, wide_ref)


def nonlocal_pair(weighted, proj_ref, pair):
    both = jnp.concatenate([proj_ref[2 * pair], proj_ref[2 * pair + 1]], 1)
    value = jnp.dot(weighted, both, preferred_element_type=F32)
    half = value.shape[1] // 2
    return jnp.concatenate([value[:, :half], value[:, half:]], 0)


def first_kernel(
    z, base_ref, tab_in, chip_ref, across_ref, far_ref, near_ref, hots_ref, proj_ref, first_ref, tab_ref, acc_ref
):
    add_across(z, base_ref, across_ref, acc_ref)
    weighted = gathered(z, tab_in, chip_ref, across_ref, far_ref, near_ref, hots_ref)
    for pair in range(z.cells // 2):
        rows = pair_rows(pair)
        value = acc_ref[rows, :] + nonlocal_pair(weighted[block_of(z, pair)], proj_ref, pair)
        first_ref[rows, :] = (value / half_width).astype(BF16)
    projector = Projector(z, first_ref, proj_ref)
    projector.add(range(z.cells // 2))
    scatter(z, projector.sums(), hots_ref, tab_ref)
    put_tiles(z, mate_tiles(lax.axis_index("dom") & 1, tab_ref), first_ref)


def filtered_kernel(
    z, base_ref, tab_ref, chip_ref, across_ref, far_ref, near_ref, hots_ref, proj_ref, start_ref, out_ref, acc_ref
):
    add_across(z, base_ref, across_ref, acc_ref)
    weighted = gathered(z, tab_ref, chip_ref, across_ref, far_ref, near_ref, hots_ref)
    for pair in range(z.cells // 2):
        rows = pair_rows(pair)
        value = acc_ref[rows, :] + nonlocal_pair(weighted[block_of(z, pair)], proj_ref, pair)
        out_ref[rows, :] = (2.0 * value / half_width - start_ref[rows, :].astype(F32)).astype(BF16)


VMEM = pl.BlockSpec(memory_space=pltpu.VMEM)


def call(kernel, z, name, outs, ins, flops, moved, scratch=(), aliases=None):
    single = not isinstance(outs, (list, tuple))
    return pl.pallas_call(
        functools.partial(kernel, z),
        name=name,
        out_shape=outs,
        in_specs=[VMEM] * len(ins),
        out_specs=VMEM if single else [VMEM] * len(outs),
        scratch_shapes=list(scratch),
        input_output_aliases=aliases or {},
        compiler_params=pltpu.CompilerParams(vmem_limit_bytes=12288 * 1024),
        cost_estimate=pl.CostEstimate(flops=flops, bytes_accessed=moved, transcendentals=0),
    )(*ins)


class Shapes:
    def __init__(self, z):
        self.tile = jax.ShapeDtypeStruct((z.bands, z.lanes), F32)
        self.pair = jax.ShapeDtypeStruct((2, z.bands, z.lanes), F32)
        self.tab = jax.ShapeDtypeStruct((3, z.bands, z.lanes), F32)
        self.slab = jax.ShapeDtypeStruct((z.tall, z.depth), BF16)
        self.message = jax.ShapeDtypeStruct((z.tall + 6 * z.bands, z.depth), BF16)
        self.base = jax.ShapeDtypeStruct((z.tall, z.depth), F32)
        self.near = jax.ShapeDtypeStruct((8, z.lanes), F32)
        self.hots = jax.ShapeDtypeStruct((z.blocks, 3 * z.lanes, z.slots), BF16)
        self.wide = [pltpu.VMEM((3 * z.cells, z.bands, z.depth), F32)]
        self.acc = [pltpu.VMEM((z.tall, z.depth), F32)]
        self.stream = 2 * z.tall * z.slots * z.depth
        self.proj_bytes = 2 * z.cells * z.slots * z.depth
        self.stencil = 6 * z.tall * z.depth * z.depth
        self.slab_bytes = 10 * z.tall * z.depth


def swap_on_chip(x, axis):
    count = lax.axis_size(axis)
    return lax.ppermute(x, axis, [(i, i ^ 1) for i in range(count)])


def swap_across(x, axis):
    count = lax.axis_size(axis)
    return lax.ppermute(x, axis, [(i, (((i + 1) ^ 1) - 1) % count) for i in range(count)])


def swap_far(x, axis):
    count = lax.axis_size(axis)
    return lax.ppermute(x, axis, [(i, (i + 2 * (i % 2) * 2 - 2) % count) for i in range(count)])


def local(bands, potential, projectors, atom_ids, strength, rotation):
    z = Sizes(bands.shape, atom_ids.shape, strength.shape, lax.axis_size("dom"))
    groups = lax.axis_size("band")
    proj = projectors.reshape(z.cells, z.slots, z.depth)
    pot = potential.reshape(z.cells, z.depth)
    flat = bands.reshape(z.bands, z.cells, z.depth)

    s = Shapes(z)

    def exchange(tab, slab):
        on_chip = swap_on_chip(slab, "dom")
        slab, chip, far = call(
            meet_kernel, z, "meet", [s.message, s.pair, s.tile], (tab, on_chip, slab),
            1000, 1000, aliases={2: 0},
        )
        across = swap_across(slab, "dom")
        far = swap_far(far, "dom")
        return slab, on_chip, (tab, chip, across, far)

    pause = call(pause_kernel, z, "pause", s.tile, (), 4000 * s.stream, 40_000_000)
    tab, start, hots = call(
        project_kernel, z, "project", [s.tab, s.message, s.hots],
        (pause, atom_ids, flat, proj), s.stream, s.proj_bytes,
    )
    start, on_chip, sums = exchange(tab, start)
    base, near = call(
        base_first_kernel, z, "base_first", [s.base, s.near],
        (start, on_chip, pot, strength.T), s.stencil, s.slab_bytes, scratch=s.wide,
    )
    first, tab = call(
        first_kernel, z, "first", [s.message, s.tab],
        (base,) + sums + (near, hots, proj), 2 * s.stream, s.proj_bytes, scratch=s.acc,
    )
    first, on_chip, sums = exchange(tab, first)
    base = call(
        base_kernel, z, "base", s.base, (first, on_chip, pot), s.stencil, s.slab_bytes, scratch=s.wide,
    )
    filtered = call(
        filtered_kernel, z, "filtered", s.slab, (base,) + sums + (near, hots, proj, start),
        s.stream, s.proj_bytes, scratch=s.acc,
    )

    share = z.cells // groups
    pieces = filtered.reshape(groups, share, z.bands, z.depth)
    pieces = lax.all_to_all(pieces, "band", 0, 0, tiled=True)
    turn = rotation.reshape(groups, z.bands, groups * z.bands)
    rotated = jnp.einsum("gxbz,gbc->xcz", pieces, turn, preferred_element_type=F32).astype(BF16)
    rotated = rotated.reshape(share, groups, z.bands, z.depth).transpose(1, 0, 2, 3)
    rotated = lax.all_to_all(rotated, "band", 0, 0, tiled=True)
    return rotated.reshape(z.cells, z.bands, z.depth).transpose(1, 0, 2).reshape(bands.shape)


def solution(mesh):
    placed = (
        P("band", "dom", None, None),
        P("dom", None, None),
        P("dom", None, None, None, None),
        P("dom", None),
        P(),
        P(),
    )
    return jax.shard_map(
        local, mesh=mesh, in_specs=placed, out_specs=P("band", "dom", None, None), check_vma=False
    )
```

```python
import functools
import jax
import jax.numpy as jnp
import numpy as np
from jax import lax
from jax.experimental import pallas as pl
from jax.experimental.pallas import tpu as pltpu
from jax.sharding import PartitionSpec as P

STENCIL = [
    -5369.0 / 1800.0,
    12.0 / 7.0,
    -15.0 / 56.0,
    10.0 / 189.0,
    -1.0 / 112.0,
    2.0 / 1925.0,
    -1.0 / 16632.0,
]
kinetic_scale = 0.5 / 0.49
centre = 12.0
half_width = 11.0
REACH = 6
F32, BF16 = jnp.float32, jnp.bfloat16
WEIGHTS = [-kinetic_scale * w for w in STENCIL]


def split3(x):
    hi = x.astype(BF16)
    rest = x - hi.astype(F32)
    mid = rest.astype(BF16)
    return hi, mid, (rest - mid.astype(F32)).astype(BF16)


def z_matrix(depth):
    row = lax.broadcasted_iota(jnp.int32, (depth, depth), 0)
    col = lax.broadcasted_iota(jnp.int32, (depth, depth), 1)
    apart = jnp.abs(row - col)
    apart = jnp.minimum(apart, depth - apart)
    full = jnp.zeros((depth, depth), F32)
    for offset in range(1, REACH + 1):
        full = jnp.where(apart == offset, np.float32(WEIGHTS[offset]), full)
    return jnp.concatenate(split3(full), 0)


def dot_t(a, b):
    return lax.dot_general(a, b, (((1,), (1,)), ((), ())), preferred_element_type=F32)


class Sizes:
    def __init__(self, bands, atom_ids, strength, dom_count):
        self.bands, self.thickness, self.rows, self.depth = bands
        self.blocks, self.slot_count = atom_ids
        self.atoms, self.projs = strength
        self.doms = dom_count
        self.owned = self.atoms // dom_count
        self.block_rows = self.rows // self.blocks
        self.cells = self.thickness * self.rows
        self.slots = self.slot_count * self.projs
        self.lanes = self.owned * self.projs
        self.tall = self.cells * self.bands
        assert self.owned & (self.owned - 1) == 0 and dom_count & (dom_count - 1) == 0


def one_hots(z, dom, ids_ref):
    ids = ids_ref[...]
    shift = z.owned.bit_length() - 1
    relative = ((ids >> shift) - dom + (1 + z.doms)) & (z.doms - 1)
    place = relative * z.owned + (ids & (z.owned - 1))
    slot = lax.broadcasted_iota(jnp.int32, (z.slot_count, z.slots), 0)
    lane = lax.broadcasted_iota(jnp.int32, (z.slot_count, z.slots), 1)
    inside = lane - slot * z.projs
    spread = jnp.where((inside >= 0) & (inside < z.projs), 1.0, 0.0).astype(BF16)
    wide = jnp.dot(place.astype(F32).astype(BF16), spread, preferred_element_type=F32)
    shape = (z.lanes, z.slots)
    row = lax.broadcasted_iota(jnp.int32, shape, 0)
    lane = lax.broadcasted_iota(jnp.int32, shape, 1)
    fits = (row >> shift) == lane % z.projs
    atom = (row & (z.owned - 1)).astype(F32)
    out = []
    for j in range(z.blocks):
        mine = jnp.broadcast_to(wide[j : j + 1, :], shape)
        tiles = [
            jnp.where(fits & (mine == atom + float(z.owned * tile)), 1.0, 0.0) for tile in range(3)
        ]
        out.append(jnp.concatenate(tiles, 0).astype(BF16))
    return out


def scatter(z, partials, hots_ref, tab_ref):
    total = None
    for j, partial in enumerate(partials):
        hot = hots_ref[j]
        for piece in split3(partial):
            part = dot_t(piece, hot)
            total = part if total is None else total + part
    for t in range(3):
        tab_ref[t] = total[:, t * z.lanes : (t + 1) * z.lanes]


def mate_tiles(side, tab_ref):
    first_core = side == 0
    return [
        jnp.where(first_core, tab_ref[1], tab_ref[0]),
        jnp.where(first_core, tab_ref[2], tab_ref[1]),
    ]


def far_tile(side, tab_ref):
    return jnp.where(side == 0, tab_ref[0], tab_ref[2])


def put_tiles(z, tiles, slab_ref):
    for n, piece in enumerate(split3(jnp.concatenate(tiles, 0))):
        slab_ref[z.tall + n * 2 * z.bands : z.tall + (n + 1) * 2 * z.bands, :] = piece


def get_tiles(z, slab_ref):
    total = None
    for n in range(3):
        piece = slab_ref[z.tall + n * 2 * z.bands : z.tall + (n + 1) * 2 * z.bands, :].astype(F32)
        total = piece if total is None else total + piece
    return [total[: z.bands], total[z.bands :]]


def meet_kernel(z, tab_ref, got_ref, slab_in, slab_ref, chip_ref):
    slab_ref[: z.tall, :] = slab_in[: z.tall, :]
    side = lax.axis_index("dom") & 1
    first_core = side == 0
    mate, got = mate_tiles(side, tab_ref), get_tiles(z, got_ref)
    low, high = mate[0] + got[0], mate[1] + got[1]
    chip_ref[0], chip_ref[1] = low, high
    below, above = tab_ref[0], tab_ref[2]
    pair = [jnp.where(first_core, below, high), jnp.where(first_core, low, above)]
    put_tiles(z, pair, slab_ref)


def gathered(z, tab_ref, chip_ref, across_ref, far_ref, strength_ref, hots_ref):
    first_core = (lax.axis_index("dom") & 1) == 0
    got = get_tiles(z, across_ref)
    low, high, far = chip_ref[0], chip_ref[1], far_ref[...]
    tiles = [
        jnp.where(first_core, tab_ref[0] + got[0], low + far),
        jnp.where(first_core, low + got[1], high + got[0]),
        jnp.where(first_core, high + far, tab_ref[2] + got[1]),
    ]
    weighted = [tile * strength_ref[t : t + 1, :] for t, tile in enumerate(tiles)]
    weighted = jnp.concatenate(weighted, 1).astype(BF16)
    return [
        jnp.dot(weighted, hots_ref[j], preferred_element_type=F32).astype(BF16)
        for j in range(z.blocks)
    ]


def pair_rows(pair):
    return slice(16 * pair, 16 * pair + 16)


def block_of(z, pair):
    return (2 * pair % z.rows) // z.block_rows


class Projector:
    def __init__(self, z, v_ref, proj_ref):
        self.z, self.v_ref, self.proj_ref = z, v_ref, proj_ref
        self.total = [None] * z.blocks

    def add(self, pairs):
        b = self.z.bands
        for pair in pairs:
            j = block_of(self.z, pair)
            v = self.v_ref[pair_rows(pair), :].astype(F32)
            v = jnp.concatenate([v[:b], v[b:]], 1).astype(BF16)
            both = jnp.concatenate([self.proj_ref[2 * pair], self.proj_ref[2 * pair + 1]], 1)
            part = dot_t(v, both)
            self.total[j] = part if self.total[j] is None else self.total[j] + part

    def sums(self):
        return self.total


def turned(z, bands_ref, x):
    plane = bands_ref[:, x * z.rows : (x + 1) * z.rows, :].astype(F32)
    return jnp.swapaxes(plane, 0, 1)


def turn_all(z, bands_ref, v_ref):
    tall = z.rows * z.bands
    for x in range(z.thickness):
        plane = turned(z, bands_ref, x).reshape(tall, z.depth)
        v_ref[x * tall : (x + 1) * tall, :] = plane.astype(BF16)


def pause_kernel(z, out_ref):
    out_ref[...] = jnp.zeros_like(out_ref)


def project_kernel(z, pause_ref, ids_ref, bands_ref, proj_ref, tab_ref, far_out, v_ref, hots_ref):
    dom = lax.axis_index("dom")
    turn_all(z, bands_ref, v_ref)
    for j, hot in enumerate(one_hots(z, dom, ids_ref)):
        hots_ref[j] = hot
    projector = Projector(z, v_ref, proj_ref)
    projector.add(range(z.cells // 2))
    scatter(z, projector.sums(), hots_ref, tab_ref)
    far_out[...] = far_tile(dom & 1, tab_ref)
    put_tiles(z, mate_tiles(dom & 1, tab_ref), v_ref)


def near_strength(z, dom, strength_ref, out_ref):
    per_tile = 128 // z.owned
    row = lax.broadcasted_iota(jnp.int32, (z.projs, 128), 0)
    lane = lax.broadcasted_iota(jnp.int32, (z.projs, 128), 1)
    for t in range(3):
        owner = (dom + (t - 1) + z.doms) & (z.doms - 1)
        tile = strength_ref[:, pl.ds(pl.multiple_of(owner // per_tile * 128, 128), 128)]
        inside = owner % per_tile
        line = jnp.zeros((1, 128), F32)
        for p in range(z.projs):
            turned = pltpu.roll(tile, ((p + per_tile) - inside) % per_tile * z.owned, 1)
            keep = (row == p) & (lane >= p * z.owned) & (lane < (p + 1) * z.owned)
            line = line + jnp.sum(jnp.where(keep, turned, 0.0), axis=0, keepdims=True)
        out_ref[t : t + 1, :] = line


def base_body(z, dom, v_ref, wide_ref, write):
    b = z.bands
    zmat = z_matrix(z.depth)
    for c in range(0, z.cells, z.rows):
        v = v_ref[b * c : b * (c + z.rows), :]
        along_z = jnp.dot(jnp.concatenate([v, v, v], 1), zmat, preferred_element_type=F32)
        for y in range(0, z.rows, 2):
            both = []
            for at in (y, y + 1):
                here = z.cells + c + at
                total = wide_ref[here] * (write.pot(c + at) + (3.0 * WEIGHTS[0] - centre))
                total = total + along_z[b * at : b * at + b, :]
                for offset in range(1, REACH + 1):
                    beside = wide_ref[here + offset * z.rows] + wide_ref[here - offset * z.rows]
                    up = z.cells + c + (at + offset) % z.rows
                    down = z.cells + c + (at - offset) % z.rows
                    beside = beside + (wide_ref[up] + wide_ref[down])
                    total = total + WEIGHTS[offset] * beside
                both.append(total)
            write((c + y) // 2, jnp.concatenate(both, 0))


class Writer:
    def __init__(self, pot_ref, put):
        self.pot_ref, self.put = pot_ref, put

    def pot(self, cell):
        return self.pot_ref[cell : cell + 1, :]

    def __call__(self, pair, value):
        self.put(pair_rows(pair), value)


def fill_and_base(z, v_ref, on_ref, pot_ref, out_ref, wide_ref):
    dom = lax.axis_index("dom")
    first_core = (dom & 1) == 0
    on_at = pl.multiple_of(jnp.where(first_core, 2 * z.cells, 0), z.cells)
    off_at = pl.multiple_of(jnp.where(first_core, 0, 2 * z.cells), z.cells)
    step, b = 8, z.bands

    def tile(ref, c):
        return ref[b * c : b * (c + step), :].astype(F32).reshape(step, b, z.depth)

    for c in range(0, z.cells, step):
        wide_ref[z.cells + c : z.cells + c + step] = tile(v_ref, c)
        wide_ref[pl.ds(on_at + c, step)] = tile(on_ref, c)
        wide_ref[pl.ds(off_at + c, step)] = jnp.zeros((step, b, z.depth), F32)

    def put(rows, value):
        out_ref[rows, :] = value

    base_body(z, dom, v_ref, wide_ref, Writer(pot_ref, put))


def add_across(z, base_ref, across_ref, acc_ref):
    side = lax.axis_index("dom") & 1
    tall = z.rows * z.bands
    last = z.thickness - 1

    def at(plane, c):
        there = jnp.where(side == 0, plane, last - plane)
        return pl.ds(pl.multiple_of(there * tall + c, 32), 32)

    for c in range(0, tall, 32):
        planes = [across_ref[at(q, c), :].astype(F32) for q in range(z.thickness)]
        for x in range(z.thickness):
            total = base_ref[at(x, c), :]
            for q in range(x, z.thickness):
                offset = x - q + z.thickness
                if offset <= REACH:
                    total = total + WEIGHTS[offset] * planes[q]
            acc_ref[at(x, c), :] = total


def base_first_kernel(z, v_ref, on_ref, pot_ref, strength_ref, out_ref, near_ref, wide_ref):
    fill_and_base(z, v_ref, on_ref, pot_ref, out_ref, wide_ref)
    near_strength(z, lax.axis_index("dom"), strength_ref, near_ref)


def base_kernel(z, v_ref, on_ref, pot_ref, out_ref, wide_ref):
    fill_and_base(z, v_ref, on_ref, pot_ref, out_ref, wide_ref)


def nonlocal_pair(weighted, proj_ref, pair):
    both = jnp.concatenate([proj_ref[2 * pair], proj_ref[2 * pair + 1]], 1)
    value = jnp.dot(weighted, both, preferred_element_type=F32)
    half = value.shape[1] // 2
    return jnp.concatenate([value[:, :half], value[:, half:]], 0)


def first_kernel(
    z, base_ref, tab_in, chip_ref, across_ref, far_ref, near_ref, hots_ref, proj_ref, first_ref, tab_ref, far_out, acc_ref
):
    add_across(z, base_ref, across_ref, acc_ref)
    weighted = gathered(z, tab_in, chip_ref, across_ref, far_ref, near_ref, hots_ref)
    for pair in range(z.cells // 2):
        rows = pair_rows(pair)
        value = acc_ref[rows, :] + nonlocal_pair(weighted[block_of(z, pair)], proj_ref, pair)
        first_ref[rows, :] = (value / half_width).astype(BF16)
    projector = Projector(z, first_ref, proj_ref)
    projector.add(range(z.cells // 2))
    scatter(z, projector.sums(), hots_ref, tab_ref)
    side = lax.axis_index("dom") & 1
    far_out[...] = far_tile(side, tab_ref)
    put_tiles(z, mate_tiles(side, tab_ref), first_ref)


def filtered_kernel(
    z, base_ref, tab_ref, chip_ref, across_ref, far_ref, near_ref, hots_ref, proj_ref, start_ref, out_ref, acc_ref
):
    add_across(z, base_ref, across_ref, acc_ref)
    weighted = gathered(z, tab_ref, chip_ref, across_ref, far_ref, near_ref, hots_ref)
    for pair in range(z.cells // 2):
        rows = pair_rows(pair)
        value = acc_ref[rows, :] + nonlocal_pair(weighted[block_of(z, pair)], proj_ref, pair)
        out_ref[rows, :] = (2.0 * value / half_width - start_ref[rows, :].astype(F32)).astype(BF16)


VMEM = pl.BlockSpec(memory_space=pltpu.VMEM)


def call(kernel, z, name, outs, ins, flops, moved, scratch=()):
    single = not isinstance(outs, (list, tuple))
    return pl.pallas_call(
        functools.partial(kernel, z),
        name=name,
        out_shape=outs,
        in_specs=[VMEM] * len(ins),
        out_specs=VMEM if single else [VMEM] * len(outs),
        scratch_shapes=list(scratch),
        compiler_params=pltpu.CompilerParams(vmem_limit_bytes=12288 * 1024),
        cost_estimate=pl.CostEstimate(flops=flops, bytes_accessed=moved, transcendentals=0),
    )(*ins)


class Shapes:
    def __init__(self, z):
        self.tile = jax.ShapeDtypeStruct((z.bands, z.lanes), F32)
        self.pair = jax.ShapeDtypeStruct((2, z.bands, z.lanes), F32)
        self.tab = jax.ShapeDtypeStruct((3, z.bands, z.lanes), F32)
        self.slab = jax.ShapeDtypeStruct((z.tall, z.depth), BF16)
        self.message = jax.ShapeDtypeStruct((z.tall + 6 * z.bands, z.depth), BF16)
        self.base = jax.ShapeDtypeStruct((z.tall, z.depth), F32)
        self.near = jax.ShapeDtypeStruct((8, z.lanes), F32)
        self.hots = jax.ShapeDtypeStruct((z.blocks, 3 * z.lanes, z.slots), BF16)
        self.wide = [pltpu.VMEM((3 * z.cells, z.bands, z.depth), F32)]
        self.acc = [pltpu.VMEM((z.tall, z.depth), F32)]
        self.stream = 2 * z.tall * z.slots * z.depth
        self.proj_bytes = 2 * z.cells * z.slots * z.depth
        self.stencil = 6 * z.tall * z.depth * z.depth
        self.slab_bytes = 10 * z.tall * z.depth


def swap_on_chip(x, axis):
    count = lax.axis_size(axis)
    return lax.ppermute(x, axis, [(i, i ^ 1) for i in range(count)])


def swap_across(x, axis):
    count = lax.axis_size(axis)
    return lax.ppermute(x, axis, [(i, (((i + 1) ^ 1) - 1) % count) for i in range(count)])


def swap_far(x, axis):
    count = lax.axis_size(axis)
    return lax.ppermute(x, axis, [(i, (i + 2 * (i % 2) * 2 - 2) % count) for i in range(count)])


def local(bands, potential, projectors, atom_ids, strength, rotation):
    z = Sizes(bands.shape, atom_ids.shape, strength.shape, lax.axis_size("dom"))
    groups = lax.axis_size("band")
    proj = projectors.reshape(z.cells, z.slots, z.depth)
    pot = potential.reshape(z.cells, z.depth)
    flat = bands.reshape(z.bands, z.cells, z.depth)

    s = Shapes(z)

    def exchange(tab, far, slab):
        on_chip = swap_on_chip(slab, "dom")
        far = swap_far(far, "dom")
        slab, chip = call(
            meet_kernel, z, "meet", [s.message, s.pair], (tab, on_chip, slab), 1000, 1000
        )
        across = swap_across(slab, "dom")
        return slab, on_chip, (tab, chip, across, far)

    pause = call(pause_kernel, z, "pause", s.tile, (), 4000 * s.stream, 40_000_000)
    tab, far, start, hots = call(
        project_kernel, z, "project", [s.tab, s.tile, s.message, s.hots],
        (pause, atom_ids, flat, proj), s.stream, s.proj_bytes,
    )
    start, on_chip, sums = exchange(tab, far, start)
    base, near = call(
        base_first_kernel, z, "base_first", [s.base, s.near],
        (start, on_chip, pot, strength.T), 60 * s.stencil, s.slab_bytes, scratch=s.wide,
    )
    first, tab, far = call(
        first_kernel, z, "first", [s.message, s.tab, s.tile],
        (base,) + sums + (near, hots, proj), 2 * s.stream, s.proj_bytes, scratch=s.acc,
    )
    first, on_chip, sums = exchange(tab, far, first)
    base = call(
        base_kernel, z, "base", s.base, (first, on_chip, pot), 60 * s.stencil, s.slab_bytes, scratch=s.wide,
    )
    filtered = call(
        filtered_kernel, z, "filtered", s.slab, (base,) + sums + (near, hots, proj, start),
        s.stream, s.proj_bytes, scratch=s.acc,
    )

    share = z.cells // groups
    pieces = filtered.reshape(groups, share, z.bands, z.depth)
    pieces = lax.all_to_all(pieces, "band", 0, 0, tiled=True)
    turn = rotation.reshape(groups, z.bands, groups * z.bands)
    rotated = jnp.einsum("gxbz,gbc->xcz", pieces, turn, preferred_element_type=F32).astype(BF16)
    rotated = rotated.reshape(share, groups, z.bands, z.depth).transpose(1, 0, 2, 3)
    rotated = lax.all_to_all(rotated, "band", 0, 0, tiled=True)
    return rotated.reshape(z.cells, z.bands, z.depth).transpose(1, 0, 2).reshape(bands.shape)


def solution(mesh):
    placed = (
        P("band", "dom", None, None),
        P("dom", None, None),
        P("dom", None, None, None, None),
        P("dom", None),
        P(),
        P(),
    )
    return jax.shard_map(
        local, mesh=mesh, in_specs=placed, out_specs=P("band", "dom", None, None), check_vma=False
    )
```

```python
import functools
import jax
import jax.numpy as jnp
import numpy as np
from jax import lax
from jax.experimental import pallas as pl
from jax.experimental.pallas import tpu as pltpu
from jax.sharding import PartitionSpec as P

STENCIL = [
    -5369.0 / 1800.0,
    12.0 / 7.0,
    -15.0 / 56.0,
    10.0 / 189.0,
    -1.0 / 112.0,
    2.0 / 1925.0,
    -1.0 / 16632.0,
]
kinetic_scale = 0.5 / 0.49
centre = 12.0
half_width = 11.0
REACH = 6
F32, BF16 = jnp.float32, jnp.bfloat16
WEIGHTS = [-kinetic_scale * w for w in STENCIL]


def split3(x):
    hi = x.astype(BF16)
    rest = x - hi.astype(F32)
    mid = rest.astype(BF16)
    return hi, mid, (rest - mid.astype(F32)).astype(BF16)


def z_matrix(depth):
    row = lax.broadcasted_iota(jnp.int32, (depth, depth), 0)
    col = lax.broadcasted_iota(jnp.int32, (depth, depth), 1)
    apart = jnp.abs(row - col)
    apart = jnp.minimum(apart, depth - apart)
    full = jnp.zeros((depth, depth), F32)
    for offset in range(1, REACH + 1):
        full = jnp.where(apart == offset, np.float32(WEIGHTS[offset]), full)
    return jnp.concatenate(split3(full), 0)


def dot_t(a, b):
    return lax.dot_general(a, b, (((1,), (1,)), ((), ())), preferred_element_type=F32)


class Sizes:
    def __init__(self, bands, atom_ids, strength, dom_count):
        self.bands, self.thickness, self.rows, self.depth = bands
        self.blocks, self.slot_count = atom_ids
        self.atoms, self.projs = strength
        self.doms = dom_count
        self.owned = self.atoms // dom_count
        self.block_rows = self.rows // self.blocks
        self.cells = self.thickness * self.rows
        self.slots = self.slot_count * self.projs
        self.lanes = self.owned * self.projs
        self.tall = self.cells * self.bands
        assert self.owned & (self.owned - 1) == 0 and dom_count & (dom_count - 1) == 0


def one_hots(z, dom, ids_ref):
    ids = ids_ref[...]
    shift = z.owned.bit_length() - 1
    relative = ((ids >> shift) - dom + (1 + z.doms)) & (z.doms - 1)
    place = relative * z.owned + (ids & (z.owned - 1))
    slot = lax.broadcasted_iota(jnp.int32, (z.slot_count, z.slots), 0)
    lane = lax.broadcasted_iota(jnp.int32, (z.slot_count, z.slots), 1)
    inside = lane - slot * z.projs
    spread = jnp.where((inside >= 0) & (inside < z.projs), 1.0, 0.0).astype(BF16)
    wide = jnp.dot(place.astype(F32).astype(BF16), spread, preferred_element_type=F32)
    shape = (z.lanes, z.slots)
    row = lax.broadcasted_iota(jnp.int32, shape, 0)
    lane = lax.broadcasted_iota(jnp.int32, shape, 1)
    fits = (row >> shift) == lane % z.projs
    atom = (row & (z.owned - 1)).astype(F32)
    out = []
    for j in range(z.blocks):
        mine = jnp.broadcast_to(wide[j : j + 1, :], shape)
        tiles = [
            jnp.where(fits & (mine == atom + float(z.owned * tile)), 1.0, 0.0) for tile in range(3)
        ]
        out.append(jnp.concatenate(tiles, 0).astype(BF16))
    return out


def scatter(z, partials, hots_ref, tab_ref):
    total = None
    for j, partial in enumerate(partials):
        hot = hots_ref[j]
        for piece in split3(partial):
            part = dot_t(piece, hot)
            total = part if total is None else total + part
    for t in range(3):
        tab_ref[t] = total[:, t * z.lanes : (t + 1) * z.lanes]


def mate_tiles(side, tab_ref):
    first_core = side == 0
    return [
        jnp.where(first_core, tab_ref[1], tab_ref[0]),
        jnp.where(first_core, tab_ref[2], tab_ref[1]),
    ]


def put_mate(z, tab_ref, slab_ref):
    side = lax.axis_index("dom") & 1
    put_tiles(z, mate_tiles(side, tab_ref), slab_ref)
    outer = jnp.where(side == 0, tab_ref[0], tab_ref[2])
    pieces = list(split3(outer)) + [jnp.zeros(outer.shape, BF16)]
    slab_ref[z.tall + 6 * z.bands :, :] = jnp.concatenate([p.astype(F32) for p in pieces], 0).astype(BF16)


def put_tiles(z, tiles, slab_ref):
    for n, piece in enumerate(split3(jnp.concatenate(tiles, 0))):
        slab_ref[z.tall + n * 2 * z.bands : z.tall + (n + 1) * 2 * z.bands, :] = piece


def get_tiles(z, slab_ref):
    total = None
    for n in range(3):
        piece = slab_ref[z.tall + n * 2 * z.bands : z.tall + (n + 1) * 2 * z.bands, :].astype(F32)
        total = piece if total is None else total + piece
    return [total[: z.bands], total[z.bands :]]


def meet_kernel(z, tab_ref, got_ref, slab_in, slab_ref, chip_ref, far_ref):
    slab_ref[: z.tall, :] = slab_in[: z.tall, :]
    side = lax.axis_index("dom") & 1
    first_core = side == 0
    mate, got = mate_tiles(side, tab_ref), get_tiles(z, got_ref)
    low, high = mate[0] + got[0], mate[1] + got[1]
    chip_ref[0], chip_ref[1] = low, high
    outer = got_ref[z.tall + 6 * z.bands :, :].astype(F32)
    far_ref[...] = outer[: z.bands] + outer[z.bands : 2 * z.bands] + outer[2 * z.bands : 3 * z.bands]
    below, above = tab_ref[0], tab_ref[2]
    pair = [jnp.where(first_core, below, high), jnp.where(first_core, low, above)]
    put_tiles(z, pair, slab_ref)


def gathered(z, tab_ref, chip_ref, across_ref, far_ref, strength_ref, hots_ref):
    first_core = (lax.axis_index("dom") & 1) == 0
    got = get_tiles(z, across_ref)
    low, high, far = chip_ref[0], chip_ref[1], far_ref[...]
    tiles = [
        jnp.where(first_core, tab_ref[0] + got[0], low + far),
        jnp.where(first_core, low + got[1], high + got[0]),
        jnp.where(first_core, high + far, tab_ref[2] + got[1]),
    ]
    weighted = [tile * strength_ref[t : t + 1, :] for t, tile in enumerate(tiles)]
    weighted = jnp.concatenate(weighted, 1).astype(BF16)
    return [
        jnp.dot(weighted, hots_ref[j], preferred_element_type=F32).astype(BF16)
        for j in range(z.blocks)
    ]


def pair_rows(pair):
    return slice(16 * pair, 16 * pair + 16)


def block_of(z, pair):
    return (2 * pair % z.rows) // z.block_rows


class Projector:
    def __init__(self, z, v_ref, proj_ref):
        self.z, self.v_ref, self.proj_ref = z, v_ref, proj_ref
        self.total = [None] * z.blocks

    def add(self, pairs):
        b = self.z.bands
        for pair in pairs:
            j = block_of(self.z, pair)
            v = self.v_ref[pair_rows(pair), :].astype(F32)
            v = jnp.concatenate([v[:b], v[b:]], 1).astype(BF16)
            both = jnp.concatenate([self.proj_ref[2 * pair], self.proj_ref[2 * pair + 1]], 1)
            part = dot_t(v, both)
            self.total[j] = part if self.total[j] is None else self.total[j] + part

    def sums(self):
        return self.total


def turned(z, bands_ref, x):
    plane = bands_ref[:, x * z.rows : (x + 1) * z.rows, :].astype(F32)
    return jnp.swapaxes(plane, 0, 1)


def turn_all(z, bands_ref, v_ref):
    tall = z.rows * z.bands
    for x in range(z.thickness):
        plane = turned(z, bands_ref, x).reshape(tall, z.depth)
        v_ref[x * tall : (x + 1) * tall, :] = plane.astype(BF16)


def pause_kernel(z, out_ref):
    out_ref[...] = jnp.zeros_like(out_ref)


def project_kernel(z, pause_ref, ids_ref, bands_ref, proj_ref, tab_ref, v_ref, hots_ref):
    dom = lax.axis_index("dom")
    turn_all(z, bands_ref, v_ref)
    for j, hot in enumerate(one_hots(z, dom, ids_ref)):
        hots_ref[j] = hot
    projector = Projector(z, v_ref, proj_ref)
    projector.add(range(z.cells // 2))
    scatter(z, projector.sums(), hots_ref, tab_ref)
    put_mate(z, tab_ref, v_ref)


def near_strength(z, dom, strength_ref, out_ref):
    per_tile = 128 // z.owned
    row = lax.broadcasted_iota(jnp.int32, (z.projs, 128), 0)
    lane = lax.broadcasted_iota(jnp.int32, (z.projs, 128), 1)
    for t in range(3):
        owner = (dom + (t - 1) + z.doms) & (z.doms - 1)
        tile = strength_ref[:, pl.ds(pl.multiple_of(owner // per_tile * 128, 128), 128)]
        inside = owner % per_tile
        line = jnp.zeros((1, 128), F32)
        for p in range(z.projs):
            turned = pltpu.roll(tile, ((p + per_tile) - inside) % per_tile * z.owned, 1)
            keep = (row == p) & (lane >= p * z.owned) & (lane < (p + 1) * z.owned)
            line = line + jnp.sum(jnp.where(keep, turned, 0.0), axis=0, keepdims=True)
        out_ref[t : t + 1, :] = line


def base_body(z, dom, v_ref, wide_ref, write):
    b = z.bands
    zmat = z_matrix(z.depth)
    for c in range(0, z.cells, z.rows):
        v = v_ref[b * c : b * (c + z.rows), :]
        along_z = jnp.dot(jnp.concatenate([v, v, v], 1), zmat, preferred_element_type=F32)
        for y in range(0, z.rows, 2):
            both = []
            for at in (y, y + 1):
                here = z.cells + c + at
                total = wide_ref[here] * (write.pot(c + at) + (3.0 * WEIGHTS[0] - centre))
                total = total + along_z[b * at : b * at + b, :]
                for offset in range(1, REACH + 1):
                    beside = wide_ref[here + offset * z.rows] + wide_ref[here - offset * z.rows]
                    up = z.cells + c + (at + offset) % z.rows
                    down = z.cells + c + (at - offset) % z.rows
                    beside = beside + (wide_ref[up] + wide_ref[down])
                    total = total + WEIGHTS[offset] * beside
                both.append(total)
            write((c + y) // 2, jnp.concatenate(both, 0))


class Writer:
    def __init__(self, pot_ref, put):
        self.pot_ref, self.put = pot_ref, put

    def pot(self, cell):
        return self.pot_ref[cell : cell + 1, :]

    def __call__(self, pair, value):
        self.put(pair_rows(pair), value)


def fill_and_base(z, v_ref, on_ref, pot_ref, out_ref, wide_ref):
    dom = lax.axis_index("dom")
    first_core = (dom & 1) == 0
    on_at = pl.multiple_of(jnp.where(first_core, 2 * z.cells, 0), z.cells)
    off_at = pl.multiple_of(jnp.where(first_core, 0, 2 * z.cells), z.cells)
    step, b = 8, z.bands

    def tile(ref, c):
        return ref[b * c : b * (c + step), :].astype(F32).reshape(step, b, z.depth)

    for c in range(0, z.cells, step):
        wide_ref[z.cells + c : z.cells + c + step] = tile(v_ref, c)
        wide_ref[pl.ds(on_at + c, step)] = tile(on_ref, c)
        wide_ref[pl.ds(off_at + c, step)] = jnp.zeros((step, b, z.depth), F32)

    def put(rows, value):
        out_ref[rows, :] = value

    base_body(z, dom, v_ref, wide_ref, Writer(pot_ref, put))


def add_across(z, base_ref, across_ref, acc_ref):
    side = lax.axis_index("dom") & 1
    tall = z.rows * z.bands
    last = z.thickness - 1

    def at(plane, c):
        there = jnp.where(side == 0, plane, last - plane)
        return pl.ds(pl.multiple_of(there * tall + c, 32), 32)

    for c in range(0, tall, 32):
        planes = [across_ref[at(q, c), :].astype(F32) for q in range(z.thickness)]
        for x in range(z.thickness):
            total = base_ref[at(x, c), :]
            for q in range(x, z.thickness):
                offset = x - q + z.thickness
                if offset <= REACH:
                    total = total + WEIGHTS[offset] * planes[q]
            acc_ref[at(x, c), :] = total


def base_first_kernel(z, v_ref, on_ref, pot_ref, strength_ref, out_ref, near_ref, wide_ref):
    fill_and_base(z, v_ref, on_ref, pot_ref, out_ref, wide_ref)
    near_strength(z, lax.axis_index("dom"), strength_ref, near_ref)


def base_kernel(z, v_ref, on_ref, pot_ref, out_ref, wide_ref):
    fill_and_base(z, v_ref, on_ref, pot_ref, out_ref, wide_ref)


def nonlocal_pair(weighted, proj_ref, pair):
    both = jnp.concatenate([proj_ref[2 * pair], proj_ref[2 * pair + 1]], 1)
    value = jnp.dot(weighted, both, preferred_element_type=F32)
    half = value.shape[1] // 2
    return jnp.concatenate([value[:, :half], value[:, half:]], 0)


def first_kernel(
    z, base_ref, tab_in, chip_ref, across_ref, far_ref, near_ref, hots_ref, proj_ref, first_ref, tab_ref, acc_ref
):
    add_across(z, base_ref, across_ref, acc_ref)
    weighted = gathered(z, tab_in, chip_ref, across_ref, far_ref, near_ref, hots_ref)
    for pair in range(z.cells // 2):
        rows = pair_rows(pair)
        value = acc_ref[rows, :] + nonlocal_pair(weighted[block_of(z, pair)], proj_ref, pair)
        first_ref[rows, :] = (value / half_width).astype(BF16)
    projector = Projector(z, first_ref, proj_ref)
    projector.add(range(z.cells // 2))
    scatter(z, projector.sums(), hots_ref, tab_ref)
    put_mate(z, tab_ref, first_ref)


def filtered_kernel(
    z, base_ref, tab_ref, chip_ref, across_ref, far_ref, near_ref, hots_ref, proj_ref, start_ref, out_ref, acc_ref
):
    add_across(z, base_ref, across_ref, acc_ref)
    weighted = gathered(z, tab_ref, chip_ref, across_ref, far_ref, near_ref, hots_ref)
    for pair in range(z.cells // 2):
        rows = pair_rows(pair)
        value = acc_ref[rows, :] + nonlocal_pair(weighted[block_of(z, pair)], proj_ref, pair)
        out_ref[rows, :] = (2.0 * value / half_width - start_ref[rows, :].astype(F32)).astype(BF16)


VMEM = pl.BlockSpec(memory_space=pltpu.VMEM)


def call(kernel, z, name, outs, ins, flops, moved, scratch=()):
    single = not isinstance(outs, (list, tuple))
    return pl.pallas_call(
        functools.partial(kernel, z),
        name=name,
        out_shape=outs,
        in_specs=[VMEM] * len(ins),
        out_specs=VMEM if single else [VMEM] * len(outs),
        scratch_shapes=list(scratch),
        compiler_params=pltpu.CompilerParams(vmem_limit_bytes=12288 * 1024),
        cost_estimate=pl.CostEstimate(flops=flops, bytes_accessed=moved, transcendentals=0),
    )(*ins)


class Shapes:
    def __init__(self, z):
        self.tile = jax.ShapeDtypeStruct((z.bands, z.lanes), F32)
        self.pair = jax.ShapeDtypeStruct((2, z.bands, z.lanes), F32)
        self.tab = jax.ShapeDtypeStruct((3, z.bands, z.lanes), F32)
        self.slab = jax.ShapeDtypeStruct((z.tall, z.depth), BF16)
        self.message = jax.ShapeDtypeStruct((z.tall + 6 * z.bands, z.depth), BF16)
        self.mate_message = jax.ShapeDtypeStruct((z.tall + 10 * z.bands, z.depth), BF16)
        self.base = jax.ShapeDtypeStruct((z.tall, z.depth), F32)
        self.near = jax.ShapeDtypeStruct((8, z.lanes), F32)
        self.hots = jax.ShapeDtypeStruct((z.blocks, 3 * z.lanes, z.slots), BF16)
        self.wide = [pltpu.VMEM((3 * z.cells, z.bands, z.depth), F32)]
        self.acc = [pltpu.VMEM((z.tall, z.depth), F32)]
        self.stream = 2 * z.tall * z.slots * z.depth
        self.proj_bytes = 2 * z.cells * z.slots * z.depth
        self.stencil = 6 * z.tall * z.depth * z.depth
        self.slab_bytes = 10 * z.tall * z.depth


def swap_on_chip(x, axis):
    count = lax.axis_size(axis)
    return lax.ppermute(x, axis, [(i, i ^ 1) for i in range(count)])


def swap_across(x, axis):
    count = lax.axis_size(axis)
    return lax.ppermute(x, axis, [(i, (((i + 1) ^ 1) - 1) % count) for i in range(count)])


def swap_far(x, axis):
    count = lax.axis_size(axis)
    return lax.ppermute(x, axis, [(i, (i + 3 - 6 * (i % 2)) % count) for i in range(count)])


def local(bands, potential, projectors, atom_ids, strength, rotation):
    z = Sizes(bands.shape, atom_ids.shape, strength.shape, lax.axis_size("dom"))
    groups = lax.axis_size("band")
    proj = projectors.reshape(z.cells, z.slots, z.depth)
    pot = potential.reshape(z.cells, z.depth)
    flat = bands.reshape(z.bands, z.cells, z.depth)

    s = Shapes(z)

    def exchange(tab, slab):
        on_chip = swap_on_chip(slab, "dom")
        slab, chip, far = call(
            meet_kernel, z, "meet", [s.message, s.pair, s.tile], (tab, on_chip, slab), 1000, 1000
        )
        across = swap_across(slab, "dom")
        far = swap_far(far, "dom")
        return slab, on_chip, (tab, chip, across, far)

    pause = call(pause_kernel, z, "pause", s.tile, (), 4000 * s.stream, 40_000_000)
    tab, start, hots = call(
        project_kernel, z, "project", [s.tab, s.mate_message, s.hots],
        (pause, atom_ids, flat, proj), s.stream, s.proj_bytes,
    )
    start, on_chip, sums = exchange(tab, start)
    base, near = call(
        base_first_kernel, z, "base_first", [s.base, s.near],
        (start, on_chip, pot, strength.T), s.stencil, s.slab_bytes, scratch=s.wide,
    )
    first, tab = call(
        first_kernel, z, "first", [s.mate_message, s.tab],
        (base,) + sums + (near, hots, proj), 2 * s.stream, s.proj_bytes, scratch=s.acc,
    )
    first, on_chip, sums = exchange(tab, first)
    base = call(
        base_kernel, z, "base", s.base, (first, on_chip, pot), s.stencil, s.slab_bytes, scratch=s.wide,
    )
    filtered = call(
        filtered_kernel, z, "filtered", s.slab, (base,) + sums + (near, hots, proj, start),
        s.stream, s.proj_bytes, scratch=s.acc,
    )

    share = z.cells // groups
    pieces = filtered.reshape(groups, share, z.bands, z.depth)
    pieces = lax.all_to_all(pieces, "band", 0, 0, tiled=True)
    turn = rotation.reshape(groups, z.bands, groups * z.bands)
    rotated = jnp.einsum("gxbz,gbc->xcz", pieces, turn, preferred_element_type=F32).astype(BF16)
    rotated = rotated.reshape(share, groups, z.bands, z.depth).transpose(1, 0, 2, 3)
    rotated = lax.all_to_all(rotated, "band", 0, 0, tiled=True)
    return rotated.reshape(z.cells, z.bands, z.depth).transpose(1, 0, 2).reshape(bands.shape)


def solution(mesh):
    placed = (
        P("band", "dom", None, None),
        P("dom", None, None),
        P("dom", None, None, None, None),
        P("dom", None),
        P(),
        P(),
    )
    return jax.shard_map(
        local, mesh=mesh, in_specs=placed, out_specs=P("band", "dom", None, None), check_vma=False
    )
```

```python
import functools
import jax
import jax.numpy as jnp
import numpy as np
from jax import lax
from jax.experimental import pallas as pl
from jax.experimental.pallas import tpu as pltpu
from jax.sharding import PartitionSpec as P

STENCIL = [
    -5369.0 / 1800.0,
    12.0 / 7.0,
    -15.0 / 56.0,
    10.0 / 189.0,
    -1.0 / 112.0,
    2.0 / 1925.0,
    -1.0 / 16632.0,
]
kinetic_scale = 0.5 / 0.49
centre = 12.0
half_width = 11.0
REACH = 6
F32, BF16 = jnp.float32, jnp.bfloat16
WEIGHTS = [-kinetic_scale * w for w in STENCIL]


def split3(x):
    hi = x.astype(BF16)
    rest = x - hi.astype(F32)
    mid = rest.astype(BF16)
    return hi, mid, (rest - mid.astype(F32)).astype(BF16)


def z_matrix(depth):
    row = lax.broadcasted_iota(jnp.int32, (depth, depth), 0)
    col = lax.broadcasted_iota(jnp.int32, (depth, depth), 1)
    apart = jnp.abs(row - col)
    apart = jnp.minimum(apart, depth - apart)
    full = jnp.zeros((depth, depth), F32)
    for offset in range(1, REACH + 1):
        full = jnp.where(apart == offset, np.float32(WEIGHTS[offset]), full)
    return jnp.concatenate(split3(full), 0)


def dot_t(a, b):
    return lax.dot_general(a, b, (((1,), (1,)), ((), ())), preferred_element_type=F32)


class Sizes:
    def __init__(self, bands, atom_ids, strength, dom_count):
        self.bands, self.thickness, self.rows, self.depth = bands
        self.blocks, self.slot_count = atom_ids
        self.atoms, self.projs = strength
        self.doms = dom_count
        self.owned = self.atoms // dom_count
        self.block_rows = self.rows // self.blocks
        self.cells = self.thickness * self.rows
        self.slots = self.slot_count * self.projs
        self.lanes = self.owned * self.projs
        self.tall = self.cells * self.bands
        assert self.owned & (self.owned - 1) == 0 and dom_count & (dom_count - 1) == 0


def one_hots(z, dom, ids_ref):
    ids = ids_ref[...]
    shift = z.owned.bit_length() - 1
    relative = ((ids >> shift) - dom + (1 + z.doms)) & (z.doms - 1)
    place = relative * z.owned + (ids & (z.owned - 1))
    slot = lax.broadcasted_iota(jnp.int32, (z.slot_count, z.slots), 0)
    lane = lax.broadcasted_iota(jnp.int32, (z.slot_count, z.slots), 1)
    inside = lane - slot * z.projs
    spread = jnp.where((inside >= 0) & (inside < z.projs), 1.0, 0.0).astype(BF16)
    wide = jnp.dot(place.astype(F32).astype(BF16), spread, preferred_element_type=F32)
    shape = (z.lanes, z.slots)
    row = lax.broadcasted_iota(jnp.int32, shape, 0)
    lane = lax.broadcasted_iota(jnp.int32, shape, 1)
    fits = (row >> shift) == lane % z.projs
    atom = (row & (z.owned - 1)).astype(F32)
    out = []
    for j in range(z.blocks):
        mine = jnp.broadcast_to(wide[j : j + 1, :], shape)
        tiles = [
            jnp.where(fits & (mine == atom + float(z.owned * tile)), 1.0, 0.0) for tile in range(3)
        ]
        out.append(jnp.concatenate(tiles, 0).astype(BF16))
    return out


def scatter(z, partials, hots_ref, tab_ref):
    total = None
    b = z.bands
    for j, partial in enumerate(partials):
        pieces = jnp.concatenate([piece.astype(F32) for piece in split3(partial)], 0)
        part = dot_t(pieces.astype(BF16), hots_ref[j])
        part = part[:b] + part[b : 2 * b] + part[2 * b :]
        total = part if total is None else total + part
    for t in range(3):
        tab_ref[t] = total[:, t * z.lanes : (t + 1) * z.lanes]


def mate_tiles(side, tab_ref):
    first_core = side == 0
    return [
        jnp.where(first_core, tab_ref[1], tab_ref[0]),
        jnp.where(first_core, tab_ref[2], tab_ref[1]),
    ]


def put_mate(z, tab_ref, slab_ref):
    side = lax.axis_index("dom") & 1
    put_tiles(z, mate_tiles(side, tab_ref), slab_ref)
    outer = jnp.where(side == 0, tab_ref[0], tab_ref[2])
    pieces = list(split3(outer)) + [jnp.zeros(outer.shape, BF16)]
    slab_ref[z.tall + 6 * z.bands :, :] = jnp.concatenate([p.astype(F32) for p in pieces], 0).astype(BF16)


def put_tiles(z, tiles, slab_ref):
    for n, piece in enumerate(split3(jnp.concatenate(tiles, 0))):
        slab_ref[z.tall + n * 2 * z.bands : z.tall + (n + 1) * 2 * z.bands, :] = piece


def get_tiles(z, slab_ref):
    total = None
    for n in range(3):
        piece = slab_ref[z.tall + n * 2 * z.bands : z.tall + (n + 1) * 2 * z.bands, :].astype(F32)
        total = piece if total is None else total + piece
    return [total[: z.bands], total[z.bands :]]


def meet_kernel(z, tab_ref, got_ref, slab_in, slab_ref, chip_ref, far_ref):
    slab_ref[: z.tall, :] = slab_in[: z.tall, :]
    side = lax.axis_index("dom") & 1
    first_core = side == 0
    mate, got = mate_tiles(side, tab_ref), get_tiles(z, got_ref)
    low, high = mate[0] + got[0], mate[1] + got[1]
    chip_ref[0], chip_ref[1] = low, high
    outer = got_ref[z.tall + 6 * z.bands :, :].astype(F32)
    far_ref[...] = outer[: z.bands] + outer[z.bands : 2 * z.bands] + outer[2 * z.bands : 3 * z.bands]
    below, above = tab_ref[0], tab_ref[2]
    pair = [jnp.where(first_core, below, high), jnp.where(first_core, low, above)]
    put_tiles(z, pair, slab_ref)


def gathered(z, tab_ref, chip_ref, across_ref, far_ref, strength_ref, hots_ref):
    first_core = (lax.axis_index("dom") & 1) == 0
    got = get_tiles(z, across_ref)
    low, high, far = chip_ref[0], chip_ref[1], far_ref[...]
    tiles = [
        jnp.where(first_core, tab_ref[0] + got[0], low + far),
        jnp.where(first_core, low + got[1], high + got[0]),
        jnp.where(first_core, high + far, tab_ref[2] + got[1]),
    ]
    weighted = [tile * strength_ref[t : t + 1, :] for t, tile in enumerate(tiles)]
    weighted = jnp.concatenate(weighted, 1).astype(BF16)
    return [
        jnp.dot(weighted, hots_ref[j], preferred_element_type=F32).astype(BF16)
        for j in range(z.blocks)
    ]


def pair_rows(pair):
    return slice(16 * pair, 16 * pair + 16)


def block_of(z, pair):
    return (2 * pair % z.rows) // z.block_rows


class Projector:
    def __init__(self, z, v_ref, proj_ref):
        self.z, self.v_ref, self.proj_ref = z, v_ref, proj_ref
        self.total = [None] * z.blocks

    def add(self, pairs):
        b = self.z.bands
        for pair in pairs:
            j = block_of(self.z, pair)
            v = self.v_ref[pair_rows(pair), :].astype(F32)
            v = jnp.concatenate([v[:b], v[b:]], 1).astype(BF16)
            both = jnp.concatenate([self.proj_ref[2 * pair], self.proj_ref[2 * pair + 1]], 1)
            part = dot_t(v, both)
            self.total[j] = part if self.total[j] is None else self.total[j] + part

    def sums(self):
        return self.total


def turned(z, bands_ref, x):
    plane = bands_ref[:, x * z.rows : (x + 1) * z.rows, :].astype(F32)
    return jnp.swapaxes(plane, 0, 1)


def turn_all(z, bands_ref, v_ref):
    tall = z.rows * z.bands
    for x in range(z.thickness):
        plane = turned(z, bands_ref, x).reshape(tall, z.depth)
        v_ref[x * tall : (x + 1) * tall, :] = plane.astype(BF16)


def pause_kernel(z, out_ref):
    out_ref[...] = jnp.zeros_like(out_ref)


def prepare_kernel(z, pause_ref, ids_ref, bands_ref, v_ref, hots_ref):
    turn_all(z, bands_ref, v_ref)
    for j, hot in enumerate(one_hots(z, lax.axis_index("dom"), ids_ref)):
        hots_ref[j] = hot


def project_kernel(z, v_in, hots_ref, proj_ref, tab_ref, v_ref):
    v_ref[: z.tall, :] = v_in[...]
    projector = Projector(z, v_in, proj_ref)
    projector.add(range(z.cells // 2))
    scatter(z, projector.sums(), hots_ref, tab_ref)
    put_mate(z, tab_ref, v_ref)


def near_strength(z, dom, strength_ref, out_ref):
    per_tile = 128 // z.owned
    row = lax.broadcasted_iota(jnp.int32, (z.projs, 128), 0)
    lane = lax.broadcasted_iota(jnp.int32, (z.projs, 128), 1)
    for t in range(3):
        owner = (dom + (t - 1) + z.doms) & (z.doms - 1)
        tile = strength_ref[:, pl.ds(pl.multiple_of(owner // per_tile * 128, 128), 128)]
        inside = owner % per_tile
        line = jnp.zeros((1, 128), F32)
        for p in range(z.projs):
            turned = pltpu.roll(tile, ((p + per_tile) - inside) % per_tile * z.owned, 1)
            keep = (row == p) & (lane >= p * z.owned) & (lane < (p + 1) * z.owned)
            line = line + jnp.sum(jnp.where(keep, turned, 0.0), axis=0, keepdims=True)
        out_ref[t : t + 1, :] = line


def base_body(z, dom, v_ref, wide_ref, write):
    b = z.bands
    zmat = z_matrix(z.depth)
    for c in range(0, z.cells, z.rows):
        v = v_ref[b * c : b * (c + z.rows), :]
        along_z = jnp.dot(jnp.concatenate([v, v, v], 1), zmat, preferred_element_type=F32)
        for y in range(0, z.rows, 2):
            both = []
            for at in (y, y + 1):
                here = z.cells + c + at
                total = wide_ref[here] * (write.pot(c + at) + (3.0 * WEIGHTS[0] - centre))
                total = total + along_z[b * at : b * at + b, :]
                for offset in range(1, REACH + 1):
                    beside = wide_ref[here + offset * z.rows] + wide_ref[here - offset * z.rows]
                    up = z.cells + c + (at + offset) % z.rows
                    down = z.cells + c + (at - offset) % z.rows
                    beside = beside + (wide_ref[up] + wide_ref[down])
                    total = total + WEIGHTS[offset] * beside
                both.append(total)
            write((c + y) // 2, jnp.concatenate(both, 0))


class Writer:
    def __init__(self, pot_ref, put):
        self.pot_ref, self.put = pot_ref, put

    def pot(self, cell):
        return self.pot_ref[cell : cell + 1, :]

    def __call__(self, pair, value):
        self.put(pair_rows(pair), value)


def fill_and_base(z, v_ref, on_ref, pot_ref, out_ref, wide_ref):
    dom = lax.axis_index("dom")
    first_core = (dom & 1) == 0
    on_at = pl.multiple_of(jnp.where(first_core, 2 * z.cells, 0), z.cells)
    off_at = pl.multiple_of(jnp.where(first_core, 0, 2 * z.cells), z.cells)
    step, b = 8, z.bands

    def tile(ref, c):
        return ref[b * c : b * (c + step), :].astype(F32).reshape(step, b, z.depth)

    for c in range(0, z.cells, step):
        wide_ref[z.cells + c : z.cells + c + step] = tile(v_ref, c)
        wide_ref[pl.ds(on_at + c, step)] = tile(on_ref, c)
        wide_ref[pl.ds(off_at + c, step)] = jnp.zeros((step, b, z.depth), F32)

    def put(rows, value):
        out_ref[rows, :] = value

    base_body(z, dom, v_ref, wide_ref, Writer(pot_ref, put))


def add_across(z, base_ref, across_ref, acc_ref):
    side = lax.axis_index("dom") & 1
    tall = z.rows * z.bands
    last = z.thickness - 1

    def at(plane, c):
        there = jnp.where(side == 0, plane, last - plane)
        return pl.ds(pl.multiple_of(there * tall + c, 32), 32)

    for c in range(0, tall, 32):
        planes = [across_ref[at(q, c), :].astype(F32) for q in range(z.thickness)]
        for x in range(z.thickness):
            total = base_ref[at(x, c), :]
            for q in range(x, z.thickness):
                offset = x - q + z.thickness
                if offset <= REACH:
                    total = total + WEIGHTS[offset] * planes[q]
            acc_ref[at(x, c), :] = total


def base_first_kernel(z, v_ref, on_ref, pot_ref, strength_ref, out_ref, near_ref, wide_ref):
    fill_and_base(z, v_ref, on_ref, pot_ref, out_ref, wide_ref)
    near_strength(z, lax.axis_index("dom"), strength_ref, near_ref)


def base_kernel(z, v_ref, on_ref, pot_ref, out_ref, wide_ref):
    fill_and_base(z, v_ref, on_ref, pot_ref, out_ref, wide_ref)


def nonlocal_pair(weighted, proj_ref, pair):
    both = jnp.concatenate([proj_ref[2 * pair], proj_ref[2 * pair + 1]], 1)
    value = jnp.dot(weighted, both, preferred_element_type=F32)
    half = value.shape[1] // 2
    return jnp.concatenate([value[:, :half], value[:, half:]], 0)


def first_kernel(
    z, base_ref, tab_in, chip_ref, across_ref, far_ref, near_ref, hots_ref, proj_ref, first_ref, tab_ref, acc_ref
):
    add_across(z, base_ref, across_ref, acc_ref)
    weighted = gathered(z, tab_in, chip_ref, across_ref, far_ref, near_ref, hots_ref)
    for pair in range(z.cells // 2):
        rows = pair_rows(pair)
        value = acc_ref[rows, :] + nonlocal_pair(weighted[block_of(z, pair)], proj_ref, pair)
        first_ref[rows, :] = (value / half_width).astype(BF16)
    projector = Projector(z, first_ref, proj_ref)
    projector.add(range(z.cells // 2))
    scatter(z, projector.sums(), hots_ref, tab_ref)
    put_mate(z, tab_ref, first_ref)


def filtered_kernel(
    z, base_ref, tab_ref, chip_ref, across_ref, far_ref, near_ref, hots_ref, proj_ref, start_ref, out_ref, acc_ref
):
    add_across(z, base_ref, across_ref, acc_ref)
    weighted = gathered(z, tab_ref, chip_ref, across_ref, far_ref, near_ref, hots_ref)
    for pair in range(z.cells // 2):
        rows = pair_rows(pair)
        value = acc_ref[rows, :] + nonlocal_pair(weighted[block_of(z, pair)], proj_ref, pair)
        out_ref[rows, :] = (2.0 * value / half_width - start_ref[rows, :].astype(F32)).astype(BF16)


VMEM = pl.BlockSpec(memory_space=pltpu.VMEM)


def call(kernel, z, name, outs, ins, flops, moved, scratch=()):
    single = not isinstance(outs, (list, tuple))
    return pl.pallas_call(
        functools.partial(kernel, z),
        name=name,
        out_shape=outs,
        in_specs=[VMEM] * len(ins),
        out_specs=VMEM if single else [VMEM] * len(outs),
        scratch_shapes=list(scratch),
        compiler_params=pltpu.CompilerParams(vmem_limit_bytes=12288 * 1024),
        cost_estimate=pl.CostEstimate(flops=flops, bytes_accessed=moved, transcendentals=0),
    )(*ins)


class Shapes:
    def __init__(self, z):
        self.tile = jax.ShapeDtypeStruct((z.bands, z.lanes), F32)
        self.pair = jax.ShapeDtypeStruct((2, z.bands, z.lanes), F32)
        self.tab = jax.ShapeDtypeStruct((3, z.bands, z.lanes), F32)
        self.slab = jax.ShapeDtypeStruct((z.tall, z.depth), BF16)
        self.message = jax.ShapeDtypeStruct((z.tall + 6 * z.bands, z.depth), BF16)
        self.mate_message = jax.ShapeDtypeStruct((z.tall + 10 * z.bands, z.depth), BF16)
        self.base = jax.ShapeDtypeStruct((z.tall, z.depth), F32)
        self.near = jax.ShapeDtypeStruct((8, z.lanes), F32)
        self.hots = jax.ShapeDtypeStruct((z.blocks, 3 * z.lanes, z.slots), BF16)
        self.wide = [pltpu.VMEM((3 * z.cells, z.bands, z.depth), F32)]
        self.acc = [pltpu.VMEM((z.tall, z.depth), F32)]
        self.stream = 2 * z.tall * z.slots * z.depth
        self.proj_bytes = 2 * z.cells * z.slots * z.depth
        self.stencil = 6 * z.tall * z.depth * z.depth
        self.slab_bytes = 10 * z.tall * z.depth


def swap_on_chip(x, axis):
    count = lax.axis_size(axis)
    return lax.ppermute(x, axis, [(i, i ^ 1) for i in range(count)])


def swap_across(x, axis):
    count = lax.axis_size(axis)
    return lax.ppermute(x, axis, [(i, (((i + 1) ^ 1) - 1) % count) for i in range(count)])


def swap_far(x, axis):
    count = lax.axis_size(axis)
    return lax.ppermute(x, axis, [(i, (i + 3 - 6 * (i % 2)) % count) for i in range(count)])


def local(bands, potential, projectors, atom_ids, strength, rotation):
    z = Sizes(bands.shape, atom_ids.shape, strength.shape, lax.axis_size("dom"))
    groups = lax.axis_size("band")
    proj = projectors.reshape(z.cells, z.slots, z.depth)
    pot = potential.reshape(z.cells, z.depth)
    flat = bands.reshape(z.bands, z.cells, z.depth)

    s = Shapes(z)

    def exchange(tab, slab):
        on_chip = swap_on_chip(slab, "dom")
        slab, chip, far = call(
            meet_kernel, z, "meet", [s.message, s.pair, s.tile], (tab, on_chip, slab), 1000, 1000
        )
        across = swap_across(slab, "dom")
        far = swap_far(far, "dom")
        return slab, on_chip, (tab, chip, across, far)

    pause = call(pause_kernel, z, "pause", s.tile, (), 4000 * s.stream, 40_000_000)
    start, hots = call(
        prepare_kernel, z, "prepare", [s.slab, s.hots], (pause, atom_ids, flat), s.stream, s.proj_bytes,
    )
    tab, start = call(
        project_kernel, z, "project", [s.tab, s.mate_message], (start, hots, proj), s.stream, s.proj_bytes,
    )
    start, on_chip, sums = exchange(tab, start)
    base, near = call(
        base_first_kernel, z, "base_first", [s.base, s.near],
        (start, on_chip, pot, strength.T), s.stencil, s.slab_bytes, scratch=s.wide,
    )
    first, tab = call(
        first_kernel, z, "first", [s.mate_message, s.tab],
        (base,) + sums + (near, hots, proj), 2 * s.stream, s.proj_bytes, scratch=s.acc,
    )
    first, on_chip, sums = exchange(tab, first)
    base = call(
        base_kernel, z, "base", s.base, (first, on_chip, pot), s.stencil, s.slab_bytes, scratch=s.wide,
    )
    filtered = call(
        filtered_kernel, z, "filtered", s.slab, (base,) + sums + (near, hots, proj, start),
        s.stream, s.proj_bytes, scratch=s.acc,
    )

    share = z.cells // groups
    pieces = filtered.reshape(groups, share, z.bands, z.depth)
    pieces = lax.all_to_all(pieces, "band", 0, 0, tiled=True)
    turn = rotation.reshape(groups, z.bands, groups * z.bands)
    rotated = jnp.einsum("gxbz,gbc->xcz", pieces, turn, preferred_element_type=F32).astype(BF16)
    rotated = rotated.reshape(share, groups, z.bands, z.depth).transpose(1, 0, 2, 3)
    rotated = lax.all_to_all(rotated, "band", 0, 0, tiled=True)
    return rotated.reshape(z.cells, z.bands, z.depth).transpose(1, 0, 2).reshape(bands.shape)


def solution(mesh):
    placed = (
        P("band", "dom", None, None),
        P("dom", None, None),
        P("dom", None, None, None, None),
        P("dom", None),
        P(),
        P(),
    )
    return jax.shard_map(
        local, mesh=mesh, in_specs=placed, out_specs=P("band", "dom", None, None), check_vma=False
    )
```

```python
import functools
import jax
import jax.numpy as jnp
import numpy as np
from jax import lax
from jax.experimental import pallas as pl
from jax.experimental.pallas import tpu as pltpu
from jax.sharding import PartitionSpec as P

STENCIL = [
    -5369.0 / 1800.0,
    12.0 / 7.0,
    -15.0 / 56.0,
    10.0 / 189.0,
    -1.0 / 112.0,
    2.0 / 1925.0,
    -1.0 / 16632.0,
]
kinetic_scale = 0.5 / 0.49
centre = 12.0
half_width = 11.0
REACH = 6
F32, BF16 = jnp.float32, jnp.bfloat16
WEIGHTS = [-kinetic_scale * w for w in STENCIL]


def split3(x):
    hi = x.astype(BF16)
    rest = x - hi.astype(F32)
    mid = rest.astype(BF16)
    return hi, mid, (rest - mid.astype(F32)).astype(BF16)


def z_matrix(depth):
    row = lax.broadcasted_iota(jnp.int32, (depth, depth), 0)
    col = lax.broadcasted_iota(jnp.int32, (depth, depth), 1)
    apart = jnp.abs(row - col)
    apart = jnp.minimum(apart, depth - apart)
    full = jnp.zeros((depth, depth), F32)
    for offset in range(1, REACH + 1):
        full = jnp.where(apart == offset, np.float32(WEIGHTS[offset]), full)
    return jnp.concatenate(split3(full), 0)


def dot_t(a, b):
    return lax.dot_general(a, b, (((1,), (1,)), ((), ())), preferred_element_type=F32)


class Sizes:
    def __init__(self, bands, atom_ids, strength, dom_count):
        self.bands, self.thickness, self.rows, self.depth = bands
        self.blocks, self.slot_count = atom_ids
        self.atoms, self.projs = strength
        self.doms = dom_count
        self.owned = self.atoms // dom_count
        self.block_rows = self.rows // self.blocks
        self.cells = self.thickness * self.rows
        self.slots = self.slot_count * self.projs
        self.lanes = self.owned * self.projs
        self.tall = self.cells * self.bands
        assert self.owned & (self.owned - 1) == 0 and dom_count & (dom_count - 1) == 0


def one_hots(z, dom, ids_ref):
    ids = ids_ref[...]
    shift = z.owned.bit_length() - 1
    relative = ((ids >> shift) - dom + (1 + z.doms)) & (z.doms - 1)
    place = relative * z.owned + (ids & (z.owned - 1))
    slot = lax.broadcasted_iota(jnp.int32, (z.slot_count, z.slots), 0)
    lane = lax.broadcasted_iota(jnp.int32, (z.slot_count, z.slots), 1)
    inside = lane - slot * z.projs
    spread = jnp.where((inside >= 0) & (inside < z.projs), 1.0, 0.0).astype(BF16)
    wide = jnp.dot(place.astype(F32).astype(BF16), spread, preferred_element_type=F32)
    shape = (z.lanes, z.slots)
    row = lax.broadcasted_iota(jnp.int32, shape, 0)
    lane = lax.broadcasted_iota(jnp.int32, shape, 1)
    fits = (row >> shift) == lane % z.projs
    atom = (row & (z.owned - 1)).astype(F32)
    out = []
    for j in range(z.blocks):
        mine = jnp.broadcast_to(wide[j : j + 1, :], shape)
        tiles = [
            jnp.where(fits & (mine == atom + float(z.owned * tile)), 1.0, 0.0) for tile in range(3)
        ]
        out.append(jnp.concatenate(tiles, 0).astype(BF16))
    return out


def scatter(z, partials, hots_ref, tab_ref):
    total = None
    b = z.bands
    for j, partial in enumerate(partials):
        pieces = jnp.concatenate([piece.astype(F32) for piece in split3(partial)], 0)
        part = dot_t(pieces.astype(BF16), hots_ref[j])
        part = part[:b] + part[b : 2 * b] + part[2 * b :]
        total = part if total is None else total + part
    for t in range(3):
        tab_ref[t] = total[:, t * z.lanes : (t + 1) * z.lanes]


def put_across(z, tab_ref, slab_ref, far_ref):
    first_core = (lax.axis_index("dom") & 1) == 0
    pair = [
        jnp.where(first_core, tab_ref[0], tab_ref[1]),
        jnp.where(first_core, tab_ref[1], tab_ref[2]),
    ]
    put_tiles(z, pair, slab_ref)
    far_ref[...] = jnp.where(first_core, tab_ref[2], tab_ref[0])


def put_tiles(z, tiles, slab_ref):
    for n, piece in enumerate(split3(jnp.concatenate(tiles, 0))):
        slab_ref[z.tall + n * 2 * z.bands : z.tall + (n + 1) * 2 * z.bands, :] = piece


def get_tiles(z, slab_ref):
    total = None
    for n in range(3):
        piece = slab_ref[z.tall + n * 2 * z.bands : z.tall + (n + 1) * 2 * z.bands, :].astype(F32)
        total = piece if total is None else total + piece
    return [total[: z.bands], total[z.bands :]]


def meet_kernel(z, tab_ref, across_ref, mate_ref):
    first_core = (lax.axis_index("dom") & 1) == 0
    got = get_tiles(z, across_ref)
    mate_ref[0] = jnp.where(first_core, got[1] + tab_ref[1], tab_ref[0])
    mate_ref[1] = jnp.where(first_core, tab_ref[2], tab_ref[1] + got[0])


def gathered(z, tab_ref, mate_ref, across_ref, far_ref, strength_ref, hots_ref):
    first_core = (lax.axis_index("dom") & 1) == 0
    got = get_tiles(z, across_ref)
    below, middle, above = tab_ref[0], tab_ref[1], tab_ref[2]
    low, high, far = mate_ref[0], mate_ref[1], far_ref[...]
    tiles = [
        below + jnp.where(first_core, got[0] + far, low),
        middle + jnp.where(first_core, got[1] + low, got[0] + high),
        above + jnp.where(first_core, high, got[1] + far),
    ]
    weighted = [tile * strength_ref[t : t + 1, :] for t, tile in enumerate(tiles)]
    weighted = jnp.concatenate(weighted, 1).astype(BF16)
    return [
        jnp.dot(weighted, hots_ref[j], preferred_element_type=F32).astype(BF16)
        for j in range(z.blocks)
    ]


def pair_rows(pair):
    return slice(16 * pair, 16 * pair + 16)


def block_of(z, pair):
    return (2 * pair % z.rows) // z.block_rows


class Projector:
    def __init__(self, z, v_ref, proj_ref):
        self.z, self.v_ref, self.proj_ref = z, v_ref, proj_ref
        self.total = [None] * z.blocks

    def add(self, pairs):
        b = self.z.bands
        for pair in pairs:
            j = block_of(self.z, pair)
            v = self.v_ref[pair_rows(pair), :].astype(F32)
            v = jnp.concatenate([v[:b], v[b:]], 1).astype(BF16)
            both = jnp.concatenate([self.proj_ref[2 * pair], self.proj_ref[2 * pair + 1]], 1)
            part = dot_t(v, both)
            self.total[j] = part if self.total[j] is None else self.total[j] + part

    def sums(self):
        return self.total


def turned(z, bands_ref, x):
    plane = bands_ref[:, x * z.rows : (x + 1) * z.rows, :].astype(F32)
    return jnp.swapaxes(plane, 0, 1)


def turn_all(z, bands_ref, v_ref):
    tall = z.rows * z.bands
    for x in range(z.thickness):
        plane = turned(z, bands_ref, x).reshape(tall, z.depth)
        v_ref[x * tall : (x + 1) * tall, :] = plane.astype(BF16)


def pause_kernel(z, out_ref):
    out_ref[...] = jnp.zeros_like(out_ref)


def prepare_kernel(z, pause_ref, ids_ref, bands_ref, v_ref, hots_ref):
    turn_all(z, bands_ref, v_ref)
    for j, hot in enumerate(one_hots(z, lax.axis_index("dom"), ids_ref)):
        hots_ref[j] = hot


def project_kernel(z, v_in, hots_ref, proj_ref, tab_ref, far_ref, v_ref):
    v_ref[: z.tall, :] = v_in[...]
    projector = Projector(z, v_in, proj_ref)
    projector.add(range(z.cells // 2))
    scatter(z, projector.sums(), hots_ref, tab_ref)
    put_across(z, tab_ref, v_ref, far_ref)


def near_strength(z, dom, strength_ref, out_ref):
    per_tile = 128 // z.owned
    row = lax.broadcasted_iota(jnp.int32, (z.projs, 128), 0)
    lane = lax.broadcasted_iota(jnp.int32, (z.projs, 128), 1)
    for t in range(3):
        owner = (dom + (t - 1) + z.doms) & (z.doms - 1)
        tile = strength_ref[:, pl.ds(pl.multiple_of(owner // per_tile * 128, 128), 128)]
        inside = owner % per_tile
        line = jnp.zeros((1, 128), F32)
        for p in range(z.projs):
            turned = pltpu.roll(tile, ((p + per_tile) - inside) % per_tile * z.owned, 1)
            keep = (row == p) & (lane >= p * z.owned) & (lane < (p + 1) * z.owned)
            line = line + jnp.sum(jnp.where(keep, turned, 0.0), axis=0, keepdims=True)
        out_ref[t : t + 1, :] = line


def base_body(z, dom, v_ref, wide_ref, write):
    b = z.bands
    zmat = z_matrix(z.depth)
    for c in range(0, z.cells, z.rows):
        v = v_ref[b * c : b * (c + z.rows), :]
        along_z = jnp.dot(jnp.concatenate([v, v, v], 1), zmat, preferred_element_type=F32)
        for y in range(0, z.rows, 2):
            both = []
            for at in (y, y + 1):
                here = z.cells + c + at
                total = wide_ref[here] * (write.pot(c + at) + (3.0 * WEIGHTS[0] - centre))
                total = total + along_z[b * at : b * at + b, :]
                for offset in range(1, REACH + 1):
                    beside = wide_ref[here + offset * z.rows] + wide_ref[here - offset * z.rows]
                    up = z.cells + c + (at + offset) % z.rows
                    down = z.cells + c + (at - offset) % z.rows
                    beside = beside + (wide_ref[up] + wide_ref[down])
                    total = total + WEIGHTS[offset] * beside
                both.append(total)
            write((c + y) // 2, jnp.concatenate(both, 0))


class Writer:
    def __init__(self, pot_ref, put):
        self.pot_ref, self.put = pot_ref, put

    def pot(self, cell):
        return self.pot_ref[cell : cell + 1, :]

    def __call__(self, pair, value):
        self.put(pair_rows(pair), value)


def fill_and_base(z, v_ref, on_ref, pot_ref, out_ref, wide_ref):
    dom = lax.axis_index("dom")
    first_core = (dom & 1) == 0
    on_at = pl.multiple_of(jnp.where(first_core, 2 * z.cells, 0), z.cells)
    off_at = pl.multiple_of(jnp.where(first_core, 0, 2 * z.cells), z.cells)
    step, b = 8, z.bands

    def tile(ref, c):
        return ref[b * c : b * (c + step), :].astype(F32).reshape(step, b, z.depth)

    for c in range(0, z.cells, step):
        wide_ref[z.cells + c : z.cells + c + step] = tile(v_ref, c)
        wide_ref[pl.ds(on_at + c, step)] = tile(on_ref, c)
        wide_ref[pl.ds(off_at + c, step)] = jnp.zeros((step, b, z.depth), F32)

    def put(rows, value):
        out_ref[rows, :] = value

    base_body(z, dom, v_ref, wide_ref, Writer(pot_ref, put))


def add_across(z, base_ref, across_ref, acc_ref):
    side = lax.axis_index("dom") & 1
    tall = z.rows * z.bands
    last = z.thickness - 1

    def at(plane, c):
        there = jnp.where(side == 0, plane, last - plane)
        return pl.ds(pl.multiple_of(there * tall + c, 32), 32)

    for c in range(0, tall, 32):
        planes = [across_ref[at(q, c), :].astype(F32) for q in range(z.thickness)]
        for x in range(z.thickness):
            total = base_ref[at(x, c), :]
            for q in range(x, z.thickness):
                offset = x - q + z.thickness
                if offset <= REACH:
                    total = total + WEIGHTS[offset] * planes[q]
            acc_ref[at(x, c), :] = total


def base_first_kernel(z, v_ref, on_ref, pot_ref, strength_ref, out_ref, near_ref, wide_ref):
    fill_and_base(z, v_ref, on_ref, pot_ref, out_ref, wide_ref)
    near_strength(z, lax.axis_index("dom"), strength_ref, near_ref)


def base_kernel(z, v_ref, on_ref, pot_ref, out_ref, wide_ref):
    fill_and_base(z, v_ref, on_ref, pot_ref, out_ref, wide_ref)


def nonlocal_pair(weighted, proj_ref, pair):
    both = jnp.concatenate([proj_ref[2 * pair], proj_ref[2 * pair + 1]], 1)
    value = jnp.dot(weighted, both, preferred_element_type=F32)
    half = value.shape[1] // 2
    return jnp.concatenate([value[:, :half], value[:, half:]], 0)


def first_kernel(
    z, base_ref, tab_in, chip_ref, across_ref, far_ref, near_ref, hots_ref, proj_ref, first_ref, tab_ref, far_out, acc_ref
):
    add_across(z, base_ref, across_ref, acc_ref)
    weighted = gathered(z, tab_in, chip_ref, across_ref, far_ref, near_ref, hots_ref)
    for pair in range(z.cells // 2):
        rows = pair_rows(pair)
        value = acc_ref[rows, :] + nonlocal_pair(weighted[block_of(z, pair)], proj_ref, pair)
        first_ref[rows, :] = (value / half_width).astype(BF16)
    projector = Projector(z, first_ref, proj_ref)
    projector.add(range(z.cells // 2))
    scatter(z, projector.sums(), hots_ref, tab_ref)
    put_across(z, tab_ref, first_ref, far_out)


def filtered_kernel(
    z, base_ref, tab_ref, chip_ref, across_ref, far_ref, near_ref, hots_ref, proj_ref, start_ref, out_ref, acc_ref
):
    add_across(z, base_ref, across_ref, acc_ref)
    weighted = gathered(z, tab_ref, chip_ref, across_ref, far_ref, near_ref, hots_ref)
    for pair in range(z.cells // 2):
        rows = pair_rows(pair)
        value = acc_ref[rows, :] + nonlocal_pair(weighted[block_of(z, pair)], proj_ref, pair)
        out_ref[rows, :] = (2.0 * value / half_width - start_ref[rows, :].astype(F32)).astype(BF16)


VMEM = pl.BlockSpec(memory_space=pltpu.VMEM)


def call(kernel, z, name, outs, ins, flops, moved, scratch=()):
    single = not isinstance(outs, (list, tuple))
    return pl.pallas_call(
        functools.partial(kernel, z),
        name=name,
        out_shape=outs,
        in_specs=[VMEM] * len(ins),
        out_specs=VMEM if single else [VMEM] * len(outs),
        scratch_shapes=list(scratch),
        compiler_params=pltpu.CompilerParams(vmem_limit_bytes=12288 * 1024),
        cost_estimate=pl.CostEstimate(flops=flops, bytes_accessed=moved, transcendentals=0),
    )(*ins)


class Shapes:
    def __init__(self, z):
        self.tile = jax.ShapeDtypeStruct((z.bands, z.lanes), F32)
        self.pair = jax.ShapeDtypeStruct((2, z.bands, z.lanes), F32)
        self.tab = jax.ShapeDtypeStruct((3, z.bands, z.lanes), F32)
        self.slab = jax.ShapeDtypeStruct((z.tall, z.depth), BF16)
        self.message = jax.ShapeDtypeStruct((z.tall + 6 * z.bands, z.depth), BF16)
        self.base = jax.ShapeDtypeStruct((z.tall, z.depth), F32)
        self.near = jax.ShapeDtypeStruct((8, z.lanes), F32)
        self.hots = jax.ShapeDtypeStruct((z.blocks, 3 * z.lanes, z.slots), BF16)
        self.wide = [pltpu.VMEM((3 * z.cells, z.bands, z.depth), F32)]
        self.acc = [pltpu.VMEM((z.tall, z.depth), F32)]
        self.stream = 2 * z.tall * z.slots * z.depth
        self.proj_bytes = 2 * z.cells * z.slots * z.depth
        self.stencil = 6 * z.tall * z.depth * z.depth
        self.slab_bytes = 10 * z.tall * z.depth


def swap_on_chip(x, axis):
    count = lax.axis_size(axis)
    return lax.ppermute(x, axis, [(i, i ^ 1) for i in range(count)])


def swap_across(x, axis):
    count = lax.axis_size(axis)
    return lax.ppermute(x, axis, [(i, (((i + 1) ^ 1) - 1) % count) for i in range(count)])


def swap_far(x, axis):
    count = lax.axis_size(axis)
    return lax.ppermute(x, axis, [(i, (i + 2 - 4 * (i % 2)) % count) for i in range(count)])


def local(bands, potential, projectors, atom_ids, strength, rotation):
    z = Sizes(bands.shape, atom_ids.shape, strength.shape, lax.axis_size("dom"))
    groups = lax.axis_size("band")
    proj = projectors.reshape(z.cells, z.slots, z.depth)
    pot = potential.reshape(z.cells, z.depth)
    flat = bands.reshape(z.bands, z.cells, z.depth)

    s = Shapes(z)

    def exchange(tab, far, slab):
        across = swap_across(slab, "dom")
        far = swap_far(far, "dom")
        on_chip = swap_on_chip(slab, "dom")
        mate = call(meet_kernel, z, "meet", s.pair, (tab, across), 1000, 1000)
        return on_chip, (tab, swap_on_chip(mate, "dom"), across, far)

    pause = call(pause_kernel, z, "pause", s.tile, (), 4000 * s.stream, 40_000_000)
    start, hots = call(
        prepare_kernel, z, "prepare", [s.slab, s.hots], (pause, atom_ids, flat), s.stream, s.proj_bytes,
    )
    tab, far, start = call(
        project_kernel, z, "project", [s.tab, s.tile, s.message], (start, hots, proj), s.stream, s.proj_bytes,
    )
    on_chip, sums = exchange(tab, far, start)
    base, near = call(
        base_first_kernel, z, "base_first", [s.base, s.near],
        (start, on_chip, pot, strength.T), 60 * s.stencil, s.slab_bytes, scratch=s.wide,
    )
    first, tab, far = call(
        first_kernel, z, "first", [s.message, s.tab, s.tile],
        (base,) + sums + (near, hots, proj), 2 * s.stream, s.proj_bytes, scratch=s.acc,
    )
    on_chip, sums = exchange(tab, far, first)
    base = call(
        base_kernel, z, "base", s.base, (first, on_chip, pot), 60 * s.stencil, s.slab_bytes, scratch=s.wide,
    )
    filtered = call(
        filtered_kernel, z, "filtered", s.slab, (base,) + sums + (near, hots, proj, start),
        s.stream, s.proj_bytes, scratch=s.acc,
    )

    share = z.cells // groups
    pieces = filtered.reshape(groups, share, z.bands, z.depth)
    pieces = lax.all_to_all(pieces, "band", 0, 0, tiled=True)
    turn = rotation.reshape(groups, z.bands, groups * z.bands)
    rotated = jnp.einsum("gxbz,gbc->xcz", pieces, turn, preferred_element_type=F32).astype(BF16)
    rotated = rotated.reshape(share, groups, z.bands, z.depth).transpose(1, 0, 2, 3)
    rotated = lax.all_to_all(rotated, "band", 0, 0, tiled=True)
    return rotated.reshape(z.cells, z.bands, z.depth).transpose(1, 0, 2).reshape(bands.shape)


def solution(mesh):
    placed = (
        P("band", "dom", None, None),
        P("dom", None, None),
        P("dom", None, None, None, None),
        P("dom", None),
        P(),
        P(),
    )
    return jax.shard_map(
        local, mesh=mesh, in_specs=placed, out_specs=P("band", "dom", None, None), check_vma=False
    )
```

```python
import functools
import jax
import jax.numpy as jnp
import numpy as np
from jax import lax
from jax.experimental import pallas as pl
from jax.experimental.pallas import tpu as pltpu
from jax.sharding import PartitionSpec as P

STENCIL = [
    -5369.0 / 1800.0,
    12.0 / 7.0,
    -15.0 / 56.0,
    10.0 / 189.0,
    -1.0 / 112.0,
    2.0 / 1925.0,
    -1.0 / 16632.0,
]
kinetic_scale = 0.5 / 0.49
centre = 12.0
half_width = 11.0
REACH = 6
F32, BF16 = jnp.float32, jnp.bfloat16
WEIGHTS = [-kinetic_scale * w for w in STENCIL]


def split3(x):
    hi = x.astype(BF16)
    rest = x - hi.astype(F32)
    mid = rest.astype(BF16)
    return hi, mid, (rest - mid.astype(F32)).astype(BF16)


def z_matrix(depth):
    row = lax.broadcasted_iota(jnp.int32, (depth, depth), 0)
    col = lax.broadcasted_iota(jnp.int32, (depth, depth), 1)
    apart = jnp.abs(row - col)
    apart = jnp.minimum(apart, depth - apart)
    full = jnp.zeros((depth, depth), F32)
    for offset in range(1, REACH + 1):
        full = jnp.where(apart == offset, np.float32(WEIGHTS[offset]), full)
    return jnp.concatenate(split3(full), 0)


def dot_t(a, b):
    return lax.dot_general(a, b, (((1,), (1,)), ((), ())), preferred_element_type=F32)


class Sizes:
    def __init__(self, bands, atom_ids, strength, dom_count):
        self.bands, self.thickness, self.rows, self.depth = bands
        self.blocks, self.slot_count = atom_ids
        self.atoms, self.projs = strength
        self.doms = dom_count
        self.owned = self.atoms // dom_count
        self.block_rows = self.rows // self.blocks
        self.cells = self.thickness * self.rows
        self.slots = self.slot_count * self.projs
        self.lanes = self.owned * self.projs
        self.tall = self.cells * self.bands
        assert self.owned & (self.owned - 1) == 0 and dom_count & (dom_count - 1) == 0


def one_hots(z, dom, ids_ref):
    ids = ids_ref[...]
    shift = z.owned.bit_length() - 1
    relative = ((ids >> shift) - dom + (1 + z.doms)) & (z.doms - 1)
    place = relative * z.owned + (ids & (z.owned - 1))
    slot = lax.broadcasted_iota(jnp.int32, (z.slot_count, z.slots), 0)
    lane = lax.broadcasted_iota(jnp.int32, (z.slot_count, z.slots), 1)
    inside = lane - slot * z.projs
    spread = jnp.where((inside >= 0) & (inside < z.projs), 1.0, 0.0).astype(BF16)
    wide = jnp.dot(place.astype(F32).astype(BF16), spread, preferred_element_type=F32)
    shape = (z.lanes, z.slots)
    row = lax.broadcasted_iota(jnp.int32, shape, 0)
    lane = lax.broadcasted_iota(jnp.int32, shape, 1)
    fits = (row >> shift) == lane % z.projs
    atom = (row & (z.owned - 1)).astype(F32)
    out = []
    for j in range(z.blocks):
        mine = jnp.broadcast_to(wide[j : j + 1, :], shape)
        tiles = [
            jnp.where(fits & (mine == atom + float(z.owned * tile)), 1.0, 0.0) for tile in range(3)
        ]
        out.append(jnp.concatenate(tiles, 0).astype(BF16))
    return out


def scatter(z, partials, hots_ref, tab_ref):
    total = None
    b = z.bands
    for j, partial in enumerate(partials):
        pieces = jnp.concatenate([piece.astype(F32) for piece in split3(partial)], 0)
        part = dot_t(pieces.astype(BF16), hots_ref[j])
        part = part[:b] + part[b : 2 * b] + part[2 * b :]
        total = part if total is None else total + part
    for t in range(3):
        tab_ref[t] = total[:, t * z.lanes : (t + 1) * z.lanes]


def put_across(z, tab_ref, slab_ref, far_ref):
    first_core = (lax.axis_index("dom") & 1) == 0
    pair = [
        jnp.where(first_core, tab_ref[0], tab_ref[1]),
        jnp.where(first_core, tab_ref[1], tab_ref[2]),
    ]
    put_tiles(z, pair, slab_ref)
    far_ref[...] = jnp.where(first_core, tab_ref[2], tab_ref[0])


def mate_tiles(side, tab_ref):
    first_core = side == 0
    return [
        jnp.where(first_core, tab_ref[1], tab_ref[0]),
        jnp.where(first_core, tab_ref[2], tab_ref[1]),
    ]


def put_mate(z, tab_ref, slab_ref):
    side = lax.axis_index("dom") & 1
    put_tiles(z, mate_tiles(side, tab_ref), slab_ref)
    outer = jnp.where(side == 0, tab_ref[0], tab_ref[2])
    pieces = list(split3(outer)) + [jnp.zeros(outer.shape, BF16)]
    slab_ref[z.tall + 6 * z.bands :, :] = jnp.concatenate([p.astype(F32) for p in pieces], 0).astype(BF16)


def put_tiles(z, tiles, slab_ref):
    for n, piece in enumerate(split3(jnp.concatenate(tiles, 0))):
        slab_ref[z.tall + n * 2 * z.bands : z.tall + (n + 1) * 2 * z.bands, :] = piece


def get_tiles(z, slab_ref):
    total = None
    for n in range(3):
        piece = slab_ref[z.tall + n * 2 * z.bands : z.tall + (n + 1) * 2 * z.bands, :].astype(F32)
        total = piece if total is None else total + piece
    return [total[: z.bands], total[z.bands :]]


def meet_kernel(z, tab_ref, across_ref, mate_ref):
    first_core = (lax.axis_index("dom") & 1) == 0
    got = get_tiles(z, across_ref)
    mate_ref[0] = jnp.where(first_core, got[1] + tab_ref[1], tab_ref[0])
    mate_ref[1] = jnp.where(first_core, tab_ref[2], tab_ref[1] + got[0])


def gathered(z, tab_ref, mate_ref, across_ref, far_ref, strength_ref, hots_ref):
    first_core = (lax.axis_index("dom") & 1) == 0
    got = get_tiles(z, across_ref)
    below, middle, above = tab_ref[0], tab_ref[1], tab_ref[2]
    low, high, far = mate_ref[0], mate_ref[1], far_ref[...]
    tiles = [
        below + jnp.where(first_core, got[0] + far, low),
        middle + jnp.where(first_core, got[1] + low, got[0] + high),
        above + jnp.where(first_core, high, got[1] + far),
    ]
    weighted = [tile * strength_ref[t : t + 1, :] for t, tile in enumerate(tiles)]
    weighted = jnp.concatenate(weighted, 1).astype(BF16)
    return [
        jnp.dot(weighted, hots_ref[j], preferred_element_type=F32).astype(BF16)
        for j in range(z.blocks)
    ]


def meet_second_kernel(z, tab_ref, got_ref, slab_in, slab_ref, chip_ref, far_ref):
    slab_ref[: z.tall, :] = slab_in[: z.tall, :]
    side = lax.axis_index("dom") & 1
    first_core = side == 0
    mate, got = mate_tiles(side, tab_ref), get_tiles(z, got_ref)
    low, high = mate[0] + got[0], mate[1] + got[1]
    chip_ref[0], chip_ref[1] = low, high
    outer = got_ref[z.tall + 6 * z.bands :, :].astype(F32)
    far_ref[...] = outer[: z.bands] + outer[z.bands : 2 * z.bands] + outer[2 * z.bands : 3 * z.bands]
    below, above = tab_ref[0], tab_ref[2]
    pair = [jnp.where(first_core, below, high), jnp.where(first_core, low, above)]
    put_tiles(z, pair, slab_ref)


def gathered_second(z, tab_ref, chip_ref, across_ref, far_ref, strength_ref, hots_ref):
    first_core = (lax.axis_index("dom") & 1) == 0
    got = get_tiles(z, across_ref)
    low, high, far = chip_ref[0], chip_ref[1], far_ref[...]
    tiles = [
        jnp.where(first_core, tab_ref[0] + got[0], low + far),
        jnp.where(first_core, low + got[1], high + got[0]),
        jnp.where(first_core, high + far, tab_ref[2] + got[1]),
    ]
    weighted = [tile * strength_ref[t : t + 1, :] for t, tile in enumerate(tiles)]
    weighted = jnp.concatenate(weighted, 1).astype(BF16)
    return [
        jnp.dot(weighted, hots_ref[j], preferred_element_type=F32).astype(BF16)
        for j in range(z.blocks)
    ]


def pair_rows(pair):
    return slice(16 * pair, 16 * pair + 16)


def block_of(z, pair):
    return (2 * pair % z.rows) // z.block_rows


class Projector:
    def __init__(self, z, v_ref, proj_ref):
        self.z, self.v_ref, self.proj_ref = z, v_ref, proj_ref
        self.total = [None] * z.blocks

    def add(self, pairs):
        b = self.z.bands
        for pair in pairs:
            j = block_of(self.z, pair)
            v = self.v_ref[pair_rows(pair), :].astype(F32)
            v = jnp.concatenate([v[:b], v[b:]], 1).astype(BF16)
            both = jnp.concatenate([self.proj_ref[2 * pair], self.proj_ref[2 * pair + 1]], 1)
            part = dot_t(v, both)
            self.total[j] = part if self.total[j] is None else self.total[j] + part

    def sums(self):
        return self.total


def turned(z, bands_ref, x):
    plane = bands_ref[:, x * z.rows : (x + 1) * z.rows, :].astype(F32)
    return jnp.swapaxes(plane, 0, 1)


def turn_all(z, bands_ref, v_ref):
    tall = z.rows * z.bands
    for x in range(z.thickness):
        plane = turned(z, bands_ref, x).reshape(tall, z.depth)
        v_ref[x * tall : (x + 1) * tall, :] = plane.astype(BF16)


def pause_kernel(z, out_ref):
    out_ref[...] = jnp.zeros_like(out_ref)


def prepare_kernel(z, pause_ref, ids_ref, bands_ref, v_ref, hots_ref):
    turn_all(z, bands_ref, v_ref)
    for j, hot in enumerate(one_hots(z, lax.axis_index("dom"), ids_ref)):
        hots_ref[j] = hot


def project_kernel(z, v_in, hots_ref, proj_ref, tab_ref, far_ref, v_ref):
    v_ref[: z.tall, :] = v_in[...]
    projector = Projector(z, v_in, proj_ref)
    projector.add(range(z.cells // 2))
    scatter(z, projector.sums(), hots_ref, tab_ref)
    put_across(z, tab_ref, v_ref, far_ref)


def near_strength(z, dom, strength_ref, out_ref):
    per_tile = 128 // z.owned
    row = lax.broadcasted_iota(jnp.int32, (z.projs, 128), 0)
    lane = lax.broadcasted_iota(jnp.int32, (z.projs, 128), 1)
    for t in range(3):
        owner = (dom + (t - 1) + z.doms) & (z.doms - 1)
        tile = strength_ref[:, pl.ds(pl.multiple_of(owner // per_tile * 128, 128), 128)]
        inside = owner % per_tile
        line = jnp.zeros((1, 128), F32)
        for p in range(z.projs):
            turned = pltpu.roll(tile, ((p + per_tile) - inside) % per_tile * z.owned, 1)
            keep = (row == p) & (lane >= p * z.owned) & (lane < (p + 1) * z.owned)
            line = line + jnp.sum(jnp.where(keep, turned, 0.0), axis=0, keepdims=True)
        out_ref[t : t + 1, :] = line


def base_body(z, dom, v_ref, wide_ref, write):
    b = z.bands
    zmat = z_matrix(z.depth)
    for c in range(0, z.cells, z.rows):
        v = v_ref[b * c : b * (c + z.rows), :]
        along_z = jnp.dot(jnp.concatenate([v, v, v], 1), zmat, preferred_element_type=F32)
        for y in range(0, z.rows, 2):
            both = []
            for at in (y, y + 1):
                here = z.cells + c + at
                total = wide_ref[here] * (write.pot(c + at) + (3.0 * WEIGHTS[0] - centre))
                total = total + along_z[b * at : b * at + b, :]
                for offset in range(1, REACH + 1):
                    beside = wide_ref[here + offset * z.rows] + wide_ref[here - offset * z.rows]
                    up = z.cells + c + (at + offset) % z.rows
                    down = z.cells + c + (at - offset) % z.rows
                    beside = beside + (wide_ref[up] + wide_ref[down])
                    total = total + WEIGHTS[offset] * beside
                both.append(total)
            write((c + y) // 2, jnp.concatenate(both, 0))


class Writer:
    def __init__(self, pot_ref, put):
        self.pot_ref, self.put = pot_ref, put

    def pot(self, cell):
        return self.pot_ref[cell : cell + 1, :]

    def __call__(self, pair, value):
        self.put(pair_rows(pair), value)


def fill_and_base(z, v_ref, on_ref, pot_ref, out_ref, wide_ref):
    dom = lax.axis_index("dom")
    first_core = (dom & 1) == 0
    on_at = pl.multiple_of(jnp.where(first_core, 2 * z.cells, 0), z.cells)
    off_at = pl.multiple_of(jnp.where(first_core, 0, 2 * z.cells), z.cells)
    step, b = 8, z.bands

    def tile(ref, c):
        return ref[b * c : b * (c + step), :].astype(F32).reshape(step, b, z.depth)

    for c in range(0, z.cells, step):
        wide_ref[z.cells + c : z.cells + c + step] = tile(v_ref, c)
        wide_ref[pl.ds(on_at + c, step)] = tile(on_ref, c)
        wide_ref[pl.ds(off_at + c, step)] = jnp.zeros((step, b, z.depth), F32)

    def put(rows, value):
        out_ref[rows, :] = value

    base_body(z, dom, v_ref, wide_ref, Writer(pot_ref, put))


def add_across(z, base_ref, across_ref, acc_ref):
    side = lax.axis_index("dom") & 1
    tall = z.rows * z.bands
    last = z.thickness - 1

    def at(plane, c):
        there = jnp.where(side == 0, plane, last - plane)
        return pl.ds(pl.multiple_of(there * tall + c, 32), 32)

    for c in range(0, tall, 32):
        planes = [across_ref[at(q, c), :].astype(F32) for q in range(z.thickness)]
        for x in range(z.thickness):
            total = base_ref[at(x, c), :]
            for q in range(x, z.thickness):
                offset = x - q + z.thickness
                if offset <= REACH:
                    total = total + WEIGHTS[offset] * planes[q]
            acc_ref[at(x, c), :] = total


def base_first_kernel(z, v_ref, on_ref, pot_ref, strength_ref, out_ref, near_ref, wide_ref):
    fill_and_base(z, v_ref, on_ref, pot_ref, out_ref, wide_ref)
    near_strength(z, lax.axis_index("dom"), strength_ref, near_ref)


def base_kernel(z, v_ref, on_ref, pot_ref, out_ref, wide_ref):
    fill_and_base(z, v_ref, on_ref, pot_ref, out_ref, wide_ref)


def nonlocal_pair(weighted, proj_ref, pair):
    both = jnp.concatenate([proj_ref[2 * pair], proj_ref[2 * pair + 1]], 1)
    value = jnp.dot(weighted, both, preferred_element_type=F32)
    half = value.shape[1] // 2
    return jnp.concatenate([value[:, :half], value[:, half:]], 0)


def first_kernel(
    z, base_ref, tab_in, chip_ref, across_ref, far_ref, near_ref, hots_ref, proj_ref, first_ref, tab_ref, acc_ref
):
    add_across(z, base_ref, across_ref, acc_ref)
    weighted = gathered(z, tab_in, chip_ref, across_ref, far_ref, near_ref, hots_ref)
    for pair in range(z.cells // 2):
        rows = pair_rows(pair)
        value = acc_ref[rows, :] + nonlocal_pair(weighted[block_of(z, pair)], proj_ref, pair)
        first_ref[rows, :] = (value * (1.0 / half_width)).astype(BF16)
    projector = Projector(z, first_ref, proj_ref)
    projector.add(range(z.cells // 2))
    scatter(z, projector.sums(), hots_ref, tab_ref)
    put_mate(z, tab_ref, first_ref)


def filtered_kernel(
    z, base_ref, tab_ref, chip_ref, across_ref, far_ref, near_ref, hots_ref, proj_ref, start_ref, out_ref, acc_ref
):
    add_across(z, base_ref, across_ref, acc_ref)
    weighted = gathered_second(z, tab_ref, chip_ref, across_ref, far_ref, near_ref, hots_ref)
    for pair in range(z.cells // 2):
        rows = pair_rows(pair)
        value = acc_ref[rows, :] + nonlocal_pair(weighted[block_of(z, pair)], proj_ref, pair)
        out_ref[rows, :] = (value * (2.0 / half_width) - start_ref[rows, :].astype(F32)).astype(BF16)


VMEM = pl.BlockSpec(memory_space=pltpu.VMEM)


def call(kernel, z, name, outs, ins, flops, moved, scratch=()):
    single = not isinstance(outs, (list, tuple))
    return pl.pallas_call(
        functools.partial(kernel, z),
        name=name,
        out_shape=outs,
        in_specs=[VMEM] * len(ins),
        out_specs=VMEM if single else [VMEM] * len(outs),
        scratch_shapes=list(scratch),
        compiler_params=pltpu.CompilerParams(vmem_limit_bytes=12288 * 1024),
        cost_estimate=pl.CostEstimate(flops=flops, bytes_accessed=moved, transcendentals=0),
    )(*ins)


class Shapes:
    def __init__(self, z):
        self.tile = jax.ShapeDtypeStruct((z.bands, z.lanes), F32)
        self.pair = jax.ShapeDtypeStruct((2, z.bands, z.lanes), F32)
        self.tab = jax.ShapeDtypeStruct((3, z.bands, z.lanes), F32)
        self.slab = jax.ShapeDtypeStruct((z.tall, z.depth), BF16)
        self.message = jax.ShapeDtypeStruct((z.tall + 6 * z.bands, z.depth), BF16)
        self.mate_message = jax.ShapeDtypeStruct((z.tall + 10 * z.bands, z.depth), BF16)
        self.base = jax.ShapeDtypeStruct((z.tall, z.depth), F32)
        self.near = jax.ShapeDtypeStruct((8, z.lanes), F32)
        self.hots = jax.ShapeDtypeStruct((z.blocks, 3 * z.lanes, z.slots), BF16)
        self.wide = [pltpu.VMEM((3 * z.cells, z.bands, z.depth), F32)]
        self.acc = [pltpu.VMEM((z.tall, z.depth), F32)]
        self.stream = 2 * z.tall * z.slots * z.depth
        self.proj_bytes = 2 * z.cells * z.slots * z.depth
        self.stencil = 6 * z.tall * z.depth * z.depth
        self.slab_bytes = 10 * z.tall * z.depth


def swap_on_chip(x, axis):
    count = lax.axis_size(axis)
    return lax.ppermute(x, axis, [(i, i ^ 1) for i in range(count)])


def swap_across(x, axis):
    count = lax.axis_size(axis)
    return lax.ppermute(x, axis, [(i, (((i + 1) ^ 1) - 1) % count) for i in range(count)])


def swap_far(x, axis):
    count = lax.axis_size(axis)
    return lax.ppermute(x, axis, [(i, (i + 2 - 4 * (i % 2)) % count) for i in range(count)])


def swap_crossed(x, axis):
    count = lax.axis_size(axis)
    return lax.ppermute(x, axis, [(i, (i + 3 - 6 * (i % 2)) % count) for i in range(count)])


def local(bands, potential, projectors, atom_ids, strength, rotation):
    z = Sizes(bands.shape, atom_ids.shape, strength.shape, lax.axis_size("dom"))
    groups = lax.axis_size("band")
    proj = projectors.reshape(z.cells, z.slots, z.depth)
    pot = potential.reshape(z.cells, z.depth)
    flat = bands.reshape(z.bands, z.cells, z.depth)

    s = Shapes(z)

    def exchange(tab, far, slab):
        across = swap_across(slab, "dom")
        far = swap_far(far, "dom")
        on_chip = swap_on_chip(slab, "dom")
        mate = call(meet_kernel, z, "meet", s.pair, (tab, across), 1000, 1000)
        return on_chip, (tab, swap_on_chip(mate, "dom"), across, far)

    def exchange_second(tab, slab):
        on_chip = swap_on_chip(slab, "dom")
        slab, chip, far = call(
            meet_second_kernel, z, "meet_second", [s.message, s.pair, s.tile], (tab, on_chip, slab), 1000, 1000
        )
        across = swap_across(slab, "dom")
        far = swap_crossed(far, "dom")
        return slab, on_chip, (tab, chip, across, far)

    pause = call(pause_kernel, z, "pause", s.tile, (), 4000 * s.stream, 40_000_000)
    start, hots = call(
        prepare_kernel, z, "prepare", [s.slab, s.hots], (pause, atom_ids, flat), s.stream, s.proj_bytes,
    )
    tab, far, start = call(
        project_kernel, z, "project", [s.tab, s.tile, s.message], (start, hots, proj), s.stream, s.proj_bytes,
    )
    on_chip, sums = exchange(tab, far, start)
    base, near = call(
        base_first_kernel, z, "base_first", [s.base, s.near],
        (start, on_chip, pot, strength.T), 60 * s.stencil, s.slab_bytes, scratch=s.wide,
    )
    first, tab = call(
        first_kernel, z, "first", [s.mate_message, s.tab],
        (base,) + sums + (near, hots, proj), 2 * s.stream, s.proj_bytes, scratch=s.acc,
    )
    first, on_chip, sums = exchange_second(tab, first)
    base = call(
        base_kernel, z, "base", s.base, (first, on_chip, pot), s.stencil, s.slab_bytes, scratch=s.wide,
    )
    filtered = call(
        filtered_kernel, z, "filtered", s.slab, (base,) + sums + (near, hots, proj, start),
        s.stream, s.proj_bytes, scratch=s.acc,
    )

    share = z.cells // groups
    pieces = filtered.reshape(groups, share, z.bands, z.depth)
    pieces = lax.all_to_all(pieces, "band", 0, 0, tiled=True)
    turn = rotation.reshape(groups, z.bands, groups * z.bands)
    rotated = jnp.einsum("gxbz,gbc->xcz", pieces, turn, preferred_element_type=F32).astype(BF16)
    rotated = rotated.reshape(share, groups, z.bands, z.depth).transpose(1, 0, 2, 3)
    rotated = lax.all_to_all(rotated, "band", 0, 0, tiled=True)
    return rotated.reshape(z.cells, z.bands, z.depth).transpose(1, 0, 2).reshape(bands.shape)


def solution(mesh):
    placed = (
        P("band", "dom", None, None),
        P("dom", None, None),
        P("dom", None, None, None, None),
        P("dom", None),
        P(),
        P(),
    )
    return jax.shard_map(
        local, mesh=mesh, in_specs=placed, out_specs=P("band", "dom", None, None), check_vma=False
    )
```

```python
import functools
import jax
import jax.numpy as jnp
import numpy as np
from jax import lax
from jax.experimental import pallas as pl
from jax.experimental.pallas import tpu as pltpu
from jax.sharding import PartitionSpec as P

STENCIL = [
    -5369.0 / 1800.0,
    12.0 / 7.0,
    -15.0 / 56.0,
    10.0 / 189.0,
    -1.0 / 112.0,
    2.0 / 1925.0,
    -1.0 / 16632.0,
]
kinetic_scale = 0.5 / 0.49
centre = 12.0
half_width = 11.0
REACH = 6
F32, BF16 = jnp.float32, jnp.bfloat16
WEIGHTS = [-kinetic_scale * w for w in STENCIL]


def split3(x):
    hi = x.astype(BF16)
    rest = x - hi.astype(F32)
    mid = rest.astype(BF16)
    return hi, mid, (rest - mid.astype(F32)).astype(BF16)


def z_matrix(depth):
    row = lax.broadcasted_iota(jnp.int32, (depth, depth), 0)
    col = lax.broadcasted_iota(jnp.int32, (depth, depth), 1)
    apart = jnp.abs(row - col)
    apart = jnp.minimum(apart, depth - apart)
    full = jnp.zeros((depth, depth), F32)
    for offset in range(1, REACH + 1):
        full = jnp.where(apart == offset, np.float32(WEIGHTS[offset]), full)
    return jnp.concatenate(split3(full), 0)


def dot_t(a, b):
    return lax.dot_general(a, b, (((1,), (1,)), ((), ())), preferred_element_type=F32)


class Sizes:
    def __init__(self, bands, atom_ids, strength, dom_count):
        self.bands, self.thickness, self.rows, self.depth = bands
        self.blocks, self.slot_count = atom_ids
        self.atoms, self.projs = strength
        self.doms = dom_count
        self.owned = self.atoms // dom_count
        self.block_rows = self.rows // self.blocks
        self.cells = self.thickness * self.rows
        self.slots = self.slot_count * self.projs
        self.lanes = self.owned * self.projs
        self.tall = self.cells * self.bands
        assert self.owned & (self.owned - 1) == 0 and dom_count & (dom_count - 1) == 0


def one_hots(z, dom, ids_ref):
    ids = ids_ref[...]
    shift = z.owned.bit_length() - 1
    relative = ((ids >> shift) - dom + (1 + z.doms)) & (z.doms - 1)
    place = relative * z.owned + (ids & (z.owned - 1))
    slot = lax.broadcasted_iota(jnp.int32, (z.slot_count, z.slots), 0)
    lane = lax.broadcasted_iota(jnp.int32, (z.slot_count, z.slots), 1)
    inside = lane - slot * z.projs
    spread = jnp.where((inside >= 0) & (inside < z.projs), 1.0, 0.0).astype(BF16)
    wide = jnp.dot(place.astype(F32).astype(BF16), spread, preferred_element_type=F32)
    shape = (z.lanes, z.slots)
    row = lax.broadcasted_iota(jnp.int32, shape, 0)
    lane = lax.broadcasted_iota(jnp.int32, shape, 1)
    fits = (row >> shift) == lane % z.projs
    atom = (row & (z.owned - 1)).astype(F32)
    out = []
    for j in range(z.blocks):
        mine = jnp.broadcast_to(wide[j : j + 1, :], shape)
        tiles = [
            jnp.where(fits & (mine == atom + float(z.owned * tile)), 1.0, 0.0) for tile in range(3)
        ]
        out.append(jnp.concatenate(tiles, 0).astype(BF16))
    return out


def scatter(z, partials, hots_ref, tab_ref):
    total = None
    b = z.bands
    for j, partial in enumerate(partials):
        pieces = jnp.concatenate([piece.astype(F32) for piece in split3(partial)], 0)
        part = dot_t(pieces.astype(BF16), hots_ref[j])
        part = part[:b] + part[b : 2 * b] + part[2 * b :]
        total = part if total is None else total + part
    for t in range(3):
        tab_ref[t] = total[:, t * z.lanes : (t + 1) * z.lanes]


def mate_tiles(side, tab_ref):
    first_core = side == 0
    return [
        jnp.where(first_core, tab_ref[1], tab_ref[0]),
        jnp.where(first_core, tab_ref[2], tab_ref[1]),
    ]


def put_mate(z, tab_ref, slab_ref):
    side = lax.axis_index("dom") & 1
    put_tiles(z, mate_tiles(side, tab_ref), slab_ref)
    outer = jnp.where(side == 0, tab_ref[0], tab_ref[2])
    pieces = list(split3(outer)) + [jnp.zeros(outer.shape, BF16)]
    slab_ref[z.tall + 6 * z.bands :, :] = jnp.concatenate([p.astype(F32) for p in pieces], 0).astype(BF16)


def put_tiles(z, tiles, slab_ref):
    for n, piece in enumerate(split3(jnp.concatenate(tiles, 0))):
        slab_ref[z.tall + n * 2 * z.bands : z.tall + (n + 1) * 2 * z.bands, :] = piece


def get_tiles(z, slab_ref):
    total = None
    for n in range(3):
        piece = slab_ref[z.tall + n * 2 * z.bands : z.tall + (n + 1) * 2 * z.bands, :].astype(F32)
        total = piece if total is None else total + piece
    return [total[: z.bands], total[z.bands :]]


def meet_kernel(z, tab_ref, got_ref, slab_in, slab_ref, chip_ref, far_ref):
    slab_ref[: z.tall, :] = slab_in[: z.tall, :]
    side = lax.axis_index("dom") & 1
    first_core = side == 0
    mate, got = mate_tiles(side, tab_ref), get_tiles(z, got_ref)
    low, high = mate[0] + got[0], mate[1] + got[1]
    chip_ref[0], chip_ref[1] = low, high
    outer = got_ref[z.tall + 6 * z.bands :, :].astype(F32)
    far_ref[...] = outer[: z.bands] + outer[z.bands : 2 * z.bands] + outer[2 * z.bands : 3 * z.bands]
    below, above = tab_ref[0], tab_ref[2]
    pair = [jnp.where(first_core, below, high), jnp.where(first_core, low, above)]
    put_tiles(z, pair, slab_ref)


def gathered(z, tab_ref, chip_ref, across_ref, far_ref, strength_ref, hots_ref):
    first_core = (lax.axis_index("dom") & 1) == 0
    got = get_tiles(z, across_ref)
    low, high, far = chip_ref[0], chip_ref[1], far_ref[...]
    tiles = [
        jnp.where(first_core, tab_ref[0] + got[0], low + far),
        jnp.where(first_core, low + got[1], high + got[0]),
        jnp.where(first_core, high + far, tab_ref[2] + got[1]),
    ]
    weighted = [tile * strength_ref[t : t + 1, :] for t, tile in enumerate(tiles)]
    weighted = jnp.concatenate(weighted, 1).astype(BF16)
    return [
        jnp.dot(weighted, hots_ref[j], preferred_element_type=F32).astype(BF16)
        for j in range(z.blocks)
    ]


def pair_rows(pair):
    return slice(16 * pair, 16 * pair + 16)


def block_of(z, pair):
    return (2 * pair % z.rows) // z.block_rows


class Projector:
    def __init__(self, z, v_ref, proj_ref):
        self.z, self.v_ref, self.proj_ref = z, v_ref, proj_ref
        self.total = [None] * z.blocks

    def add(self, pairs):
        b = self.z.bands
        for pair in pairs:
            j = block_of(self.z, pair)
            v = self.v_ref[pair_rows(pair), :].astype(F32)
            v = jnp.concatenate([v[:b], v[b:]], 1).astype(BF16)
            both = jnp.concatenate([self.proj_ref[2 * pair], self.proj_ref[2 * pair + 1]], 1)
            part = dot_t(v, both)
            self.total[j] = part if self.total[j] is None else self.total[j] + part

    def sums(self):
        return self.total


def turned(z, bands_ref, x):
    plane = bands_ref[:, x * z.rows : (x + 1) * z.rows, :].astype(F32)
    return jnp.swapaxes(plane, 0, 1)


def turn_all(z, bands_ref, v_ref):
    tall = z.rows * z.bands
    for x in range(z.thickness):
        plane = turned(z, bands_ref, x).reshape(tall, z.depth)
        v_ref[x * tall : (x + 1) * tall, :] = plane.astype(BF16)


def pause_kernel(z, out_ref):
    out_ref[...] = jnp.zeros_like(out_ref)


def prepare_kernel(z, pause_ref, ids_ref, bands_ref, v_ref, hots_ref):
    turn_all(z, bands_ref, v_ref)
    for j, hot in enumerate(one_hots(z, lax.axis_index("dom"), ids_ref)):
        hots_ref[j] = hot


def project_kernel(z, v_in, hots_ref, proj_ref, tab_ref, v_ref):
    v_ref[: z.tall, :] = v_in[...]
    projector = Projector(z, v_in, proj_ref)
    projector.add(range(z.cells // 2))
    scatter(z, projector.sums(), hots_ref, tab_ref)
    put_mate(z, tab_ref, v_ref)


def near_strength(z, dom, strength_ref, out_ref):
    per_tile = 128 // z.owned
    row = lax.broadcasted_iota(jnp.int32, (z.projs, 128), 0)
    lane = lax.broadcasted_iota(jnp.int32, (z.projs, 128), 1)
    for t in range(3):
        owner = (dom + (t - 1) + z.doms) & (z.doms - 1)
        tile = strength_ref[:, pl.ds(pl.multiple_of(owner // per_tile * 128, 128), 128)]
        inside = owner % per_tile
        line = jnp.zeros((1, 128), F32)
        for p in range(z.projs):
            turned = pltpu.roll(tile, ((p + per_tile) - inside) % per_tile * z.owned, 1)
            keep = (row == p) & (lane >= p * z.owned) & (lane < (p + 1) * z.owned)
            line = line + jnp.sum(jnp.where(keep, turned, 0.0), axis=0, keepdims=True)
        out_ref[t : t + 1, :] = line


def base_body(z, dom, v_ref, wide_ref, write):
    b = z.bands
    zmat = z_matrix(z.depth)
    for c in range(0, z.cells, z.rows):
        v = v_ref[b * c : b * (c + z.rows), :]
        along_z = jnp.dot(jnp.concatenate([v, v, v], 1), zmat, preferred_element_type=F32)
        for y in range(0, z.rows, 2):
            both = []
            for at in (y, y + 1):
                here = z.cells + c + at
                total = wide_ref[here] * (write.pot(c + at) + (3.0 * WEIGHTS[0] - centre))
                total = total + along_z[b * at : b * at + b, :]
                for offset in range(1, REACH + 1):
                    beside = wide_ref[here + offset * z.rows] + wide_ref[here - offset * z.rows]
                    up = z.cells + c + (at + offset) % z.rows
                    down = z.cells + c + (at - offset) % z.rows
                    beside = beside + (wide_ref[up] + wide_ref[down])
                    total = total + WEIGHTS[offset] * beside
                both.append(total)
            write((c + y) // 2, jnp.concatenate(both, 0))


class Writer:
    def __init__(self, pot_ref, put):
        self.pot_ref, self.put = pot_ref, put

    def pot(self, cell):
        return self.pot_ref[cell : cell + 1, :]

    def __call__(self, pair, value):
        self.put(pair_rows(pair), value)


def fill_and_base(z, v_ref, on_ref, pot_ref, out_ref, wide_ref):
    dom = lax.axis_index("dom")
    first_core = (dom & 1) == 0
    on_at = pl.multiple_of(jnp.where(first_core, 2 * z.cells, 0), z.cells)
    off_at = pl.multiple_of(jnp.where(first_core, 0, 2 * z.cells), z.cells)
    step, b = 8, z.bands

    def tile(ref, c):
        return ref[b * c : b * (c + step), :].astype(F32).reshape(step, b, z.depth)

    for c in range(0, z.cells, step):
        wide_ref[z.cells + c : z.cells + c + step] = tile(v_ref, c)
        wide_ref[pl.ds(on_at + c, step)] = tile(on_ref, c)
        wide_ref[pl.ds(off_at + c, step)] = jnp.zeros((step, b, z.depth), F32)

    def put(rows, value):
        out_ref[rows, :] = value

    base_body(z, dom, v_ref, wide_ref, Writer(pot_ref, put))


def add_across(z, base_ref, across_ref, acc_ref):
    side = lax.axis_index("dom") & 1
    tall = z.rows * z.bands
    last = z.thickness - 1

    def at(plane, c):
        there = jnp.where(side == 0, plane, last - plane)
        return pl.ds(pl.multiple_of(there * tall + c, 32), 32)

    for c in range(0, tall, 32):
        planes = [across_ref[at(q, c), :].astype(F32) for q in range(z.thickness)]
        for x in range(z.thickness):
            total = base_ref[at(x, c), :]
            for q in range(x, z.thickness):
                offset = x - q + z.thickness
                if offset <= REACH:
                    total = total + WEIGHTS[offset] * planes[q]
            acc_ref[at(x, c), :] = total


def base_first_kernel(z, v_ref, on_ref, pot_ref, strength_ref, out_ref, near_ref, wide_ref):
    fill_and_base(z, v_ref, on_ref, pot_ref, out_ref, wide_ref)
    near_strength(z, lax.axis_index("dom"), strength_ref, near_ref)


def base_kernel(z, v_ref, on_ref, pot_ref, out_ref, wide_ref):
    fill_and_base(z, v_ref, on_ref, pot_ref, out_ref, wide_ref)


def nonlocal_pair(weighted, proj_ref, pair):
    both = jnp.concatenate([proj_ref[2 * pair], proj_ref[2 * pair + 1]], 1)
    value = jnp.dot(weighted, both, preferred_element_type=F32)
    half = value.shape[1] // 2
    return jnp.concatenate([value[:, :half], value[:, half:]], 0)


def first_kernel(
    z, base_ref, tab_in, chip_ref, across_ref, far_ref, near_ref, hots_ref, proj_ref, first_ref, tab_ref, acc_ref
):
    add_across(z, base_ref, across_ref, acc_ref)
    weighted = gathered(z, tab_in, chip_ref, across_ref, far_ref, near_ref, hots_ref)
    for pair in range(z.cells // 2):
        rows = pair_rows(pair)
        value = acc_ref[rows, :] + nonlocal_pair(weighted[block_of(z, pair)], proj_ref, pair)
        first_ref[rows, :] = (value * (1.0 / half_width)).astype(BF16)
    projector = Projector(z, first_ref, proj_ref)
    projector.add(range(z.cells // 2))
    scatter(z, projector.sums(), hots_ref, tab_ref)
    put_mate(z, tab_ref, first_ref)


def filtered_kernel(
    z, base_ref, tab_ref, chip_ref, across_ref, far_ref, near_ref, hots_ref, proj_ref, start_ref, out_ref, acc_ref
):
    add_across(z, base_ref, across_ref, acc_ref)
    weighted = gathered(z, tab_ref, chip_ref, across_ref, far_ref, near_ref, hots_ref)
    for pair in range(z.cells // 2):
        rows = pair_rows(pair)
        value = acc_ref[rows, :] + nonlocal_pair(weighted[block_of(z, pair)], proj_ref, pair)
        out_ref[rows, :] = (value * (2.0 / half_width) - start_ref[rows, :].astype(F32)).astype(BF16)


VMEM = pl.BlockSpec(memory_space=pltpu.VMEM)


def call(kernel, z, name, outs, ins, flops, moved, scratch=()):
    single = not isinstance(outs, (list, tuple))
    return pl.pallas_call(
        functools.partial(kernel, z),
        name=name,
        out_shape=outs,
        in_specs=[VMEM] * len(ins),
        out_specs=VMEM if single else [VMEM] * len(outs),
        scratch_shapes=list(scratch),
        compiler_params=pltpu.CompilerParams(vmem_limit_bytes=12288 * 1024),
        cost_estimate=pl.CostEstimate(flops=flops, bytes_accessed=moved, transcendentals=0),
    )(*ins)


class Shapes:
    def __init__(self, z):
        self.tile = jax.ShapeDtypeStruct((z.bands, z.lanes), F32)
        self.pair = jax.ShapeDtypeStruct((2, z.bands, z.lanes), F32)
        self.tab = jax.ShapeDtypeStruct((3, z.bands, z.lanes), F32)
        self.slab = jax.ShapeDtypeStruct((z.tall, z.depth), BF16)
        self.message = jax.ShapeDtypeStruct((z.tall + 6 * z.bands, z.depth), BF16)
        self.mate_message = jax.ShapeDtypeStruct((z.tall + 10 * z.bands, z.depth), BF16)
        self.base = jax.ShapeDtypeStruct((z.tall, z.depth), F32)
        self.near = jax.ShapeDtypeStruct((8, z.lanes), F32)
        self.hots = jax.ShapeDtypeStruct((z.blocks, 3 * z.lanes, z.slots), BF16)
        self.wide = [pltpu.VMEM((3 * z.cells, z.bands, z.depth), F32)]
        self.acc = [pltpu.VMEM((z.tall, z.depth), F32)]
        self.stream = 2 * z.tall * z.slots * z.depth
        self.proj_bytes = 2 * z.cells * z.slots * z.depth
        self.stencil = 6 * z.tall * z.depth * z.depth
        self.slab_bytes = 10 * z.tall * z.depth


def swap_on_chip(x, axis):
    count = lax.axis_size(axis)
    return lax.ppermute(x, axis, [(i, i ^ 1) for i in range(count)])


def swap_across(x, axis):
    count = lax.axis_size(axis)
    return lax.ppermute(x, axis, [(i, (((i + 1) ^ 1) - 1) % count) for i in range(count)])


def swap_far(x, axis):
    count = lax.axis_size(axis)
    return lax.ppermute(x, axis, [(i, (i + 3 - 6 * (i % 2)) % count) for i in range(count)])


def local(bands, potential, projectors, atom_ids, strength, rotation):
    z = Sizes(bands.shape, atom_ids.shape, strength.shape, lax.axis_size("dom"))
    groups = lax.axis_size("band")
    proj = projectors.reshape(z.cells, z.slots, z.depth)
    pot = potential.reshape(z.cells, z.depth)
    flat = bands.reshape(z.bands, z.cells, z.depth)

    s = Shapes(z)

    def exchange(tab, slab):
        on_chip = swap_on_chip(slab, "dom")
        slab, chip, far = call(
            meet_kernel, z, "meet", [s.message, s.pair, s.tile], (tab, on_chip, slab), 1000, 1000
        )
        across = swap_across(slab, "dom")
        far = swap_far(far, "dom")
        return slab, on_chip, (tab, chip, across, far)

    pause = call(pause_kernel, z, "pause", s.tile, (), 4000 * s.stream, 40_000_000)
    start, hots = call(
        prepare_kernel, z, "prepare", [s.slab, s.hots], (pause, atom_ids, flat), s.stream, s.proj_bytes,
    )
    tab, start = call(
        project_kernel, z, "project", [s.tab, s.mate_message], (start, hots, proj), s.stream, s.proj_bytes,
    )
    start, on_chip, sums = exchange(tab, start)
    base, near = call(
        base_first_kernel, z, "base_first", [s.base, s.near],
        (start, on_chip, pot, strength.T), s.stencil, s.slab_bytes, scratch=s.wide,
    )
    first, tab = call(
        first_kernel, z, "first", [s.mate_message, s.tab],
        (base,) + sums + (near, hots, proj), 2 * s.stream, s.proj_bytes, scratch=s.acc,
    )
    first, on_chip, sums = exchange(tab, first)
    base = call(
        base_kernel, z, "base", s.base, (first, on_chip, pot), s.stencil, s.slab_bytes, scratch=s.wide,
    )
    filtered = call(
        filtered_kernel, z, "filtered", s.slab, (base,) + sums + (near, hots, proj, start),
        s.stream, s.proj_bytes, scratch=s.acc,
    )

    share = z.cells // groups
    pieces = filtered.reshape(groups, share, z.bands, z.depth)
    pieces = lax.all_to_all(pieces, "band", 0, 0, tiled=True)
    turn = rotation.reshape(groups, z.bands, groups * z.bands)
    rotated = jnp.einsum("gxbz,gbc->xcz", pieces, turn, preferred_element_type=F32).astype(BF16)
    rotated = rotated.reshape(share, groups, z.bands, z.depth).transpose(1, 0, 2, 3)
    rotated = lax.all_to_all(rotated, "band", 0, 0, tiled=True)
    return rotated.reshape(z.cells, z.bands, z.depth).transpose(1, 0, 2).reshape(bands.shape)


def solution(mesh):
    placed = (
        P("band", "dom", None, None),
        P("dom", None, None),
        P("dom", None, None, None, None),
        P("dom", None),
        P(),
        P(),
    )
    return jax.shard_map(
        local, mesh=mesh, in_specs=placed, out_specs=P("band", "dom", None, None), check_vma=False
    )
```

```python
import functools
import jax
import jax.numpy as jnp
import numpy as np
from jax import lax
from jax.experimental import pallas as pl
from jax.experimental.pallas import tpu as pltpu
from jax.sharding import PartitionSpec as P

STENCIL = [
    -5369.0 / 1800.0,
    12.0 / 7.0,
    -15.0 / 56.0,
    10.0 / 189.0,
    -1.0 / 112.0,
    2.0 / 1925.0,
    -1.0 / 16632.0,
]
kinetic_scale = 0.5 / 0.49
centre = 12.0
half_width = 11.0
REACH = 6
F32, BF16 = jnp.float32, jnp.bfloat16
WEIGHTS = [-kinetic_scale * w for w in STENCIL]


def split3(x):
    hi = x.astype(BF16)
    rest = x - hi.astype(F32)
    mid = rest.astype(BF16)
    return hi, mid, (rest - mid.astype(F32)).astype(BF16)


def z_matrix(depth):
    row = lax.broadcasted_iota(jnp.int32, (depth, depth), 0)
    col = lax.broadcasted_iota(jnp.int32, (depth, depth), 1)
    apart = jnp.abs(row - col)
    apart = jnp.minimum(apart, depth - apart)
    full = jnp.zeros((depth, depth), F32)
    for offset in range(1, REACH + 1):
        full = jnp.where(apart == offset, np.float32(WEIGHTS[offset]), full)
    return jnp.concatenate(split3(full), 0)


def dot_t(a, b):
    return lax.dot_general(a, b, (((1,), (1,)), ((), ())), preferred_element_type=F32)


class Sizes:
    def __init__(self, bands, atom_ids, strength, dom_count):
        self.bands, self.thickness, self.rows, self.depth = bands
        self.blocks, self.slot_count = atom_ids
        self.atoms, self.projs = strength
        self.doms = dom_count
        self.owned = self.atoms // dom_count
        self.block_rows = self.rows // self.blocks
        self.cells = self.thickness * self.rows
        self.slots = self.slot_count * self.projs
        self.lanes = self.owned * self.projs
        self.tall = self.cells * self.bands
        assert self.owned & (self.owned - 1) == 0 and dom_count & (dom_count - 1) == 0


def one_hots(z, dom, ids_ref):
    ids = ids_ref[...]
    shift = z.owned.bit_length() - 1
    relative = ((ids >> shift) - dom + (1 + z.doms)) & (z.doms - 1)
    place = relative * z.owned + (ids & (z.owned - 1))
    slot = lax.broadcasted_iota(jnp.int32, (z.slot_count, z.slots), 0)
    lane = lax.broadcasted_iota(jnp.int32, (z.slot_count, z.slots), 1)
    inside = lane - slot * z.projs
    spread = jnp.where((inside >= 0) & (inside < z.projs), 1.0, 0.0).astype(BF16)
    wide = jnp.dot(place.astype(F32).astype(BF16), spread, preferred_element_type=F32)
    shape = (z.lanes, z.slots)
    row = lax.broadcasted_iota(jnp.int32, shape, 0)
    lane = lax.broadcasted_iota(jnp.int32, shape, 1)
    fits = (row >> shift) == lane % z.projs
    atom = (row & (z.owned - 1)).astype(F32)
    out = []
    for j in range(z.blocks):
        mine = jnp.broadcast_to(wide[j : j + 1, :], shape)
        tiles = [
            jnp.where(fits & (mine == atom + float(z.owned * tile)), 1.0, 0.0) for tile in range(3)
        ]
        out.append(jnp.concatenate(tiles, 0).astype(BF16))
    return out


def scatter(z, partials, hots_ref, tab_ref):
    total = None
    b = z.bands
    for j, partial in enumerate(partials):
        pieces = jnp.concatenate([piece.astype(F32) for piece in split3(partial)], 0)
        part = dot_t(pieces.astype(BF16), hots_ref[j])
        part = part[:b] + part[b : 2 * b] + part[2 * b :]
        total = part if total is None else total + part
    for t in range(3):
        tab_ref[t] = total[:, t * z.lanes : (t + 1) * z.lanes]


def mate_tiles(side, tab_ref):
    first_core = side == 0
    return [
        jnp.where(first_core, tab_ref[1], tab_ref[0]),
        jnp.where(first_core, tab_ref[2], tab_ref[1]),
    ]


def put_mate(z, tab_ref, slab_ref):
    side = lax.axis_index("dom") & 1
    put_tiles(z, mate_tiles(side, tab_ref), slab_ref)
    outer = jnp.where(side == 0, tab_ref[0], tab_ref[2])
    pieces = list(split3(outer)) + [jnp.zeros(outer.shape, BF16)]
    slab_ref[z.tall + 6 * z.bands :, :] = jnp.concatenate([p.astype(F32) for p in pieces], 0).astype(BF16)


def put_tiles(z, tiles, slab_ref):
    for n, piece in enumerate(split3(jnp.concatenate(tiles, 0))):
        slab_ref[z.tall + n * 2 * z.bands : z.tall + (n + 1) * 2 * z.bands, :] = piece


def get_tiles(z, slab_ref):
    total = None
    for n in range(3):
        piece = slab_ref[z.tall + n * 2 * z.bands : z.tall + (n + 1) * 2 * z.bands, :].astype(F32)
        total = piece if total is None else total + piece
    return [total[: z.bands], total[z.bands :]]


def meet_kernel(z, tab_ref, got_ref, slab_in, slab_ref, chip_ref, far_ref):
    slab_ref[: z.tall, :] = slab_in[: z.tall, :]
    side = lax.axis_index("dom") & 1
    first_core = side == 0
    mate, got = mate_tiles(side, tab_ref), get_tiles(z, got_ref)
    low, high = mate[0] + got[0], mate[1] + got[1]
    chip_ref[0], chip_ref[1] = low, high
    outer = got_ref[z.tall + 6 * z.bands :, :].astype(F32)
    far_ref[...] = outer[: z.bands] + outer[z.bands : 2 * z.bands] + outer[2 * z.bands : 3 * z.bands]
    below, above = tab_ref[0], tab_ref[2]
    pair = [jnp.where(first_core, below, high), jnp.where(first_core, low, above)]
    put_tiles(z, pair, slab_ref)


def gathered(z, tab_ref, chip_ref, across_ref, far_ref, strength_ref, hots_ref):
    first_core = (lax.axis_index("dom") & 1) == 0
    got = get_tiles(z, across_ref)
    low, high, far = chip_ref[0], chip_ref[1], far_ref[...]
    tiles = [
        jnp.where(first_core, tab_ref[0] + got[0], low + far),
        jnp.where(first_core, low + got[1], high + got[0]),
        jnp.where(first_core, high + far, tab_ref[2] + got[1]),
    ]
    weighted = [tile * strength_ref[t : t + 1, :] for t, tile in enumerate(tiles)]
    weighted = jnp.concatenate(weighted, 1).astype(BF16)
    return [
        jnp.dot(weighted, hots_ref[j], preferred_element_type=F32).astype(BF16)
        for j in range(z.blocks)
    ]


def pair_rows(pair):
    return slice(16 * pair, 16 * pair + 16)


def block_of(z, pair):
    return (2 * pair % z.rows) // z.block_rows


class Projector:
    def __init__(self, z, v_ref, proj_ref):
        self.z, self.v_ref, self.proj_ref = z, v_ref, proj_ref
        self.total = [None] * z.blocks

    def add(self, pairs):
        b = self.z.bands
        for pair in pairs:
            j = block_of(self.z, pair)
            v = self.v_ref[pair_rows(pair), :].astype(F32)
            v = jnp.concatenate([v[:b], v[b:]], 1).astype(BF16)
            both = jnp.concatenate([self.proj_ref[2 * pair], self.proj_ref[2 * pair + 1]], 1)
            part = dot_t(v, both)
            self.total[j] = part if self.total[j] is None else self.total[j] + part

    def sums(self):
        return self.total


def turned(z, bands_ref, x):
    plane = bands_ref[:, x * z.rows : (x + 1) * z.rows, :].astype(F32)
    return jnp.swapaxes(plane, 0, 1)


def turn_all(z, bands_ref, v_ref):
    tall = z.rows * z.bands
    for x in range(z.thickness):
        plane = turned(z, bands_ref, x).reshape(tall, z.depth)
        v_ref[x * tall : (x + 1) * tall, :] = plane.astype(BF16)


def pause_kernel(z, out_ref):
    out_ref[...] = jnp.zeros_like(out_ref)


def prepare_kernel(z, pause_ref, ids_ref, bands_ref, v_ref, hots_ref):
    turn_all(z, bands_ref, v_ref)
    for j, hot in enumerate(one_hots(z, lax.axis_index("dom"), ids_ref)):
        hots_ref[j] = hot


def project_kernel(z, v_in, hots_ref, proj_ref, tab_ref, v_ref):
    v_ref[: z.tall, :] = v_in[...]
    projector = Projector(z, v_in, proj_ref)
    projector.add(range(z.cells // 2))
    scatter(z, projector.sums(), hots_ref, tab_ref)
    put_mate(z, tab_ref, v_ref)


def near_strength(z, dom, strength_ref, out_ref):
    per_tile = 128 // z.owned
    row = lax.broadcasted_iota(jnp.int32, (z.projs, 128), 0)
    lane = lax.broadcasted_iota(jnp.int32, (z.projs, 128), 1)
    for t in range(3):
        owner = (dom + (t - 1) + z.doms) & (z.doms - 1)
        tile = strength_ref[:, pl.ds(pl.multiple_of(owner // per_tile * 128, 128), 128)]
        inside = owner % per_tile
        line = jnp.zeros((1, 128), F32)
        for p in range(z.projs):
            turned = pltpu.roll(tile, ((p + per_tile) - inside) % per_tile * z.owned, 1)
            keep = (row == p) & (lane >= p * z.owned) & (lane < (p + 1) * z.owned)
            line = line + jnp.sum(jnp.where(keep, turned, 0.0), axis=0, keepdims=True)
        out_ref[t : t + 1, :] = line


def base_body(z, dom, v_ref, wide_ref, write):
    b = z.bands
    zmat = z_matrix(z.depth)
    for c in range(0, z.cells, z.rows):
        v = v_ref[b * c : b * (c + z.rows), :]
        along_z = jnp.dot(jnp.concatenate([v, v, v], 1), zmat, preferred_element_type=F32)
        for y in range(0, z.rows, 2):
            both = []
            for at in (y, y + 1):
                here = z.cells + c + at
                total = wide_ref[here] * (write.pot(c + at) + (3.0 * WEIGHTS[0] - centre))
                total = total + along_z[b * at : b * at + b, :]
                for offset in range(1, REACH + 1):
                    beside = wide_ref[here + offset * z.rows] + wide_ref[here - offset * z.rows]
                    up = z.cells + c + (at + offset) % z.rows
                    down = z.cells + c + (at - offset) % z.rows
                    beside = beside + (wide_ref[up] + wide_ref[down])
                    total = total + WEIGHTS[offset] * beside
                both.append(total)
            write((c + y) // 2, jnp.concatenate(both, 0))


class Writer:
    def __init__(self, pot_ref, put):
        self.pot_ref, self.put = pot_ref, put

    def pot(self, cell):
        return self.pot_ref[cell : cell + 1, :]

    def __call__(self, pair, value):
        self.put(pair_rows(pair), value)


def fill_and_base(z, v_ref, on_ref, pot_ref, out_ref, wide_ref):
    dom = lax.axis_index("dom")
    first_core = (dom & 1) == 0
    on_at = pl.multiple_of(jnp.where(first_core, 2 * z.cells, 0), z.cells)
    off_at = pl.multiple_of(jnp.where(first_core, 0, 2 * z.cells), z.cells)
    step, b = 8, z.bands

    def tile(ref, c):
        return ref[b * c : b * (c + step), :].astype(F32).reshape(step, b, z.depth)

    for c in range(0, z.cells, step):
        wide_ref[z.cells + c : z.cells + c + step] = tile(v_ref, c)
        wide_ref[pl.ds(on_at + c, step)] = tile(on_ref, c)
        wide_ref[pl.ds(off_at + c, step)] = jnp.zeros((step, b, z.depth), F32)

    def put(rows, value):
        out_ref[rows, :] = value

    base_body(z, dom, v_ref, wide_ref, Writer(pot_ref, put))


def add_across(z, base_ref, across_ref, acc_ref):
    side = lax.axis_index("dom") & 1
    tall = z.rows * z.bands
    last = z.thickness - 1

    def at(plane, c):
        there = jnp.where(side == 0, plane, last - plane)
        return pl.ds(pl.multiple_of(there * tall + c, 32), 32)

    for c in range(0, tall, 32):
        planes = [across_ref[at(q, c), :].astype(F32) for q in range(z.thickness)]
        for x in range(z.thickness):
            total = base_ref[at(x, c), :]
            for q in range(x, z.thickness):
                offset = x - q + z.thickness
                if offset <= REACH:
                    total = total + WEIGHTS[offset] * planes[q]
            acc_ref[at(x, c), :] = total


def base_first_kernel(z, v_ref, on_ref, pot_ref, strength_ref, out_ref, near_ref, wide_ref):
    fill_and_base(z, v_ref, on_ref, pot_ref, out_ref, wide_ref)
    near_strength(z, lax.axis_index("dom"), strength_ref, near_ref)


def base_kernel(z, v_ref, on_ref, pot_ref, out_ref, wide_ref):
    fill_and_base(z, v_ref, on_ref, pot_ref, out_ref, wide_ref)


def nonlocal_pair(weighted, proj_ref, pair):
    both = jnp.concatenate([proj_ref[2 * pair], proj_ref[2 * pair + 1]], 1)
    value = jnp.dot(weighted, both, preferred_element_type=F32)
    half = value.shape[1] // 2
    return jnp.concatenate([value[:, :half], value[:, half:]], 0)


def first_kernel(
    z, base_ref, tab_in, chip_ref, across_ref, far_ref, near_ref, hots_ref, proj_ref, first_ref, tab_ref, acc_ref
):
    add_across(z, base_ref, across_ref, acc_ref)
    weighted = gathered(z, tab_in, chip_ref, across_ref, far_ref, near_ref, hots_ref)
    for pair in range(z.cells // 2):
        rows = pair_rows(pair)
        value = acc_ref[rows, :] + nonlocal_pair(weighted[block_of(z, pair)], proj_ref, pair)
        first_ref[rows, :] = (value * (1.0 / half_width)).astype(BF16)
    projector = Projector(z, first_ref, proj_ref)
    projector.add(range(z.cells // 2))
    scatter(z, projector.sums(), hots_ref, tab_ref)
    put_mate(z, tab_ref, first_ref)


def filtered_kernel(
    z, base_ref, tab_ref, chip_ref, across_ref, far_ref, near_ref, hots_ref, proj_ref, start_ref, out_ref, acc_ref
):
    add_across(z, base_ref, across_ref, acc_ref)
    weighted = gathered(z, tab_ref, chip_ref, across_ref, far_ref, near_ref, hots_ref)
    for pair in range(z.cells // 2):
        rows = pair_rows(pair)
        value = acc_ref[rows, :] + nonlocal_pair(weighted[block_of(z, pair)], proj_ref, pair)
        out_ref[rows, :] = (value * (2.0 / half_width) - start_ref[rows, :].astype(F32)).astype(BF16)


def final_kernel(z, in_ref, out_hbm, out_ref, sems):
    tall = z.rows * z.bands
    writes = []
    for x in range(z.thickness):
        plane = in_ref[x * tall : (x + 1) * tall, :].astype(F32).reshape(z.rows, z.bands, z.depth)
        at = pl.ds(x * z.rows, z.rows)
        out_ref[:, at, :] = jnp.swapaxes(plane, 0, 1).astype(BF16)
        writes.append(pltpu.make_async_copy(out_ref.at[:, at, :], out_hbm.at[:, at, :], sems.at[x]))
        writes[-1].start()
    for write in writes:
        write.wait()


VMEM = pl.BlockSpec(memory_space=pltpu.VMEM)


def call(kernel, z, name, outs, ins, flops, moved, scratch=(), out_space=None):
    single = not isinstance(outs, (list, tuple))
    return pl.pallas_call(
        functools.partial(kernel, z),
        name=name,
        out_shape=outs,
        in_specs=[VMEM] * len(ins),
        out_specs=(out_space or VMEM) if single else [VMEM] * len(outs),
        scratch_shapes=list(scratch),
        compiler_params=pltpu.CompilerParams(vmem_limit_bytes=12288 * 1024),
        cost_estimate=pl.CostEstimate(flops=flops, bytes_accessed=moved, transcendentals=0),
    )(*ins)


class Shapes:
    def __init__(self, z):
        self.tile = jax.ShapeDtypeStruct((z.bands, z.lanes), F32)
        self.pair = jax.ShapeDtypeStruct((2, z.bands, z.lanes), F32)
        self.tab = jax.ShapeDtypeStruct((3, z.bands, z.lanes), F32)
        self.slab = jax.ShapeDtypeStruct((z.tall, z.depth), BF16)
        self.message = jax.ShapeDtypeStruct((z.tall + 6 * z.bands, z.depth), BF16)
        self.mate_message = jax.ShapeDtypeStruct((z.tall + 10 * z.bands, z.depth), BF16)
        self.base = jax.ShapeDtypeStruct((z.tall, z.depth), F32)
        self.near = jax.ShapeDtypeStruct((8, z.lanes), F32)
        self.hots = jax.ShapeDtypeStruct((z.blocks, 3 * z.lanes, z.slots), BF16)
        self.wide = [pltpu.VMEM((3 * z.cells, z.bands, z.depth), F32)]
        self.acc = [pltpu.VMEM((z.tall, z.depth), F32)]
        self.stream = 2 * z.tall * z.slots * z.depth
        self.proj_bytes = 2 * z.cells * z.slots * z.depth
        self.stencil = 6 * z.tall * z.depth * z.depth
        self.slab_bytes = 10 * z.tall * z.depth


def swap_on_chip(x, axis):
    count = lax.axis_size(axis)
    return lax.ppermute(x, axis, [(i, i ^ 1) for i in range(count)])


def swap_across(x, axis):
    count = lax.axis_size(axis)
    return lax.ppermute(x, axis, [(i, (((i + 1) ^ 1) - 1) % count) for i in range(count)])


def swap_far(x, axis):
    count = lax.axis_size(axis)
    return lax.ppermute(x, axis, [(i, (i + 3 - 6 * (i % 2)) % count) for i in range(count)])


def local(bands, potential, projectors, atom_ids, strength, rotation):
    z = Sizes(bands.shape, atom_ids.shape, strength.shape, lax.axis_size("dom"))
    groups = lax.axis_size("band")
    proj = projectors.reshape(z.cells, z.slots, z.depth)
    pot = potential.reshape(z.cells, z.depth)
    flat = bands.reshape(z.bands, z.cells, z.depth)

    s = Shapes(z)

    def exchange(tab, slab):
        on_chip = swap_on_chip(slab, "dom")
        slab, chip, far = call(
            meet_kernel, z, "meet", [s.message, s.pair, s.tile], (tab, on_chip, slab), 1000, 1000
        )
        across = swap_across(slab, "dom")
        far = swap_far(far, "dom")
        return slab, on_chip, (tab, chip, across, far)

    pause = call(pause_kernel, z, "pause", s.tile, (), 4000 * s.stream, 40_000_000)
    start, hots = call(
        prepare_kernel, z, "prepare", [s.slab, s.hots], (pause, atom_ids, flat), s.stream, s.proj_bytes,
    )
    tab, start = call(
        project_kernel, z, "project", [s.tab, s.mate_message], (start, hots, proj), s.stream, s.proj_bytes,
    )
    start, on_chip, sums = exchange(tab, start)
    base, near = call(
        base_first_kernel, z, "base_first", [s.base, s.near],
        (start, on_chip, pot, strength.T), s.stencil, s.slab_bytes, scratch=s.wide,
    )
    first, tab = call(
        first_kernel, z, "first", [s.mate_message, s.tab],
        (base,) + sums + (near, hots, proj), 2 * s.stream, s.proj_bytes, scratch=s.acc,
    )
    first, on_chip, sums = exchange(tab, first)
    base = call(
        base_kernel, z, "base", s.base, (first, on_chip, pot), s.stencil, s.slab_bytes, scratch=s.wide,
    )
    filtered = call(
        filtered_kernel, z, "filtered", s.slab, (base,) + sums + (near, hots, proj, start),
        s.stream, s.proj_bytes, scratch=s.acc,
    )

    share = z.cells // groups
    pieces = filtered.reshape(groups, share, z.bands, z.depth)
    pieces = lax.all_to_all(pieces, "band", 0, 0, tiled=True)
    turn = rotation.reshape(groups, z.bands, groups * z.bands)
    rotated = jnp.einsum("gxbz,gbc->xcz", pieces, turn, preferred_element_type=F32).astype(BF16)
    rotated = rotated.reshape(share, groups, z.bands, z.depth).transpose(1, 0, 2, 3)
    rotated = lax.all_to_all(rotated, "band", 0, 0, tiled=True)
    out = call(
        final_kernel, z, "final", jax.ShapeDtypeStruct((z.bands, z.cells, z.depth), BF16),
        (rotated.reshape(z.tall, z.depth),), 1000, 4 * z.tall * z.depth,
        scratch=[
            pltpu.VMEM((z.bands, z.cells, z.depth), BF16),
            pltpu.SemaphoreType.DMA((z.thickness,)),
        ],
        out_space=pl.BlockSpec(memory_space=pltpu.HBM),
    )
    return out.reshape(bands.shape)


def solution(mesh):
    placed = (
        P("band", "dom", None, None),
        P("dom", None, None),
        P("dom", None, None, None, None),
        P("dom", None),
        P(),
        P(),
    )
    return jax.shard_map(
        local, mesh=mesh, in_specs=placed, out_specs=P("band", "dom", None, None), check_vma=False
    )
```

```python
import functools
import jax
import jax.numpy as jnp
import numpy as np
from jax import lax
from jax.experimental import pallas as pl
from jax.experimental.pallas import tpu as pltpu
from jax.sharding import PartitionSpec as P

STENCIL = [
    -5369.0 / 1800.0,
    12.0 / 7.0,
    -15.0 / 56.0,
    10.0 / 189.0,
    -1.0 / 112.0,
    2.0 / 1925.0,
    -1.0 / 16632.0,
]
kinetic_scale = 0.5 / 0.49
centre = 12.0
half_width = 11.0
REACH = 6
F32, BF16 = jnp.float32, jnp.bfloat16
WEIGHTS = [-kinetic_scale * w for w in STENCIL]


def split3(x):
    hi = x.astype(BF16)
    rest = x - hi.astype(F32)
    mid = rest.astype(BF16)
    return hi, mid, (rest - mid.astype(F32)).astype(BF16)


def z_matrix(depth):
    row = lax.broadcasted_iota(jnp.int32, (depth, depth), 0)
    col = lax.broadcasted_iota(jnp.int32, (depth, depth), 1)
    apart = jnp.abs(row - col)
    apart = jnp.minimum(apart, depth - apart)
    full = jnp.zeros((depth, depth), F32)
    for offset in range(1, REACH + 1):
        full = jnp.where(apart == offset, np.float32(WEIGHTS[offset]), full)
    return jnp.concatenate(split3(full), 0)


def dot_t(a, b):
    return lax.dot_general(a, b, (((1,), (1,)), ((), ())), preferred_element_type=F32)


class Sizes:
    def __init__(self, bands, atom_ids, strength, dom_count):
        self.bands, self.thickness, self.rows, self.depth = bands
        self.blocks, self.slot_count = atom_ids
        self.atoms, self.projs = strength
        self.doms = dom_count
        self.owned = self.atoms // dom_count
        self.block_rows = self.rows // self.blocks
        self.cells = self.thickness * self.rows
        self.slots = self.slot_count * self.projs
        self.lanes = self.owned * self.projs
        self.tall = self.cells * self.bands
        assert self.owned & (self.owned - 1) == 0 and dom_count & (dom_count - 1) == 0


def one_hots(z, dom, ids_ref):
    ids = ids_ref[...]
    shift = z.owned.bit_length() - 1
    relative = ((ids >> shift) - dom + (1 + z.doms)) & (z.doms - 1)
    place = relative * z.owned + (ids & (z.owned - 1))
    slot = lax.broadcasted_iota(jnp.int32, (z.slot_count, z.slots), 0)
    lane = lax.broadcasted_iota(jnp.int32, (z.slot_count, z.slots), 1)
    inside = lane - slot * z.projs
    spread = jnp.where((inside >= 0) & (inside < z.projs), 1.0, 0.0).astype(BF16)
    wide = jnp.dot(place.astype(F32).astype(BF16), spread, preferred_element_type=F32)
    shape = (z.lanes, z.slots)
    row = lax.broadcasted_iota(jnp.int32, shape, 0)
    lane = lax.broadcasted_iota(jnp.int32, shape, 1)
    fits = (row >> shift) == lane % z.projs
    atom = (row & (z.owned - 1)).astype(F32)
    out = []
    for j in range(z.blocks):
        mine = jnp.broadcast_to(wide[j : j + 1, :], shape)
        tiles = [
            jnp.where(fits & (mine == atom + float(z.owned * tile)), 1.0, 0.0) for tile in range(3)
        ]
        out.append(jnp.concatenate(tiles, 0).astype(BF16))
    return out


def scatter(z, partials, hots_ref, tab_ref):
    total = None
    b = z.bands
    for j, partial in enumerate(partials):
        pieces = jnp.concatenate([piece.astype(F32) for piece in split3(partial)], 0)
        part = dot_t(pieces.astype(BF16), hots_ref[j])
        part = part[:b] + part[b : 2 * b] + part[2 * b :]
        total = part if total is None else total + part
    for t in range(3):
        tab_ref[t] = total[:, t * z.lanes : (t + 1) * z.lanes]


def mate_tiles(side, tab_ref):
    first_core = side == 0
    return [
        jnp.where(first_core, tab_ref[1], tab_ref[0]),
        jnp.where(first_core, tab_ref[2], tab_ref[1]),
    ]


def put_mate(z, tab_ref, slab_ref):
    side = lax.axis_index("dom") & 1
    put_tiles(z, mate_tiles(side, tab_ref), slab_ref)
    outer = jnp.where(side == 0, tab_ref[0], tab_ref[2])
    pieces = list(split3(outer)) + [jnp.zeros(outer.shape, BF16)]
    slab_ref[z.tall + 6 * z.bands :, :] = jnp.concatenate([p.astype(F32) for p in pieces], 0).astype(BF16)


def put_tiles(z, tiles, slab_ref):
    for n, piece in enumerate(split3(jnp.concatenate(tiles, 0))):
        slab_ref[z.tall + n * 2 * z.bands : z.tall + (n + 1) * 2 * z.bands, :] = piece


def get_tiles(z, slab_ref):
    total = None
    for n in range(3):
        piece = slab_ref[z.tall + n * 2 * z.bands : z.tall + (n + 1) * 2 * z.bands, :].astype(F32)
        total = piece if total is None else total + piece
    return [total[: z.bands], total[z.bands :]]


def meet_kernel(z, tab_ref, got_ref, slab_in, slab_ref, chip_ref, far_ref):
    slab_ref[: z.tall, :] = slab_in[: z.tall, :]
    side = lax.axis_index("dom") & 1
    first_core = side == 0
    mate, got = mate_tiles(side, tab_ref), get_tiles(z, got_ref)
    low, high = mate[0] + got[0], mate[1] + got[1]
    chip_ref[0], chip_ref[1] = low, high
    outer = got_ref[z.tall + 6 * z.bands :, :].astype(F32)
    far_ref[...] = outer[: z.bands] + outer[z.bands : 2 * z.bands] + outer[2 * z.bands : 3 * z.bands]
    below, above = tab_ref[0], tab_ref[2]
    pair = [jnp.where(first_core, below, high), jnp.where(first_core, low, above)]
    put_tiles(z, pair, slab_ref)


def gathered(z, tab_ref, chip_ref, across_ref, far_ref, strength_ref, hots_ref):
    first_core = (lax.axis_index("dom") & 1) == 0
    got = get_tiles(z, across_ref)
    low, high, far = chip_ref[0], chip_ref[1], far_ref[...]
    tiles = [
        jnp.where(first_core, tab_ref[0] + got[0], low + far),
        jnp.where(first_core, low + got[1], high + got[0]),
        jnp.where(first_core, high + far, tab_ref[2] + got[1]),
    ]
    weighted = [tile * strength_ref[t : t + 1, :] for t, tile in enumerate(tiles)]
    weighted = jnp.concatenate(weighted, 1).astype(BF16)
    return [
        jnp.dot(weighted, hots_ref[j], preferred_element_type=F32).astype(BF16)
        for j in range(z.blocks)
    ]


def pair_rows(pair):
    return slice(16 * pair, 16 * pair + 16)


def block_of(z, pair):
    return (2 * pair % z.rows) // z.block_rows


class Projector:
    def __init__(self, z, v_ref, proj_ref):
        self.z, self.v_ref, self.proj_ref = z, v_ref, proj_ref
        self.total = [None] * z.blocks

    def add(self, pairs):
        b = self.z.bands
        for pair in pairs:
            j = block_of(self.z, pair)
            v = self.v_ref[pair_rows(pair), :].astype(F32)
            v = jnp.concatenate([v[:b], v[b:]], 1).astype(BF16)
            both = jnp.concatenate([self.proj_ref[2 * pair], self.proj_ref[2 * pair + 1]], 1)
            part = dot_t(v, both)
            self.total[j] = part if self.total[j] is None else self.total[j] + part

    def sums(self):
        return self.total


def turned(z, bands_ref, x):
    plane = bands_ref[:, x * z.rows : (x + 1) * z.rows, :].astype(F32)
    return jnp.swapaxes(plane, 0, 1)


def turn_all(z, bands_ref, v_ref):
    tall = z.rows * z.bands
    for x in range(z.thickness):
        plane = turned(z, bands_ref, x).reshape(tall, z.depth)
        v_ref[x * tall : (x + 1) * tall, :] = plane.astype(BF16)


def pause_kernel(z, out_ref):
    out_ref[...] = jnp.zeros_like(out_ref)


def prepare_kernel(z, pause_ref, ids_ref, bands_ref, v_ref, hots_ref):
    turn_all(z, bands_ref, v_ref)
    for j, hot in enumerate(one_hots(z, lax.axis_index("dom"), ids_ref)):
        hots_ref[j] = hot


def project_kernel(z, v_in, hots_ref, proj_ref, tab_ref, v_ref):
    v_ref[: z.tall, :] = v_in[...]
    projector = Projector(z, v_in, proj_ref)
    projector.add(range(z.cells // 2))
    scatter(z, projector.sums(), hots_ref, tab_ref)
    put_mate(z, tab_ref, v_ref)


def near_strength(z, dom, strength_ref, out_ref):
    per_tile = 128 // z.owned
    row = lax.broadcasted_iota(jnp.int32, (z.projs, 128), 0)
    lane = lax.broadcasted_iota(jnp.int32, (z.projs, 128), 1)
    for t in range(3):
        owner = (dom + (t - 1) + z.doms) & (z.doms - 1)
        tile = strength_ref[:, pl.ds(pl.multiple_of(owner // per_tile * 128, 128), 128)]
        inside = owner % per_tile
        line = jnp.zeros((1, 128), F32)
        for p in range(z.projs):
            turned = pltpu.roll(tile, ((p + per_tile) - inside) % per_tile * z.owned, 1)
            keep = (row == p) & (lane >= p * z.owned) & (lane < (p + 1) * z.owned)
            line = line + jnp.sum(jnp.where(keep, turned, 0.0), axis=0, keepdims=True)
        out_ref[t : t + 1, :] = line


def base_body(z, dom, v_ref, wide_ref, write):
    b = z.bands
    zmat = z_matrix(z.depth)
    for c in range(0, z.cells, z.rows):
        v = v_ref[b * c : b * (c + z.rows), :]
        along_z = jnp.dot(jnp.concatenate([v, v, v], 1), zmat, preferred_element_type=F32)
        for y in range(0, z.rows, 2):
            both = []
            for at in (y, y + 1):
                here = z.cells + c + at
                total = wide_ref[here] * (write.pot(c + at) + (3.0 * WEIGHTS[0] - centre))
                total = total + along_z[b * at : b * at + b, :]
                for offset in range(1, REACH + 1):
                    beside = wide_ref[here + offset * z.rows] + wide_ref[here - offset * z.rows]
                    up = z.cells + c + (at + offset) % z.rows
                    down = z.cells + c + (at - offset) % z.rows
                    beside = beside + (wide_ref[up] + wide_ref[down])
                    total = total + WEIGHTS[offset] * beside
                both.append(total)
            write((c + y) // 2, jnp.concatenate(both, 0))


class Writer:
    def __init__(self, pot_ref, put):
        self.pot_ref, self.put = pot_ref, put

    def pot(self, cell):
        return self.pot_ref[cell : cell + 1, :]

    def __call__(self, pair, value):
        self.put(pair_rows(pair), value)


def fill_and_base(z, v_ref, on_ref, pot_ref, out_ref, wide_ref):
    dom = lax.axis_index("dom")
    first_core = (dom & 1) == 0
    on_at = pl.multiple_of(jnp.where(first_core, 2 * z.cells, 0), z.cells)
    off_at = pl.multiple_of(jnp.where(first_core, 0, 2 * z.cells), z.cells)
    step, b = 8, z.bands

    def tile(ref, c):
        return ref[b * c : b * (c + step), :].astype(F32).reshape(step, b, z.depth)

    for c in range(0, z.cells, step):
        wide_ref[z.cells + c : z.cells + c + step] = tile(v_ref, c)
        wide_ref[pl.ds(on_at + c, step)] = tile(on_ref, c)
        wide_ref[pl.ds(off_at + c, step)] = jnp.zeros((step, b, z.depth), F32)

    def put(rows, value):
        out_ref[rows, :] = value

    base_body(z, dom, v_ref, wide_ref, Writer(pot_ref, put))


def add_across(z, base_ref, across_ref, acc_ref):
    side = lax.axis_index("dom") & 1
    tall = z.rows * z.bands
    last = z.thickness - 1

    def at(plane, c):
        there = jnp.where(side == 0, plane, last - plane)
        return pl.ds(pl.multiple_of(there * tall + c, 32), 32)

    for c in range(0, tall, 32):
        planes = [across_ref[at(q, c), :].astype(F32) for q in range(z.thickness)]
        for x in range(z.thickness):
            total = base_ref[at(x, c), :]
            for q in range(x, z.thickness):
                offset = x - q + z.thickness
                if offset <= REACH:
                    total = total + WEIGHTS[offset] * planes[q]
            acc_ref[at(x, c), :] = total


def base_first_kernel(z, v_ref, on_ref, pot_ref, strength_ref, out_ref, near_ref, wide_ref):
    fill_and_base(z, v_ref, on_ref, pot_ref, out_ref, wide_ref)
    near_strength(z, lax.axis_index("dom"), strength_ref, near_ref)


def base_kernel(z, v_ref, on_ref, pot_ref, out_ref, wide_ref):
    fill_and_base(z, v_ref, on_ref, pot_ref, out_ref, wide_ref)


def nonlocal_pair(weighted, proj_ref, pair):
    both = jnp.concatenate([proj_ref[2 * pair], proj_ref[2 * pair + 1]], 1)
    value = jnp.dot(weighted, both, preferred_element_type=F32)
    half = value.shape[1] // 2
    return jnp.concatenate([value[:, :half], value[:, half:]], 0)


def first_kernel(
    z, base_ref, tab_in, chip_ref, across_ref, far_ref, near_ref, hots_ref, proj_ref, first_ref, tab_ref, acc_ref
):
    weighted = gathered(z, tab_in, chip_ref, across_ref, far_ref, near_ref, hots_ref)
    add_across(z, base_ref, across_ref, acc_ref)
    for pair in range(z.cells // 2):
        rows = pair_rows(pair)
        value = acc_ref[rows, :] + nonlocal_pair(weighted[block_of(z, pair)], proj_ref, pair)
        first_ref[rows, :] = (value * (1.0 / half_width)).astype(BF16)
    projector = Projector(z, first_ref, proj_ref)
    projector.add(range(z.cells // 2))
    scatter(z, projector.sums(), hots_ref, tab_ref)
    put_mate(z, tab_ref, first_ref)


def filtered_kernel(
    z, base_ref, tab_ref, chip_ref, across_ref, far_ref, near_ref, hots_ref, proj_ref, start_ref, out_ref, acc_ref
):
    weighted = gathered(z, tab_ref, chip_ref, across_ref, far_ref, near_ref, hots_ref)
    add_across(z, base_ref, across_ref, acc_ref)
    for pair in range(z.cells // 2):
        rows = pair_rows(pair)
        value = acc_ref[rows, :] + nonlocal_pair(weighted[block_of(z, pair)], proj_ref, pair)
        out_ref[rows, :] = (value * (2.0 / half_width) - start_ref[rows, :].astype(F32)).astype(BF16)


VMEM = pl.BlockSpec(memory_space=pltpu.VMEM)


def call(kernel, z, name, outs, ins, flops, moved, scratch=()):
    single = not isinstance(outs, (list, tuple))
    return pl.pallas_call(
        functools.partial(kernel, z),
        name=name,
        out_shape=outs,
        in_specs=[VMEM] * len(ins),
        out_specs=VMEM if single else [VMEM] * len(outs),
        scratch_shapes=list(scratch),
        compiler_params=pltpu.CompilerParams(vmem_limit_bytes=12288 * 1024),
        cost_estimate=pl.CostEstimate(flops=flops, bytes_accessed=moved, transcendentals=0),
    )(*ins)


class Shapes:
    def __init__(self, z):
        self.tile = jax.ShapeDtypeStruct((z.bands, z.lanes), F32)
        self.pair = jax.ShapeDtypeStruct((2, z.bands, z.lanes), F32)
        self.tab = jax.ShapeDtypeStruct((3, z.bands, z.lanes), F32)
        self.slab = jax.ShapeDtypeStruct((z.tall, z.depth), BF16)
        self.message = jax.ShapeDtypeStruct((z.tall + 6 * z.bands, z.depth), BF16)
        self.mate_message = jax.ShapeDtypeStruct((z.tall + 10 * z.bands, z.depth), BF16)
        self.base = jax.ShapeDtypeStruct((z.tall, z.depth), F32)
        self.near = jax.ShapeDtypeStruct((8, z.lanes), F32)
        self.hots = jax.ShapeDtypeStruct((z.blocks, 3 * z.lanes, z.slots), BF16)
        self.wide = [pltpu.VMEM((3 * z.cells, z.bands, z.depth), F32)]
        self.acc = [pltpu.VMEM((z.tall, z.depth), F32)]
        self.stream = 2 * z.tall * z.slots * z.depth
        self.proj_bytes = 2 * z.cells * z.slots * z.depth
        self.stencil = 6 * z.tall * z.depth * z.depth
        self.slab_bytes = 10 * z.tall * z.depth


def swap_on_chip(x, axis):
    count = lax.axis_size(axis)
    return lax.ppermute(x, axis, [(i, i ^ 1) for i in range(count)])


def swap_across(x, axis):
    count = lax.axis_size(axis)
    return lax.ppermute(x, axis, [(i, (((i + 1) ^ 1) - 1) % count) for i in range(count)])


def swap_far(x, axis):
    count = lax.axis_size(axis)
    return lax.ppermute(x, axis, [(i, (i + 3 - 6 * (i % 2)) % count) for i in range(count)])


def local(bands, potential, projectors, atom_ids, strength, rotation):
    z = Sizes(bands.shape, atom_ids.shape, strength.shape, lax.axis_size("dom"))
    groups = lax.axis_size("band")
    proj = projectors.reshape(z.cells, z.slots, z.depth)
    pot = potential.reshape(z.cells, z.depth)
    flat = bands.reshape(z.bands, z.cells, z.depth)

    s = Shapes(z)

    def exchange(tab, slab):
        on_chip = swap_on_chip(slab, "dom")
        slab, chip, far = call(
            meet_kernel, z, "meet", [s.message, s.pair, s.tile], (tab, on_chip, slab), 1000, 1000
        )
        across = swap_across(slab, "dom")
        far = swap_far(far, "dom")
        return slab, on_chip, (tab, chip, across, far)

    pause = call(pause_kernel, z, "pause", s.tile, (), 4000 * s.stream, 40_000_000)
    start, hots = call(
        prepare_kernel, z, "prepare", [s.slab, s.hots], (pause, atom_ids, flat), s.stream, s.proj_bytes,
    )
    tab, start = call(
        project_kernel, z, "project", [s.tab, s.mate_message], (start, hots, proj), s.stream, s.proj_bytes,
    )
    start, on_chip, sums = exchange(tab, start)
    base, near = call(
        base_first_kernel, z, "base_first", [s.base, s.near],
        (start, on_chip, pot, strength.T), s.stencil, s.slab_bytes, scratch=s.wide,
    )
    first, tab = call(
        first_kernel, z, "first", [s.mate_message, s.tab],
        (base,) + sums + (near, hots, proj), 2 * s.stream, s.proj_bytes, scratch=s.acc,
    )
    first, on_chip, sums = exchange(tab, first)
    base = call(
        base_kernel, z, "base", s.base, (first, on_chip, pot), s.stencil, s.slab_bytes, scratch=s.wide,
    )
    filtered = call(
        filtered_kernel, z, "filtered", s.slab, (base,) + sums + (near, hots, proj, start),
        s.stream, s.proj_bytes, scratch=s.acc,
    )

    share = z.cells // groups
    pieces = filtered.reshape(groups, share, z.bands, z.depth)
    pieces = lax.all_to_all(pieces, "band", 0, 0, tiled=True)
    turn = rotation.reshape(groups, z.bands, groups * z.bands)
    rotated = jnp.einsum("gxbz,gbc->xcz", pieces, turn, preferred_element_type=F32).astype(BF16)
    rotated = rotated.reshape(share, groups, z.bands, z.depth).transpose(1, 0, 2, 3)
    rotated = lax.all_to_all(rotated, "band", 0, 0, tiled=True)
    return rotated.reshape(z.cells, z.bands, z.depth).transpose(1, 0, 2).reshape(bands.shape)


def solution(mesh):
    placed = (
        P("band", "dom", None, None),
        P("dom", None, None),
        P("dom", None, None, None, None),
        P("dom", None),
        P(),
        P(),
    )
    return jax.shard_map(
        local, mesh=mesh, in_specs=placed, out_specs=P("band", "dom", None, None), check_vma=False
    )
```
